32 devices in a mesh: tube: 2 (over x), gy: 4 (over y, core), gz: 4 (over z).
Axes of the slice: x: 2, y: 2, z: 4, core: 2. Of those that a mesh axis runs over, the one named last changes fastest.
Arguments:
- state: float32 [13, 32, 32, 512], P(None, 'tube', 'gy', 'gz'), as said below
- fresh: float32 [13, 32, 512], P(None, 'gy', 'gz'), as said below
- substeps: int32 [32, 32, 512], P('tube', 'gy', 'gz'), may hold values from 1 to 8, as said below
- shift: int32 [], replicated, may hold values from 1 to 12
Outputs:
- advanced: float32 [13, 32, 32, 512], P(None, 'tube', 'gy', 'gz')
The draws below stay inside these ranges and needn't reach their ends.
Inputs may be any that keep to these rules, and one draw needn't show every extreme that they name: `state`: the first nine components are positive partial densities; the energy exceeds the kinetic and chemical energy by a positive thermal part. `fresh`: the same conventions as state. `substeps`: at most 8; some cell takes 8 in every draw.
All inputs are finite; a program needn't handle non-finite values.
Results may differ from the reference program's by a relative error of at most 0.0003.
Values sent between devices are 32-bit elements; how exact they have to be, the bound alone decides.
No kernel may reach another device: no remote copies, remote signals or barrier semaphores. Data moves between devices by JAX's collectives and lax.ppermute only.
A program may use at most 64 MiB of HBM per device.

```python
import jax
import jax.numpy as jnp
import numpy as np
from jax import lax

SMAX = 12
CMAX = 8
NX = 32
NY = 32
NZ = 512


molar_table = [2.016 / 18.015, 31.998 / 18.015, 18.015 / 18.015, 1.008 / 18.015, 15.999 / 18.015, 17.007 / 18.015, 33.006 / 18.015, 34.014 / 18.015, 28.014 / 18.015]


factor_table = [2.5, 2.5, 3.0, 1.5, 1.5, 2.5, 3.0, 3.0, 2.5]


energy_table = [0.0, 0.0, -1.5, 12.0, 1.5, 0.25, 0.02, -0.45, 0.0]


burnt_base = [0.03, 0.15, 0.3, 0.01, 0.02, 0.04, 0.005, 0.005, 0.7]


fresh_base = [0.06, 0.25, 0.02, 0.004, 0.004, 0.006, 0.002, 0.002, 0.75]


def gas_sample(key, grid_extents, base):
    stochastic_seeds = jax.random.split(key, 4)
    lead = (1,) * len(grid_extents)
    base_col = jnp.asarray(base, jnp.float32).reshape((9,) + lead)
    constituent_grids = base_col * jnp.exp(jax.random.uniform(stochastic_seeds[0], (9,) + grid_extents, jnp.float32, -0.7, 0.7))
    stir = 0.25 * jnp.clip(jax.random.normal(stochastic_seeds[1], (3,) + grid_extents, jnp.float32), -3.0, 3.0)
    kelvin_level = jax.random.uniform(stochastic_seeds[2], grid_extents, jnp.float32, 1.0, 2.2)
    drift = jnp.asarray([-1.0, 0.0, 0.0], jnp.float32).reshape((3,) + lead)
    if len(grid_extents) == 3:
        plane_seeds = jax.random.split(stochastic_seeds[3], 3)
        plane_shape = (grid_extents[0], 1, 1)
        plane_density = jnp.exp(jax.random.uniform(plane_seeds[0], plane_shape, jnp.float32, -1.0, 1.0))
        plane_heat = jax.random.uniform(plane_seeds[1], plane_shape, jnp.float32, 0.75, 1.35)
        plane_speed = jax.random.uniform(plane_seeds[2], plane_shape, jnp.float32, -0.5, 0.5)
        constituent_grids = constituent_grids * plane_density[None]
        kelvin_level = kelvin_level * plane_heat
        drift = drift + jnp.concatenate([plane_speed[None], jnp.zeros((2,) + plane_shape, jnp.float32)], axis=0)
    fluid_speed_vector = drift + stir
    kilograms_per_volume = jnp.sum(constituent_grids, axis=0)
    calorific_entries = jnp.asarray([factor_table[constituent_count] / molar_table[constituent_count] for constituent_count in range(9)], jnp.float32).reshape((9,) + lead)
    enthalpy_of_creation = jnp.asarray(energy_table, jnp.float32).reshape((9,) + lead)
    overall_conserved_work = jnp.sum(constituent_grids * calorific_entries, axis=0) * kelvin_level + jnp.sum(constituent_grids * enthalpy_of_creation, axis=0) + 0.5 * kilograms_per_volume * jnp.sum(fluid_speed_vector * fluid_speed_vector, axis=0)
    return jnp.concatenate([constituent_grids, kilograms_per_volume[None] * fluid_speed_vector, overall_conserved_work[None]], axis=0)


def draw_state(key, part):
    return gas_sample(jax.random.fold_in(key, 11), (NX, NY, NZ), burnt_base)


def draw_fresh(key, part):
    return gas_sample(jax.random.fold_in(key, 23), (NY, NZ), fresh_base)


def draw_substeps(key, part):
    plane = lax.broadcasted_iota(jnp.int32, (NX, NY, NZ), 0)
    band = plane >= NX - max(NX // 8, 1)
    top = jnp.where(band, CMAX, 2)
    raw = jax.random.randint(jax.random.fold_in(key, 37), (NX, NY, NZ), 0, 1 << 20)
    counts = 1 + raw % top
    return counts.at[NX - 1, NY - 1, NZ - 1].set(CMAX)


def setup_inputs(seed: int = 0) -> dict:
    keys = jax.random.split(jax.random.key(seed), 5)
    state = draw_state(jax.random.fold_in(keys[4], 71), 0)
    fresh = draw_fresh(jax.random.fold_in(keys[4], 71), 0)
    substeps = draw_substeps(jax.random.fold_in(keys[4], 71), 0)
    shift = jax.random.randint(keys[3], (), 1, SMAX + 1).astype(jnp.int32)
    return {"state": state, "fresh": fresh, "substeps": substeps, "shift": shift}


molar_mass = np.array([2.016, 31.998, 18.015, 1.008, 15.999, 17.007, 33.006, 34.014, 28.014]) / 18.015
heat_factor = np.array([2.5, 2.5, 3.0, 1.5, 1.5, 2.5, 3.0, 3.0, 2.5])
formation = np.array([0.0, 0.0, -1.5, 12.0, 1.5, 0.25, 0.02, -0.45, 0.0])
consumed_stoichiometry = [(3, 1, 9), (4, 5, 9), (4, 0, 9), (3, 5, 9), (0, 5, 9), (2, 3, 9), (4, 2, 9), (5, 5, 9), (0, 8, 9), (3, 3, 8), (4, 4, 8), (3, 4, 8), (3, 5, 8), (3, 1, 8), (6, 3, 9), (6, 3, 9), (6, 4, 9), (6, 5, 9), (6, 6, 9), (7, 8, 9), (7, 3, 9)]
products = [(4, 5), (3, 1), (3, 5), (4, 0), (2, 3), (0, 5), (5, 5), (4, 2), (3, 3), (0,), (1,), (5,), (2,), (6,), (0, 1), (5, 5), (1, 5), (2, 1), (7, 1), (5, 5), (2, 5)]
arrhenius_coefficients = [30.0, 8.0, 20.0, 6.0, 25.0, 10.0, 12.0, 5.0, 4.0, 20.0, 15.0, 18.0, 22.0, 25.0, 30.0, 25.0, 20.0, 30.0, 10.0, 6.0, 15.0]
arrhenius_barrier = [4.0, 1.0, 3.0, 1.5, 1.5, 4.5, 4.0, 1.5, 6.0, 0.5, 0.5, 0.5, 0.5, 0.3, 0.8, 0.5, 0.3, 0.3, 0.5, 5.0, 1.5]
time_step = 0.05

def stoich_table():
    table = np.zeros((9, 21))
    for constituent_count in range(21):
        for which in consumed_stoichiometry[constituent_count]:
            if which < 9:
                table[which, constituent_count] -= 1.0
        for which in products[constituent_count]:
            table[which, constituent_count] += 1.0
    return table * molar_mass[:, None]

def column(values, array):
    return jnp.asarray(values, dtype=array.dtype).reshape((9,) + (1,) * (array.ndim - 1))

def weno_side(first, second, third, fourth, fifth):
    smooth_a = 13.0 / 12.0 * (first - 2.0 * second + third) ** 2 + 0.25 * (first - 4.0 * second + 3.0 * third) ** 2
    smooth_b = 13.0 / 12.0 * (second - 2.0 * third + fourth) ** 2 + 0.25 * (second - fourth) ** 2
    smooth_c = 13.0 / 12.0 * (third - 2.0 * fourth + fifth) ** 2 + 0.25 * (3.0 * third - 4.0 * fourth + fifth) ** 2
    weight_a = 0.1 / (1e-06 + smooth_a) ** 2
    weight_b = 0.6 / (1e-06 + smooth_b) ** 2
    weight_c = 0.3 / (1e-06 + smooth_c) ** 2
    total = weight_a + weight_b + weight_c
    blend = weight_a * (2.0 * first - 7.0 * second + 11.0 * third) + weight_b * (-second + 5.0 * third + 2.0 * fourth) + weight_c * (2.0 * third + 5.0 * fourth - fifth)
    return blend / (6.0 * total)

def flux_change(ghosted_grid_values, array_axis, count):
    constituent_grids = ghosted_grid_values[:9]
    kilograms_per_volume = lax.optimization_barrier(jnp.sum(constituent_grids, axis=0))
    momentum = ghosted_grid_values[9:12]
    motion_work = 0.5 * lax.optimization_barrier(jnp.sum(momentum * momentum, axis=0)) / kilograms_per_volume
    specific_warming_coefficient = lax.optimization_barrier(jnp.sum(constituent_grids * column(heat_factor / molar_mass, constituent_grids), axis=0))
    combustion_portion = lax.optimization_barrier(jnp.sum(constituent_grids * column(formation, constituent_grids), axis=0))
    kelvin_level = (ghosted_grid_values[12] - motion_work - combustion_portion) / specific_warming_coefficient
    blend_accumulation = lax.optimization_barrier(jnp.sum(constituent_grids * column(1.0 / molar_mass, constituent_grids), axis=0))
    thermodynamic_stress = blend_accumulation * kelvin_level
    sound = jnp.sqrt((1.0 + blend_accumulation / specific_warming_coefficient) * thermodynamic_stress / kilograms_per_volume)
    row = 8 + array_axis
    fluid_speed_vector = ghosted_grid_values[row] / kilograms_per_volume
    flux = ghosted_grid_values * fluid_speed_vector[None]
    flux = jnp.concatenate([flux[:row], (flux[row] + thermodynamic_stress)[None], flux[row + 1:12], (flux[12] + thermodynamic_stress * fluid_speed_vector)[None]], axis=0)
    speed = (jnp.abs(fluid_speed_vector) + sound)[None]

    def take(array, offset):
        return lax.slice_in_dim(array, offset, offset + count + 1, axis=array_axis)
    alpha = take(speed, 0)
    for offset in range(1, 6):
        alpha = jnp.maximum(alpha, take(speed, offset))
    plus = [0.5 * (take(flux, offset) + alpha * take(ghosted_grid_values, offset)) for offset in range(5)]
    minus = [0.5 * (take(flux, offset) - alpha * take(ghosted_grid_values, offset)) for offset in range(1, 6)]
    face = weno_side(plus[0], plus[1], plus[2], plus[3], plus[4]) + weno_side(minus[4], minus[3], minus[2], minus[1], minus[0])
    return lax.slice_in_dim(face, 1, count + 1, axis=array_axis) - lax.slice_in_dim(face, 0, count, axis=array_axis)

def react_step(constituent_grids, thermal_content, step_size):
    specific_warming_coefficient = lax.optimization_barrier(jnp.sum(constituent_grids * column(heat_factor / molar_mass, constituent_grids), axis=0))
    combustion_portion = lax.optimization_barrier(jnp.sum(constituent_grids * column(formation, constituent_grids), axis=0))
    kelvin_level = (thermal_content - combustion_portion) / specific_warming_coefficient
    moles_per_volume = constituent_grids * column(1.0 / molar_mass, constituent_grids)
    moles_per_volume = jnp.concatenate([moles_per_volume, jnp.ones_like(moles_per_volume[:1])], axis=0)
    progress_speeds = jnp.stack([arrhenius_coefficients[constituent_count] * jnp.exp(-arrhenius_barrier[constituent_count] / kelvin_level) * moles_per_volume[consumed_stoichiometry[constituent_count][0]] * moles_per_volume[consumed_stoichiometry[constituent_count][1]] * moles_per_volume[consumed_stoichiometry[constituent_count][2]] for constituent_count in range(21)])
    table = jnp.asarray(stoich_table(), dtype=constituent_grids.dtype)
    omega = jnp.dot(table, progress_speeds, precision=lax.Precision.HIGHEST)
    return constituent_grids + step_size[None] * omega

def react_cells(constituent_grids, thermal_content, counts, turns):
    step_size = time_step / counts.astype(constituent_grids.dtype)

    def advance(index, current):
        moved = react_step(current, thermal_content, step_size)
        return jnp.where((index < counts)[None], moved, current)
    return lax.fori_loop(0, turns, advance, constituent_grids)

def reference(state, fresh, substeps, shift):
    comps, planes, width_y, width_z = state.shape
    inflow = jnp.broadcast_to(fresh[:, None], (comps, SMAX, width_y, width_z))
    joined = jnp.concatenate([state, inflow], axis=1)
    start = lax.dynamic_slice_in_dim(joined, shift.astype(jnp.int32), planes, 1)
    ghosts = jnp.broadcast_to(fresh[:, None], (comps, 3, width_y, width_z))

    def evaluate(current):
        edge = jnp.broadcast_to(current[:, :1], (comps, 3, width_y, width_z))
        x_ext = jnp.concatenate([edge, current, ghosts], axis=1)
        y_ext = jnp.pad(current, ((0, 0), (0, 0), (3, 3), (0, 0)), mode='wrap')
        z_ext = jnp.pad(current, ((0, 0), (0, 0), (0, 0), (3, 3)), mode='wrap')

        def strip(index):
            lower = index * 4
            x_part = lax.dynamic_slice_in_dim(x_ext, lower, 4, 2)
            y_part = lax.dynamic_slice_in_dim(y_ext, lower, 10, 2)
            z_part = lax.dynamic_slice_in_dim(z_ext, lower, 4, 2)
            return -(flux_change(x_part, 1, planes) + flux_change(y_part, 2, 4) + flux_change(z_part, 3, width_z))
        stacked = lax.map(strip, jnp.arange(width_y // 4))
        return jnp.transpose(stacked, (1, 2, 0, 3, 4)).reshape(comps, planes, width_y, width_z)
    first = start + time_step * evaluate(start)
    second = 0.75 * start + 0.25 * (first + time_step * evaluate(first))
    third = 1.0 / 3.0 * start + 2.0 / 3.0 * (second + time_step * evaluate(second))
    kilograms_per_volume = lax.optimization_barrier(jnp.sum(third[:9], axis=0))
    thermal_content = third[12] - 0.5 * lax.optimization_barrier(jnp.sum(third[9:12] * third[9:12], axis=0)) / kilograms_per_volume
    cells = planes * width_y * width_z
    reacted = react_cells(third[:9].reshape(9, cells), thermal_content.reshape(cells), substeps.reshape(cells), CMAX)
    return jnp.concatenate([reacted.reshape(9, planes, width_y, width_z), third[9:]], axis=0)
```

```python
import functools

import jax
import jax.numpy as jnp
import numpy as np
from jax import lax
from jax.experimental import pallas as pl
from jax.experimental.pallas import tpu as pltpu
from jax.sharding import PartitionSpec as P

SMAX = 12
HALO = 3
NCOMP = 13
ROWS = 8
SCALE = 0.25
TIME_STEP = 0.05
FLUX_FACTOR = -TIME_STEP / (6.0 * SCALE)

MOLAR = np.array([2.016, 31.998, 18.015, 1.008, 15.999, 17.007, 33.006, 34.014, 28.014]) / 18.015
GAS = 1.0 / MOLAR
FORMATION = np.array([0.0, 0.0, -1.5, 12.0, 1.5, 0.25, 0.02, -0.45, 0.0])
REACTANTS = [
    (3, 1), (4, 5), (4, 0), (3, 5), (0, 5), (2, 3), (4, 2), (5, 5), (0, 8), (3, 3, 8), (4, 4, 8),
    (3, 4, 8), (3, 5, 8), (3, 1, 8), (6, 3), (6, 3), (6, 4), (6, 5), (6, 6), (7, 8), (7, 3),
]
PRODUCTS = [
    (4, 5), (3, 1), (3, 5), (4, 0), (2, 3), (0, 5), (5, 5), (4, 2), (3, 3), (0,), (1,),
    (5,), (2,), (6,), (0, 1), (5, 5), (1, 5), (2, 1), (7, 1), (5, 5), (2, 5),
]
PREFACTOR = [
    30.0, 8.0, 20.0, 6.0, 25.0, 10.0, 12.0, 5.0, 4.0, 20.0, 15.0,
    18.0, 22.0, 25.0, 30.0, 25.0, 20.0, 30.0, 10.0, 6.0, 15.0,
]
BARRIER = [
    4.0, 1.0, 3.0, 1.5, 1.5, 4.5, 4.0, 1.5, 6.0, 0.5, 0.5,
    0.5, 0.5, 0.3, 0.8, 0.5, 0.3, 0.3, 0.5, 5.0, 1.5,
]

KAPPA = 0.609375
EPS = 3.0 * SCALE * SCALE * 1e-6


def rcp(x):
    return pl.reciprocal(x, approx=True)


def correction(d1, d2, d3, d4):
    k2 = KAPPA * (d2 * d2) + EPS
    k3 = KAPPA * (d3 * d3) + EPS
    xa = d1 - 1.375 * d2
    xb = d3 - 0.625 * d2
    xc = d4 - 1.375 * d3
    ra = rcp(xa * xa + k2)
    rb = rcp(xb * xb + k2)
    rc = rcp(xc * xc + k3)
    wa = ra * ra
    wb = 6.0 * (rb * rb)
    wc = 3.0 * (rc * rc)
    return ((xa + xb) * wa + (0.5 * (d2 + d4) - d3) * wc) * rcp(wa + wb + wc)


def face_flux(du, df, f2, f3, alpha):
    e = [alpha * d for d in du]
    p = [df[k] + e[k] for k in range(4)]
    m = [None] + [df[k] - e[k] for k in range(1, 5)]
    linear = 3.0 * (f2 + f3) - e[2] + 0.5 * (p[1] - m[3])
    return linear - correction(p[0], p[1], p[2], p[3]) + correction(m[4], m[3], m[2], m[1])


def sweep(cells, fluxes, alpha, first, last):
    du, df = {}, {}
    out = {}
    for j in range(first, last + 1):
        for k in range(j, j + 5):
            if k not in du:
                du[k] = cells(k + 1) - cells(k)
                df[k] = fluxes(k + 1) - fluxes(k)
        out[j] = face_flux(
            [du[k] for k in range(j, j + 5)],
            [df[k] for k in range(j, j + 5)],
            fluxes(j + 2),
            fluxes(j + 3),
            alpha(j),
        )
    return out


def memo(load):
    return functools.lru_cache(maxsize=None)(load)


def thermo(u):
    g = [u[k] if GAS[k] == 1.0 else u[k] * float(GAS[k]) for k in range(9)]
    s2 = g[2] + g[6] + g[7]
    s3 = g[3] + g[4]
    gas = (g[0] + g[1]) + (g[5] + g[8]) + (s2 + s3)
    heat = 2.5 * gas + (0.5 * s2 - s3)
    bond = 1.5 * (u[4] - u[2]) + 12.0 * u[3] + 0.25 * u[5] + 0.02 * u[6] - 0.45 * u[7]
    rho = ((u[0] + u[1]) + (u[2] + u[3])) + ((u[4] + u[5]) + (u[6] + u[7])) + u[8]
    back = 1.0 / rho
    cold = 1.0 / heat
    motion = 0.5 * (u[9] * u[9] + u[10] * u[10] + u[11] * u[11]) * back
    temperature = (u[12] - motion - bond) * cold
    pressure = gas * temperature
    sound = jnp.sqrt((1.0 + gas * cold) * pressure * back)
    return back, pressure, sound


def for_components(dim, body):
    special = 8 + dim

    def step(i, _):
        body(i + jnp.where(i >= special, 1, 0).astype(jnp.int32), 0)
        return 0

    lax.fori_loop(0, NCOMP - 2, step, 0)
    body(special, 1)
    body(NCOMP - 1, 2)


def flux_of(u, speed, pressure, kind):
    if kind == 0:
        return u * speed
    if kind == 1:
        return u * speed + SCALE * pressure()
    return (u + pressure()) * speed


def alphas(speed, faces, alpha_ref, rows):
    values = memo(lambda i: speed[pl.ds(i * rows, ROWS), :])
    for j in range(faces):
        top = values(j)
        for k in range(1, 6):
            top = jnp.maximum(top, values(j + k))
        alpha_ref[pl.ds(j * rows, ROWS), :] = top


def stage_kernel(
    stage, planes, width_y, width_z, x_msgs, place,
    u_ref, uz_ref, start_ref, fresh_ref, xlo_ref, xhi_ref, ylo_ref, yhi_ref, zlo_ref, zhi_ref,
    *refs,
):
    groups = planes // ROWS
    zvecs = width_z // ROWS
    tubes = place[1]
    tube = place[0]
    first = stage == 1
    last = stage == 3
    refs = list(refs)
    new_ref = refs.pop(0)
    if not last:
        newz_ref = refs.pop(0)
        xmsg_refs = [refs.pop(0) for _ in range(x_msgs)]
        ymsg_lo, ymsg_hi, zmsg_lo, zmsg_hi = [refs.pop(0) for _ in range(4)]
    (
        xh, ux, px, ax, alx, uy, py, ay, aly, uz, pz, az, alz, tmp, accx, accy, accz,
    ) = refs

    def ghosts(c, _):
        for k in range(HALO):
            here = pl.ds(k * ROWS, ROWS)
            lo, hi = xlo_ref[c, here, :], xhi_ref[c, here, :]
            if not first:
                lo = jnp.where(tube == 0, u_ref[c, pl.ds(0, ROWS), :], lo)
                hi = jnp.where(tube == tubes - 1, fresh_ref[c], hi)
            xh[c, here, :] = lo
            xh[c, pl.ds((HALO + k) * ROWS, ROWS), :] = hi
        return 0

    lax.fori_loop(0, NCOMP, ghosts, 0)

    def own(i, _):
        for k in range(2):
            p = i * 2 + k
            here = pl.ds(pl.multiple_of(p * ROWS, ROWS), ROWS)
            u = [u_ref[c, here, :] for c in range(NCOMP)]
            back, pressure, sound = thermo(u)
            back, sound = SCALE * back, SCALE * sound
            there = pl.ds(pl.multiple_of((p + HALO) * ROWS, ROWS), ROWS)
            speeds = [u[9 + d] * back for d in range(3)]
            ux[there, :] = speeds[0]
            px[there, :] = pressure
            ax[there, :] = jnp.abs(speeds[0]) + sound
            ystart = pl.ds(HALO * planes + p, width_y, stride=planes)
            uy[ystart, :] = speeds[1]
            py[ystart, :] = pressure
            ay[ystart, :] = jnp.abs(speeds[1]) + sound
            tmp[0, here, :] = speeds[2]
            tmp[1, here, :] = pressure
            tmp[2, here, :] = jnp.abs(speeds[2]) + sound
        return 0

    lax.fori_loop(0, planes // 2, own, 0)
    for ref, k in ((uz, 0), (pz, 1), (az, 2)):
        ref[pl.ds(ROWS, width_z), :] = tmp[k].T

    def ghost_thermo(u, d, speed_ref, pressure_ref, top_ref, row):
        back, pressure, sound = thermo(u)
        speed = u[9 + d] * (SCALE * back)
        speed_ref[pl.ds(row, ROWS), :] = speed
        pressure_ref[pl.ds(row, ROWS), :] = pressure
        top_ref[pl.ds(row, ROWS), :] = jnp.abs(speed) + SCALE * sound

    for k in range(2 * HALO):
        row = k if k < HALO else planes + k
        u = [xh[c, pl.ds(k * ROWS, ROWS), :] for c in range(NCOMP)]
        ghost_thermo(u, 0, ux, px, ax, row * ROWS)
    for ref, offset in ((ylo_ref, 0), (yhi_ref, HALO + width_y)):
        def ghost_y(k, _, ref=ref, offset=offset):
            for g in range(groups):
                u = [ref[c, pl.ds(k * planes + g * ROWS, ROWS), :] for c in range(NCOMP)]
                ghost_thermo(u, 1, uy, py, ay, (offset + k) * planes + g * ROWS)
            return 0
        lax.fori_loop(0, HALO, ghost_y, 0)
    for ref, row in ((zlo_ref, 0), (zhi_ref, ROWS + width_z)):
        u = [ref[c] for c in range(NCOMP)]
        ghost_thermo(u, 2, uz, pz, az, row)

    alphas(ax, planes + 1, alx, ROWS)
    for g in range(groups):
        values = memo(lambda i: ay[pl.ds(i * planes + g * ROWS, ROWS), :])
        for j in range(width_y + 1):
            top = values(j)
            for k in range(1, 6):
                top = jnp.maximum(top, values(j + k))
            aly[pl.ds(j * planes + g * ROWS, ROWS), :] = top

    def zvec(ref, i):
        return ref[pl.ds(ROWS - HALO + i, ROWS, stride=zvecs), :]

    values_z = memo(lambda i: zvec(az, i))
    for j in range(zvecs + 1):
        top = values_z(j)
        for k in range(1, 6):
            top = jnp.maximum(top, values_z(j + k))
        alz[pl.ds(j * ROWS, ROWS), :] = top

    def x_body(c, kind):
        def cell(i):
            if HALO <= i < planes + HALO:
                return u_ref[c, pl.ds((i - HALO) * ROWS, ROWS), :]
            k = i if i < HALO else i - planes
            return xh[c, pl.ds(k * ROWS, ROWS), :]
        cells = memo(cell)
        fluxes = memo(lambda i: flux_of(
            cells(i), ux[pl.ds(i * ROWS, ROWS), :], lambda: px[pl.ds(i * ROWS, ROWS), :], kind))
        out = sweep(cells, fluxes, lambda j: alx[pl.ds(j * ROWS, ROWS), :], 0, planes)
        for i in range(planes):
            accx[c, pl.ds(i * ROWS, ROWS), :] = out[i + 1] - out[i]

    for_components(1, x_body)

    def y_body(c, kind):
        for g in range(groups):
            def cell(i):
                if HALO <= i < width_y + HALO:
                    return u_ref[c, pl.ds(g * ROWS * width_y + i - HALO, ROWS, stride=width_y), :]
                if i < HALO:
                    return ylo_ref[c, pl.ds(i * planes + g * ROWS, ROWS), :]
                return yhi_ref[c, pl.ds((i - HALO - width_y) * planes + g * ROWS, ROWS), :]
            cells = memo(cell)
            def at(ref):
                return lambda i: ref[pl.ds(i * planes + g * ROWS, ROWS), :]
            fluxes = memo(lambda i: flux_of(cells(i), at(uy)(i), lambda: at(py)(i), kind))
            out = sweep(cells, fluxes, at(aly), 0, width_y)
            for i in range(width_y):
                accy[c, pl.ds(g * ROWS * width_y + i, ROWS, stride=width_y), :] = out[i + 1] - out[i]

    for_components(2, y_body)

    row = lax.broadcasted_iota(jnp.int32, (ROWS, planes * width_y), 0)

    def z_body(c, kind):
        def cell(i):
            value = uz_ref[c, pl.ds(ROWS - HALO + i, ROWS, stride=zvecs), :]
            if i < HALO:
                edge = zlo_ref[c, pl.ds(ROWS - HALO + i, 1), :]
                value = jnp.where(row == 0, edge, value)
            elif i >= zvecs + HALO:
                edge = zhi_ref[c, pl.ds(i - zvecs - HALO, 1), :]
                value = jnp.where(row == ROWS - 1, edge, value)
            return value
        cells = memo(cell)
        fluxes = memo(lambda i: flux_of(cells(i), zvec(uz, i), lambda: zvec(pz, i), kind))
        out = sweep(cells, fluxes, lambda j: alz[pl.ds(j * ROWS, ROWS), :], 0, zvecs)
        for i in range(zvecs):
            accz[c, pl.ds(i, ROWS, stride=zvecs), :] = out[i + 1] - out[i]

    for_components(3, z_body)

    def combine(c, _):
        change = FLUX_FACTOR * (accz[c].T + accx[c] + accy[c])
        if stage == 1:
            value = u_ref[c] + change
        elif stage == 2:
            value = 0.75 * start_ref[c] + 0.25 * (u_ref[c] + change)
        else:
            value = (1.0 / 3.0) * start_ref[c] + (2.0 / 3.0) * (u_ref[c] + change)
        new_ref[c] = value
        if not last:
            newz_ref[c, pl.ds(ROWS, width_z), :] = value.T
        return 0

    lax.fori_loop(0, NCOMP, combine, 0)
    if not last:
        messages(planes, width_y, width_z, place, new_ref, newz_ref, xmsg_refs,
                 ymsg_lo, ymsg_hi, zmsg_lo, zmsg_hi)


def messages(planes, width_y, width_z, place, u_ref, uz_ref, xmsg_refs, ylo, yhi, zlo, zhi):
    def body(c, _):
        for n, ref in enumerate(xmsg_refs):
            begin = place[2 + n]
            for k in range(HALO):
                rows = pl.ds(pl.multiple_of((begin + k) * ROWS, ROWS), ROWS)
                ref[c, pl.ds(k * ROWS, ROWS), :] = u_ref[c, rows, :]
        for k in range(HALO):
            for g in range(planes // ROWS):
                there = pl.ds(k * planes + g * ROWS, ROWS)
                base = g * ROWS * width_y + k
                yhi[c, there, :] = u_ref[c, pl.ds(base, ROWS, stride=width_y), :]
                ylo[c, there, :] = u_ref[
                    c, pl.ds(base + width_y - HALO, ROWS, stride=width_y), :]
        zhi[c] = uz_ref[c, pl.ds(ROWS, ROWS), :]
        zlo[c] = uz_ref[c, pl.ds(width_z, ROWS), :]
        return 0

    lax.fori_loop(0, NCOMP, body, 0)


def assemble_kernel(
    planes, width_y, width_z, place, state_ref, ahead_ref, behind_ref, fresh_ref,
    u_ref, uz_ref, xlo_ref, xhi_ref, ymsg_lo, ymsg_hi, zmsg_lo, zmsg_hi, joined,
):
    tube, tubes, shift = place[0], place[1], place[4]
    tail = behind_ref.shape[1] // ROWS
    total = tail + planes + ahead_ref.shape[1] // ROWS

    def body(c, _):
        joined[pl.ds(0, tail * ROWS), :] = behind_ref[c]
        joined[pl.ds(tail * ROWS, planes * ROWS), :] = state_ref[c]
        fresh = fresh_ref[c]
        for i in range(tail + planes, total):
            value = ahead_ref[c, pl.ds((i - tail - planes) * ROWS, ROWS), :]
            joined[pl.ds(i * ROWS, ROWS), :] = jnp.where(tube == tubes - 1, fresh, value)

        def plane(i):
            return joined[pl.ds(pl.multiple_of((tail + shift + i) * ROWS, ROWS), ROWS), :]

        for i in range(planes):
            u_ref[c, pl.ds(i * ROWS, ROWS), :] = plane(i)
        ground = plane(0)
        for k in range(HALO):
            xhi_ref[c, pl.ds(k * ROWS, ROWS), :] = plane(planes + k)
            xlo_ref[c, pl.ds(k * ROWS, ROWS), :] = jnp.where(tube == 0, ground, plane(k - HALO))
        uz_ref[c, pl.ds(ROWS, width_z), :] = u_ref[c].T
        return 0

    lax.fori_loop(0, NCOMP, body, 0)
    messages(planes, width_y, width_z, place, u_ref, uz_ref, [],
             ymsg_lo, ymsg_hi, zmsg_lo, zmsg_hi)


def powers_of(back):
    a = jnp.exp(-0.5 * back)
    b = jnp.exp(-0.3 * back)
    a2 = a * a
    a3 = a2 * a
    a4 = a2 * a2
    a6 = a3 * a3
    a8 = a4 * a4
    return {0.5: a, 0.3: b, 1.0: a2, 1.5: a3, 3.0: a6, 4.0: a8, 4.5: a8 * a, 5.0: a8 * a2,
            6.0: a6 * a6, 0.8: a * b}


def react(conc, internal, size):
    s2 = conc[2] + conc[6] + conc[7]
    s3 = conc[3] + conc[4]
    heat = 2.5 * (((conc[0] + conc[1]) + (conc[5] + conc[8])) + (s2 + s3)) + (0.5 * s2 - s3)
    bond = None
    for k in range(9):
        if FORMATION[k]:
            term = float(FORMATION[k] * MOLAR[k]) * conc[k]
            bond = term if bond is None else bond + term
    boltzmann = powers_of(heat / (internal - bond))
    pairs = {}
    omega = [None] * 9

    def add(k, value):
        omega[k] = value if omega[k] is None else omega[k] + value

    def sub(k, value):
        omega[k] = -value if omega[k] is None else omega[k] - value

    def rate(j):
        names = REACTANTS[j]
        key = tuple(sorted(names))
        if key not in pairs:
            value = conc[names[0]] * conc[names[1]]
            if len(names) == 3:
                base = tuple(sorted(names[:2]))
                if base not in pairs:
                    pairs[base] = value
                value = pairs[base] * conc[8]
            pairs[key] = value
        return (PREFACTOR[j] * boltzmann[BARRIER[j]]) * pairs[key]

    j = 0
    while j < len(REACTANTS):
        value = rate(j)
        back = j + 1 < len(REACTANTS) and REACTANTS[j + 1] == PRODUCTS[j] \
            and PRODUCTS[j + 1] == REACTANTS[j]
        if back:
            value = value - rate(j + 1)
        for k in range(9):
            times = PRODUCTS[j].count(k) - REACTANTS[j].count(k)
            if times == 0:
                continue
            amount = value if abs(times) == 1 else value + value
            if times > 0:
                add(k, amount)
            else:
                sub(k, amount)
        j += 2 if back else 1
    return [conc[k] + size * omega[k] for k in range(9)]


def chemistry_kernel(planes, span, third_ref, counts_ref, out_ref):
    for c in range(9, NCOMP):
        out_ref[c] = third_ref[c]

    def block(i, _):
        rows = [
            pl.ds(pl.multiple_of((i * span + k) * ROWS, ROWS), ROWS) for k in range(span)
        ]
        counts = [counts_ref[r, :] for r in rows]
        sizes = [TIME_STEP / n.astype(jnp.float32) for n in counts]
        most = counts[0]
        for n in counts[1:]:
            most = jnp.maximum(most, n)
        turns = jnp.max(most)
        conc, internal = [], []
        for r in rows:
            u = [third_ref[c, r, :] for c in range(NCOMP)]
            rho = ((u[0] + u[1]) + (u[2] + u[3])) + ((u[4] + u[5]) + (u[6] + u[7])) + u[8]
            internal.append(
                u[12] - 0.5 * (u[9] * u[9] + u[10] * u[10] + u[11] * u[11]) / rho)
            conc.append([u[k] * float(GAS[k]) for k in range(9)])

        def advance(index, carry):
            new = []
            for k in range(span):
                moved = react(carry[k], internal[k], sizes[k])
                keep = index < counts[k]
                new.append([jnp.where(keep, m, o) for m, o in zip(moved, carry[k])])
            return new

        conc = lax.fori_loop(0, turns, advance, conc)
        for k in range(span):
            for c in range(9):
                out_ref[c, rows[k], :] = conc[k][c] * float(MOLAR[c])
        return 0

    lax.fori_loop(0, planes // span, block, 0)


def shape(*dims):
    return jax.ShapeDtypeStruct(dims, jnp.float32)


def call(kernel, out_shape, scratch, n_in):
    vmem = pl.BlockSpec(memory_space=pltpu.VMEM)
    return pl.pallas_call(
        kernel,
        out_shape=out_shape,
        in_specs=[pl.BlockSpec(memory_space=pltpu.SMEM)] + [vmem] * (n_in - 1),
        out_specs=jax.tree.map(lambda _: vmem, out_shape),
        scratch_shapes=scratch,
        compiler_params=pltpu.CompilerParams(vmem_limit_bytes=48 * 1024 * 1024),
    )


def moved(value, axis, steps, closed):
    count = lax.axis_size(axis)
    pairs = [(i, (i + steps) % count) for i in range(count) if closed or 0 <= i + steps < count]
    return lax.ppermute(value, axis, pairs)


def on_device(state, fresh, substeps, shift):
    comps, planes, width_y, width_z = state.shape
    cross = planes * width_y
    tubes = lax.axis_size("tube")
    tube = lax.axis_index("tube")
    swap = tubes == 2
    x_msgs = 1 if swap else 2
    begins = [jnp.where(tube == 0, planes - HALO, 0), 0] if swap else [0, planes - HALO]
    place = jnp.stack([
        tube.astype(jnp.int32), jnp.int32(tubes), jnp.asarray(begins[0], jnp.int32),
        jnp.asarray(begins[1], jnp.int32), shift.astype(jnp.int32)])

    reach = SMAX + HALO
    flat = state.reshape(comps, cross, width_z)
    if swap:
        out = jnp.where(tube == 0, flat[:, cross - reach * width_y:], flat[:, :reach * width_y])
        ahead = lax.ppermute(out, "tube", [(0, 1), (1, 0)])
        behind = ahead[:, (reach - 2) * width_y:]
    else:
        ahead = moved(flat[:, :reach * width_y], "tube", -1, False)
        behind = moved(flat[:, cross - 2 * width_y:], "tube", 1, False)

    full = shape(comps, cross, width_z)
    fullz = shape(comps, width_z + 2 * ROWS, cross)
    xs = shape(comps, HALO * ROWS, width_z)
    ys = shape(comps, HALO * planes, width_z)
    zs = shape(comps, ROWS, cross)
    start, uz, xlo, xhi, *msgs = call(
        functools.partial(assemble_kernel, planes, width_y, width_z),
        (full, fullz, xs, xs, ys, ys, zs, zs),
        [pltpu.VMEM(((2 + planes + reach) * ROWS, width_z), jnp.float32)],
        5,
    )(place, flat, ahead, behind, fresh)

    def plain(*dims):
        return pltpu.VMEM(dims, jnp.float32)

    rows_x = (planes + 2 * HALO) * ROWS
    rows_y = (width_y + 2 * HALO) * planes
    rows_z = width_z + 2 * ROWS
    zvecs = width_z // ROWS
    scratch = (
        [plain(comps, 2 * HALO * ROWS, width_z)]
        + [plain(rows_x, width_z)] * 3 + [plain((planes + 1) * ROWS, width_z)]
        + [plain(rows_y, width_z)] * 3 + [plain((width_y + 1) * planes, width_z)]
        + [plain(rows_z, cross)] * 3 + [plain((zvecs + 1) * ROWS, cross)]
        + [plain(3, cross, width_z), plain(comps, cross, width_z), plain(comps, cross, width_z),
           plain(comps, width_z, cross)]
    )
    current = start
    for stage in (1, 2, 3):
        ylo = moved(msgs[0], "gy", 1, True)
        yhi = moved(msgs[1], "gy", -1, True)
        zlo = moved(msgs[2], "gz", 1, True)
        zhi = moved(msgs[3], "gz", -1, True)
        outs = (full,)
        if stage < 3:
            outs = (full, fullz) + (xs,) * x_msgs + (ys, ys, zs, zs)
        current, *rest = call(
            functools.partial(stage_kernel, stage, planes, width_y, width_z, x_msgs),
            outs, scratch, 11,
        )(place, current, uz, start, fresh, xlo, xhi, ylo, yhi, zlo, zhi)
        if stage < 3:
            uz, *rest = rest
            msgs = rest[x_msgs:]
            if swap:
                xlo = xhi = lax.ppermute(rest[0], "tube", [(0, 1), (1, 0)])
            else:
                xhi = moved(rest[0], "tube", -1, False)
                xlo = moved(rest[1], "tube", 1, False)

    vmem = pl.BlockSpec(memory_space=pltpu.VMEM)
    reacted = pl.pallas_call(
        functools.partial(chemistry_kernel, planes, 4),
        out_shape=full,
        in_specs=[vmem, vmem],
        out_specs=vmem,
        compiler_params=pltpu.CompilerParams(vmem_limit_bytes=48 * 1024 * 1024),
    )(current, substeps.reshape(cross, width_z))
    return reacted.reshape(state.shape)


def solution(mesh):
    return jax.shard_map(
        on_device,
        mesh=mesh,
        in_specs=(P(None, "tube", "gy", "gz"), P(None, "gy", "gz"), P("tube", "gy", "gz"), P()),
        out_specs=P(None, "tube", "gy", "gz"),
        check_vma=False,
    )
```

```python
import functools

import jax
import jax.numpy as jnp
import numpy as np
from jax import lax
from jax.experimental import pallas as pl
from jax.experimental.pallas import tpu as pltpu
from jax.sharding import PartitionSpec as P

SMAX = 12
HALO = 3
NCOMP = 13
ROWS = 8
SCALE = 0.25
TIME_STEP = 0.05
FLUX_FACTOR = -TIME_STEP / (6.0 * SCALE)

MOLAR = np.array([2.016, 31.998, 18.015, 1.008, 15.999, 17.007, 33.006, 34.014, 28.014]) / 18.015
GAS = 1.0 / MOLAR
FORMATION = np.array([0.0, 0.0, -1.5, 12.0, 1.5, 0.25, 0.02, -0.45, 0.0])
REACTANTS = [
    (3, 1), (4, 5), (4, 0), (3, 5), (0, 5), (2, 3), (4, 2), (5, 5), (0, 8), (3, 3, 8), (4, 4, 8),
    (3, 4, 8), (3, 5, 8), (3, 1, 8), (6, 3), (6, 3), (6, 4), (6, 5), (6, 6), (7, 8), (7, 3),
]
PRODUCTS = [
    (4, 5), (3, 1), (3, 5), (4, 0), (2, 3), (0, 5), (5, 5), (4, 2), (3, 3), (0,), (1,),
    (5,), (2,), (6,), (0, 1), (5, 5), (1, 5), (2, 1), (7, 1), (5, 5), (2, 5),
]
PREFACTOR = [
    30.0, 8.0, 20.0, 6.0, 25.0, 10.0, 12.0, 5.0, 4.0, 20.0, 15.0,
    18.0, 22.0, 25.0, 30.0, 25.0, 20.0, 30.0, 10.0, 6.0, 15.0,
]
BARRIER = [
    4.0, 1.0, 3.0, 1.5, 1.5, 4.5, 4.0, 1.5, 6.0, 0.5, 0.5,
    0.5, 0.5, 0.3, 0.8, 0.5, 0.3, 0.3, 0.5, 5.0, 1.5,
]

KAPPA = 0.609375
EPS = 3.0 * SCALE * SCALE * 1e-6


def rcp(x):
    return pl.reciprocal(x, approx=True)


def correction(d1, d2, d3, d4):
    k2 = KAPPA * (d2 * d2) + EPS
    k3 = KAPPA * (d3 * d3) + EPS
    xa = d1 - 1.375 * d2
    xb = d3 - 0.625 * d2
    xc = d4 - 1.375 * d3
    ra = rcp(xa * xa + k2)
    rb = rcp(xb * xb + k2)
    rc = rcp(xc * xc + k3)
    wa = ra * ra
    wb = 6.0 * (rb * rb)
    wc = 3.0 * (rc * rc)
    return ((xa + xb) * wa + (0.5 * (d2 + d4) - d3) * wc) * rcp(wa + wb + wc)


def face_flux(du, df, f2, f3, alpha):
    e = [alpha * d for d in du]
    p = [df[k] + e[k] for k in range(4)]
    m = [None] + [df[k] - e[k] for k in range(1, 5)]
    linear = 3.0 * (f2 + f3) - e[2] + 0.5 * (p[1] - m[3])
    return linear - correction(p[0], p[1], p[2], p[3]) + correction(m[4], m[3], m[2], m[1])


def sweep(cells, fluxes, alpha, first, last):
    du, df = {}, {}
    out = {}
    for j in range(first, last + 1):
        for k in range(j, j + 5):
            if k not in du:
                du[k] = cells(k + 1) - cells(k)
                df[k] = fluxes(k + 1) - fluxes(k)
        out[j] = face_flux(
            [du[k] for k in range(j, j + 5)],
            [df[k] for k in range(j, j + 5)],
            fluxes(j + 2),
            fluxes(j + 3),
            alpha(j),
        )
    return out


def memo(load):
    return functools.lru_cache(maxsize=None)(load)


def thermo(u):
    g = [u[k] if GAS[k] == 1.0 else u[k] * float(GAS[k]) for k in range(9)]
    s2 = g[2] + g[6] + g[7]
    s3 = g[3] + g[4]
    gas = (g[0] + g[1]) + (g[5] + g[8]) + (s2 + s3)
    heat = 2.5 * gas + (0.5 * s2 - s3)
    bond = 1.5 * (u[4] - u[2]) + 12.0 * u[3] + 0.25 * u[5] + 0.02 * u[6] - 0.45 * u[7]
    rho = ((u[0] + u[1]) + (u[2] + u[3])) + ((u[4] + u[5]) + (u[6] + u[7])) + u[8]
    back = 1.0 / rho
    cold = 1.0 / heat
    motion = 0.5 * (u[9] * u[9] + u[10] * u[10] + u[11] * u[11]) * back
    temperature = (u[12] - motion - bond) * cold
    pressure = gas * temperature
    sound = jnp.sqrt((1.0 + gas * cold) * pressure * back)
    return back, pressure, sound


def for_components(dim, body):
    special = 8 + dim

    def step(i, _):
        body(i + jnp.where(i >= special, 1, 0).astype(jnp.int32), 0)
        return 0

    lax.fori_loop(0, NCOMP - 2, step, 0)
    body(special, 1)
    body(NCOMP - 1, 2)


def flux_of(u, speed, pressure, kind):
    if kind == 0:
        return u * speed
    if kind == 1:
        return u * speed + SCALE * pressure()
    return (u + pressure()) * speed


def own_thermo(planes, width_y, u_ref, x_refs, y_refs, z_refs, tmp):
    def own(i, _):
        for k in range(2):
            p = i * 2 + k
            here = pl.ds(pl.multiple_of(p * ROWS, ROWS), ROWS)
            u = [u_ref[c, here, :] for c in range(NCOMP)]
            back, pressure, sound = thermo(u)
            back, sound = SCALE * back, SCALE * sound
            across = pl.ds(p, width_y, stride=planes)
            for d, where in ((0, here), (1, across), (2, here)):
                speed = u[9 + d] * back
                for n, value in enumerate((speed, pressure, jnp.abs(speed) + sound)):
                    if d == 2:
                        tmp[n, where, :] = value
                    else:
                        (x_refs, y_refs)[d][n][where, :] = value
        return 0

    lax.fori_loop(0, planes // 2, own, 0)
    for n in range(3):
        z_refs[n][pl.ds(ROWS, tmp.shape[2]), :] = tmp[n].T


def inner_kernel(
    planes, width_y, width_z, u_ref, uz_ref,
    ux, px, ax, uy, py, ay, uz, pz, az, accx, accy, accz, alx, aly, alz, tmp,
):
    groups = planes // ROWS
    zvecs = width_z // ROWS
    own_thermo(planes, width_y, u_ref, (ux, px, ax), (uy, py, ay), (uz, pz, az), tmp)

    def xvec(ref):
        return lambda i: ref[pl.ds((i - HALO) * ROWS, ROWS), :]

    def yvec(ref, g):
        return lambda i: ref[pl.ds((i - HALO) * planes + g * ROWS, ROWS), :]

    def zvec(ref):
        return lambda i: ref[pl.ds(ROWS - HALO + i, ROWS, stride=zvecs), :]

    largest(xvec(ax), range(HALO, planes - HALO + 1), alx, lambda j: j * ROWS)
    for g in range(groups):
        largest(yvec(ay, g), range(HALO, width_y - HALO + 1), aly,
                lambda j: j * planes + g * ROWS)
    largest(zvec(az), range(HALO, zvecs - HALO + 1), alz, lambda j: j * ROWS)

    def inner(n, cells, speed, pressure, kind, alpha, put):
        cells = memo(cells)
        fluxes = memo(lambda i: flux_of(cells(i), speed(i), lambda: pressure(i), kind))
        out = sweep(cells, fluxes, alpha, HALO, n - HALO)
        put(HALO - 1, out[HALO])
        for i in range(HALO, n - HALO):
            put(i, out[i + 1] - out[i])
        put(n - HALO, out[n - HALO])

    def x_body(c, kind):
        def put(i, value):
            accx[c, pl.ds(i * ROWS, ROWS), :] = value
        inner(planes, lambda i: u_ref[c, pl.ds((i - HALO) * ROWS, ROWS), :], xvec(ux), xvec(px),
              kind, lambda j: alx[pl.ds(j * ROWS, ROWS), :], put)

    for_components(1, x_body)

    def z_body(c, kind):
        def put(i, value):
            accz[c, pl.ds(i, ROWS, stride=zvecs), :] = value
        inner(zvecs, lambda i: uz_ref[c, pl.ds(ROWS - HALO + i, ROWS, stride=zvecs), :],
              zvec(uz), zvec(pz), kind, lambda j: alz[pl.ds(j * ROWS, ROWS), :], put)

    for_components(3, z_body)

    def y_body(c, kind):
        for g in range(groups):
            def put(i, value, g=g):
                accy[c, pl.ds(g * ROWS * width_y + i, ROWS, stride=width_y), :] = value
            def cell(i, g=g):
                return u_ref[c, pl.ds(g * ROWS * width_y + i - HALO, ROWS, stride=width_y), :]
            inner(width_y, cell, yvec(uy, g), yvec(py, g), kind,
                  lambda j: aly[pl.ds(j * planes + g * ROWS, ROWS), :], put)

    for_components(2, y_body)


def largest(speed, faces, ref, place):
    values = memo(speed)
    for j in faces:
        top = values(j)
        for k in range(1, 6):
            top = jnp.maximum(top, values(j + k))
        ref[pl.ds(place(j), ROWS), :] = top


def outer_kernel(
    stage, planes, width_y, width_z, x_msgs, place,
    u_ref, uz_ref, start_ref, fresh_ref, xlo_ref, xhi_ref, ylo_ref, yhi_ref, zlo_ref, zhi_ref,
    ux, px, ax, uy, py, ay, uz, pz, az, accx, accy, accz, *refs,
):
    groups = planes // ROWS
    zvecs = width_z // ROWS
    tube, tubes = place[0], place[1]
    last = stage == 3
    refs = list(refs)
    new_ref = refs.pop(0)
    if not last:
        newz_ref = refs.pop(0)
        xmsg_refs = [refs.pop(0) for _ in range(x_msgs)]
        ymsg_lo, ymsg_hi, zmsg_lo, zmsg_hi = [refs.pop(0) for _ in range(4)]
    xh, gx, gy, gz, alx, aly, alz, edgex, edgey, edgez = refs

    def ghosts(c, _):
        for k in range(HALO):
            here = pl.ds(k * ROWS, ROWS)
            lo = jnp.where(tube == 0, u_ref[c, pl.ds(0, ROWS), :], xlo_ref[c, here, :])
            hi = jnp.where(tube == tubes - 1, fresh_ref[c], xhi_ref[c, here, :])
            xh[c, here, :] = lo
            xh[c, pl.ds((HALO + k) * ROWS, ROWS), :] = hi
        return 0

    lax.fori_loop(0, NCOMP, ghosts, 0)

    def ghost_thermo(u, d, ref, row):
        back, pressure, sound = thermo(u)
        speed = u[9 + d] * (SCALE * back)
        for n, value in enumerate((speed, pressure, jnp.abs(speed) + SCALE * sound)):
            ref[n, pl.ds(row, ROWS), :] = value

    for k in range(2 * HALO):
        ghost_thermo([xh[c, pl.ds(k * ROWS, ROWS), :] for c in range(NCOMP)], 0, gx, k * ROWS)
    for ref, offset in ((ylo_ref, 0), (yhi_ref, HALO)):
        def ghost_y(k, _, ref=ref, offset=offset):
            for g in range(groups):
                row = pl.multiple_of(k * planes + g * ROWS, ROWS)
                u = [ref[c, pl.ds(row, ROWS), :] for c in range(NCOMP)]
                ghost_thermo(u, 1, gy, pl.multiple_of(offset * planes + row, ROWS))
            return 0
        lax.fori_loop(0, HALO, ghost_y, 0)
    ghost_thermo([zlo_ref[c] for c in range(NCOMP)], 2, gz, 0)
    ghost_thermo([zhi_ref[c] for c in range(NCOMP)], 2, gz, ROWS)

    def xvec(ref, n):
        def load(i):
            if HALO <= i < planes + HALO:
                return ref[pl.ds((i - HALO) * ROWS, ROWS), :]
            return gx[n, pl.ds((i if i < HALO else i - planes) * ROWS, ROWS), :]
        return load

    def yvec(ref, n, g):
        def load(i):
            if HALO <= i < width_y + HALO:
                return ref[pl.ds((i - HALO) * planes + g * ROWS, ROWS), :]
            return gy[n, pl.ds((i if i < HALO else i - width_y) * planes + g * ROWS, ROWS), :]
        return load

    row = lax.broadcasted_iota(jnp.int32, (ROWS, planes * width_y), 0)

    def joined(i, load, lo, hi):
        value = load(pl.ds(ROWS - HALO + i, ROWS, stride=zvecs))
        if i < HALO:
            return jnp.where(row == 0, lo(pl.ds(ROWS - HALO + i, 1)), value)
        if i >= zvecs + HALO:
            return jnp.where(row == ROWS - 1, hi(pl.ds(i - zvecs - HALO, 1)), value)
        return value

    def zvec(ref, n):
        def load(i):
            return joined(i, lambda s: ref[s, :], lambda s: gz[n, s, :],
                          lambda s: gz[n, pl.ds(ROWS + s.start, 1), :])
        return load

    def ends(n):
        return list(range(HALO)) + list(range(n - HALO + 1, n + 1))

    largest(xvec(ax, 2), ends(planes), alx, lambda j: j * ROWS)
    for g in range(groups):
        largest(yvec(ay, 2, g), ends(width_y), aly, lambda j: j * planes + g * ROWS)
    largest(zvec(az, 2), ends(zvecs), alz, lambda j: j * ROWS)

    def outer(n, cells, speed, pressure, kind, alpha, given, put):
        cells = memo(cells)
        fluxes = memo(lambda i: flux_of(cells(i), speed(i), lambda: pressure(i), kind))
        out = sweep(cells, fluxes, alpha, 0, HALO - 1)
        out[HALO] = given(HALO - 1)
        for i in range(HALO):
            put(i, out[i + 1] - out[i])
        out = sweep(cells, fluxes, alpha, n - HALO + 1, n)
        out[n - HALO] = given(n - HALO)
        for i in range(n - HALO, n):
            put(i, out[i + 1] - out[i])

    def x_body(c, kind):
        def cell(i):
            if HALO <= i < planes + HALO:
                return u_ref[c, pl.ds((i - HALO) * ROWS, ROWS), :]
            return xh[c, pl.ds((i if i < HALO else i - planes) * ROWS, ROWS), :]
        def put(i, value):
            edgex[c, pl.ds((i if i < HALO else i - planes + 2 * HALO) * ROWS, ROWS), :] = value
        outer(planes, cell, xvec(ux, 0), xvec(px, 1), kind,
              lambda j: alx[pl.ds(j * ROWS, ROWS), :],
              lambda i: accx[c, pl.ds(i * ROWS, ROWS), :], put)

    for_components(1, x_body)

    def z_body(c, kind):
        def cell(i):
            return joined(i, lambda s: uz_ref[c, s, :], lambda s: zlo_ref[c, s, :],
                          lambda s: zhi_ref[c, s, :])
        def put(i, value):
            edgez[c, pl.ds(i, ROWS, stride=zvecs), :] = value
        outer(zvecs, cell, zvec(uz, 0), zvec(pz, 1), kind,
              lambda j: alz[pl.ds(j * ROWS, ROWS), :],
              lambda i: accz[c, pl.ds(i, ROWS, stride=zvecs), :], put)

    for_components(3, z_body)

    def y_body(c, kind):
        for g in range(groups):
            base = g * ROWS * width_y
            def cell(i, g=g, base=base):
                if HALO <= i < width_y + HALO:
                    return u_ref[c, pl.ds(base + i - HALO, ROWS, stride=width_y), :]
                if i < HALO:
                    return ylo_ref[c, pl.ds(i * planes + g * ROWS, ROWS), :]
                return yhi_ref[c, pl.ds((i - HALO - width_y) * planes + g * ROWS, ROWS), :]
            def put(i, value, base=base):
                edgey[c, pl.ds(base + i, ROWS, stride=width_y), :] = value
            outer(width_y, cell, yvec(uy, 0, g), yvec(py, 1, g), kind,
                  lambda j: aly[pl.ds(j * planes + g * ROWS, ROWS), :],
                  lambda i: accy[c, pl.ds(base + i, ROWS, stride=width_y), :], put)

    for_components(2, y_body)

    def between(n, rows, width):
        position = lax.broadcasted_iota(jnp.int32, (rows, width), 0) % n
        return (position >= HALO) & (position < n - HALO)

    inside_y = between(width_y, planes * width_y, width_z)
    inside_z = between(zvecs, width_z, planes * width_y)

    def combine(c, _):
        change_z = jnp.where(inside_z, accz[c], edgez[c]).T
        change_y = jnp.where(inside_y, accy[c], edgey[c])
        low, high = HALO * ROWS, (planes - HALO) * ROWS
        change_x = jnp.concatenate([
            edgex[c, pl.ds(0, low), :], accx[c, pl.ds(low, high - low), :],
            edgex[c, pl.ds(low, low), :]], axis=0)
        change = FLUX_FACTOR * (change_x + change_y + change_z)
        if stage == 1:
            value = u_ref[c] + change
        elif stage == 2:
            value = 0.75 * start_ref[c] + 0.25 * (u_ref[c] + change)
        else:
            value = (1.0 / 3.0) * start_ref[c] + (2.0 / 3.0) * (u_ref[c] + change)
        new_ref[c] = value
        if not last:
            newz_ref[c, pl.ds(ROWS, width_z), :] = value.T
        return 0

    lax.fori_loop(0, NCOMP, combine, 0)
    if not last:
        messages(planes, width_y, width_z, place, new_ref, newz_ref, xmsg_refs,
                 ymsg_lo, ymsg_hi, zmsg_lo, zmsg_hi)


def messages(planes, width_y, width_z, place, u_ref, uz_ref, xmsg_refs, ylo, yhi, zlo, zhi):
    def body(c, _):
        for n, ref in enumerate(xmsg_refs):
            begin = place[2 + n]
            for k in range(HALO):
                rows = pl.ds(pl.multiple_of((begin + k) * ROWS, ROWS), ROWS)
                ref[c, pl.ds(k * ROWS, ROWS), :] = u_ref[c, rows, :]
        for k in range(HALO):
            for g in range(planes // ROWS):
                there = pl.ds(k * planes + g * ROWS, ROWS)
                base = g * ROWS * width_y + k
                yhi[c, there, :] = u_ref[c, pl.ds(base, ROWS, stride=width_y), :]
                ylo[c, there, :] = u_ref[
                    c, pl.ds(base + width_y - HALO, ROWS, stride=width_y), :]
        zhi[c] = uz_ref[c, pl.ds(ROWS, ROWS), :]
        zlo[c] = uz_ref[c, pl.ds(width_z, ROWS), :]
        return 0

    lax.fori_loop(0, NCOMP, body, 0)


def assemble_kernel(
    planes, width_y, width_z, x_msgs, place, state_ref, ahead_ref, fresh_ref, u_ref, uz_ref, *refs,
):
    refs = list(refs)
    xmsg_refs = [refs.pop(0) for _ in range(x_msgs)]
    ymsg_lo, ymsg_hi, zmsg_lo, zmsg_hi, joined = refs
    tube, tubes, shift = place[0], place[1], place[4]
    total = planes + ahead_ref.shape[1] // ROWS

    def body(c, _):
        joined[pl.ds(0, planes * ROWS), :] = state_ref[c]
        fresh = fresh_ref[c]
        for i in range(planes, total):
            value = ahead_ref[c, pl.ds((i - planes) * ROWS, ROWS), :]
            joined[pl.ds(i * ROWS, ROWS), :] = jnp.where(tube == tubes - 1, fresh, value)
        for i in range(planes):
            u_ref[c, pl.ds(i * ROWS, ROWS), :] = joined[
                pl.ds(pl.multiple_of((shift + i) * ROWS, ROWS), ROWS), :]
        uz_ref[c, pl.ds(ROWS, width_z), :] = u_ref[c].T
        return 0

    lax.fori_loop(0, NCOMP, body, 0)
    messages(planes, width_y, width_z, place, u_ref, uz_ref, xmsg_refs,
             ymsg_lo, ymsg_hi, zmsg_lo, zmsg_hi)


def powers_of(back):
    a = jnp.exp(-0.5 * back)
    b = jnp.exp(-0.3 * back)
    a2 = a * a
    a3 = a2 * a
    a4 = a2 * a2
    a6 = a3 * a3
    a8 = a4 * a4
    return {0.5: a, 0.3: b, 1.0: a2, 1.5: a3, 3.0: a6, 4.0: a8, 4.5: a8 * a, 5.0: a8 * a2,
            6.0: a6 * a6, 0.8: a * b}


def react(conc, internal, size):
    s2 = conc[2] + conc[6] + conc[7]
    s3 = conc[3] + conc[4]
    heat = 2.5 * (((conc[0] + conc[1]) + (conc[5] + conc[8])) + (s2 + s3)) + (0.5 * s2 - s3)
    bond = None
    for k in range(9):
        if FORMATION[k]:
            term = float(FORMATION[k] * MOLAR[k]) * conc[k]
            bond = term if bond is None else bond + term
    boltzmann = powers_of(heat / (internal - bond))
    pairs = {}
    omega = [None] * 9

    def add(k, value):
        omega[k] = value if omega[k] is None else omega[k] + value

    def sub(k, value):
        omega[k] = -value if omega[k] is None else omega[k] - value

    def rate(j):
        names = REACTANTS[j]
        key = tuple(sorted(names))
        if key not in pairs:
            value = conc[names[0]] * conc[names[1]]
            if len(names) == 3:
                base = tuple(sorted(names[:2]))
                if base not in pairs:
                    pairs[base] = value
                value = pairs[base] * conc[8]
            pairs[key] = value
        return (PREFACTOR[j] * boltzmann[BARRIER[j]]) * pairs[key]

    j = 0
    while j < len(REACTANTS):
        value = rate(j)
        back = j + 1 < len(REACTANTS) and REACTANTS[j + 1] == PRODUCTS[j] \
            and PRODUCTS[j + 1] == REACTANTS[j]
        if back:
            value = value - rate(j + 1)
        for k in range(9):
            times = PRODUCTS[j].count(k) - REACTANTS[j].count(k)
            if times == 0:
                continue
            amount = value if abs(times) == 1 else value + value
            if times > 0:
                add(k, amount)
            else:
                sub(k, amount)
        j += 2 if back else 1
    return [conc[k] + size * omega[k] for k in range(9)]


def chemistry_kernel(planes, span, third_ref, counts_ref, out_ref):
    for c in range(9, NCOMP):
        out_ref[c] = third_ref[c]

    def block(i, _):
        rows = [
            pl.ds(pl.multiple_of((i * span + k) * ROWS, ROWS), ROWS) for k in range(span)
        ]
        counts = [counts_ref[r, :] for r in rows]
        sizes = [TIME_STEP / n.astype(jnp.float32) for n in counts]
        most = counts[0]
        for n in counts[1:]:
            most = jnp.maximum(most, n)
        turns = jnp.max(most)
        conc, internal = [], []
        for r in rows:
            u = [third_ref[c, r, :] for c in range(NCOMP)]
            rho = ((u[0] + u[1]) + (u[2] + u[3])) + ((u[4] + u[5]) + (u[6] + u[7])) + u[8]
            internal.append(
                u[12] - 0.5 * (u[9] * u[9] + u[10] * u[10] + u[11] * u[11]) / rho)
            conc.append([u[k] * float(GAS[k]) for k in range(9)])

        def advance(index, carry):
            new = []
            for k in range(span):
                moved = react(carry[k], internal[k], sizes[k])
                keep = index < counts[k]
                new.append([jnp.where(keep, m, o) for m, o in zip(moved, carry[k])])
            return new

        conc = lax.fori_loop(0, turns, advance, conc)
        for k in range(span):
            for c in range(9):
                out_ref[c, rows[k], :] = conc[k][c] * float(MOLAR[c])
        return 0

    lax.fori_loop(0, planes // span, block, 0)


def shape(*dims):
    return jax.ShapeDtypeStruct(dims, jnp.float32)


def call(kernel, out_shape, scratch, n_in, scalars=True):
    vmem = pl.BlockSpec(memory_space=pltpu.VMEM)
    specs = [vmem] * n_in
    if scalars:
        specs[0] = pl.BlockSpec(memory_space=pltpu.SMEM)
    return pl.pallas_call(
        kernel,
        out_shape=out_shape,
        in_specs=specs,
        out_specs=jax.tree.map(lambda _: vmem, out_shape),
        scratch_shapes=[pltpu.VMEM(dims, jnp.float32) for dims in scratch],
        compiler_params=pltpu.CompilerParams(vmem_limit_bytes=48 * 1024 * 1024),
    )


def moved(value, axis, steps, closed):
    count = lax.axis_size(axis)
    pairs = [(i, (i + steps) % count) for i in range(count) if closed or 0 <= i + steps < count]
    return lax.ppermute(value, axis, pairs)


def on_device(state, fresh, substeps, shift):
    comps, planes, width_y, width_z = state.shape
    cross = planes * width_y
    zvecs = width_z // ROWS
    tubes = lax.axis_size("tube")
    tube = lax.axis_index("tube")
    swap = tubes == 2
    x_msgs = 1 if swap else 2
    begins = [jnp.where(tube == 0, planes - HALO, 0), 0] if swap else [0, planes - HALO]
    place = jnp.stack([
        tube.astype(jnp.int32), jnp.int32(tubes), jnp.asarray(begins[0], jnp.int32),
        jnp.asarray(begins[1], jnp.int32), shift.astype(jnp.int32)])

    full = shape(comps, cross, width_z)
    fullz = shape(comps, width_z + 2 * ROWS, cross)
    xs = shape(comps, HALO * ROWS, width_z)
    ys = shape(comps, HALO * planes, width_z)
    zs = shape(comps, ROWS, cross)
    sent = (full, fullz) + (xs,) * x_msgs + (ys, ys, zs, zs)
    flat = state.reshape(comps, cross, width_z)

    def shifted(reach):
        def branch():
            ahead = moved(flat[:, :reach * width_y], "tube", -1, False)
            return call(
                functools.partial(assemble_kernel, planes, width_y, width_z, x_msgs),
                sent, [((planes + reach) * ROWS, width_z)], 4,
            )(place, flat, ahead, fresh)
        return branch

    pieces = 4
    size = SMAX // pieces
    start, uz, *msgs = lax.switch(
        (shift.astype(jnp.int32) - 1) // size, [shifted((n + 1) * size) for n in range(pieces)])

    in_x, in_y, in_z = shape(cross, width_z), shape(cross, width_z), shape(
        width_z + 2 * ROWS, cross)
    inner_out = (in_x,) * 3 + (in_y,) * 3 + (in_z,) * 3 + (full, full, shape(comps, width_z, cross))
    al = [((planes + 1) * ROWS, width_z), ((width_y + 1) * planes, width_z),
          ((zvecs + 1) * ROWS, cross)]
    inner_scratch = al + [(3, cross, width_z)]
    outer_scratch = [
        (comps, 2 * HALO * ROWS, width_z), (3, 2 * HALO * ROWS, width_z),
        (3, 2 * HALO * planes, width_z), (3, 2 * ROWS, cross),
        *al, (comps, 2 * HALO * ROWS, width_z), (comps, cross, width_z), (comps, width_z, cross)]
    current = start
    for stage in (1, 2, 3):
        xmsg, (ylo, yhi, zlo, zhi) = msgs[:x_msgs], msgs[x_msgs:]
        ylo = moved(ylo, "gy", 1, True)
        yhi = moved(yhi, "gy", -1, True)
        if swap:
            xlo = xhi = lax.ppermute(xmsg[0], "tube", [(0, 1), (1, 0)])
        else:
            xhi = moved(xmsg[0], "tube", -1, False)
            xlo = moved(xmsg[1], "tube", 1, False)
        zlo = moved(zlo, "gz", 1, True)
        zhi = moved(zhi, "gz", -1, True)
        inner = call(
            functools.partial(inner_kernel, planes, width_y, width_z),
            inner_out, inner_scratch, 2, False)(current, uz)
        current, *rest = call(
            functools.partial(outer_kernel, stage, planes, width_y, width_z, x_msgs),
            (full,) if stage == 3 else sent, outer_scratch, 11 + len(inner_out),
        )(place, current, uz, start, fresh, xlo, xhi, ylo, yhi, zlo, zhi, *inner)
        if stage < 3:
            uz, *msgs = rest

    vmem = pl.BlockSpec(memory_space=pltpu.VMEM)
    reacted = pl.pallas_call(
        functools.partial(chemistry_kernel, planes, 4),
        out_shape=full,
        in_specs=[vmem, vmem],
        out_specs=vmem,
        compiler_params=pltpu.CompilerParams(vmem_limit_bytes=48 * 1024 * 1024),
    )(current, substeps.reshape(cross, width_z))
    return reacted.reshape(state.shape)


def solution(mesh):
    return jax.shard_map(
        on_device,
        mesh=mesh,
        in_specs=(P(None, "tube", "gy", "gz"), P(None, "gy", "gz"), P("tube", "gy", "gz"), P()),
        out_specs=P(None, "tube", "gy", "gz"),
        check_vma=False,
    )
```

```python
import functools

import jax
import jax.numpy as jnp
import numpy as np
from jax import lax
from jax.experimental import pallas as pl
from jax.experimental.pallas import tpu as pltpu
from jax.sharding import PartitionSpec as P

SMAX = 12
HALO = 3
NCOMP = 13
ROWS = 8
SCALE = 0.25
TIME_STEP = 0.05
FLUX_FACTOR = -TIME_STEP / (6.0 * SCALE)

MOLAR = np.array([2.016, 31.998, 18.015, 1.008, 15.999, 17.007, 33.006, 34.014, 28.014]) / 18.015
GAS = 1.0 / MOLAR
FORMATION = np.array([0.0, 0.0, -1.5, 12.0, 1.5, 0.25, 0.02, -0.45, 0.0])
REACTANTS = [
    (3, 1), (4, 5), (4, 0), (3, 5), (0, 5), (2, 3), (4, 2), (5, 5), (0, 8), (3, 3, 8), (4, 4, 8),
    (3, 4, 8), (3, 5, 8), (3, 1, 8), (6, 3), (6, 3), (6, 4), (6, 5), (6, 6), (7, 8), (7, 3),
]
PRODUCTS = [
    (4, 5), (3, 1), (3, 5), (4, 0), (2, 3), (0, 5), (5, 5), (4, 2), (3, 3), (0,), (1,),
    (5,), (2,), (6,), (0, 1), (5, 5), (1, 5), (2, 1), (7, 1), (5, 5), (2, 5),
]
PREFACTOR = [
    30.0, 8.0, 20.0, 6.0, 25.0, 10.0, 12.0, 5.0, 4.0, 20.0, 15.0,
    18.0, 22.0, 25.0, 30.0, 25.0, 20.0, 30.0, 10.0, 6.0, 15.0,
]
BARRIER = [
    4.0, 1.0, 3.0, 1.5, 1.5, 4.5, 4.0, 1.5, 6.0, 0.5, 0.5,
    0.5, 0.5, 0.3, 0.8, 0.5, 0.3, 0.3, 0.5, 5.0, 1.5,
]

KAPPA = 0.609375
EPS = 3.0 * SCALE * SCALE * 1e-6


def rcp(x):
    return pl.reciprocal(x, approx=True)


def correction(d1, d2, d3, d4):
    k2 = KAPPA * (d2 * d2) + EPS
    k3 = KAPPA * (d3 * d3) + EPS
    xa = d1 - 1.375 * d2
    xb = d3 - 0.625 * d2
    xc = d4 - 1.375 * d3
    ra = rcp(xa * xa + k2)
    rb = rcp(xb * xb + k2)
    rc = rcp(xc * xc + k3)
    wa = ra * ra
    wb = 6.0 * (rb * rb)
    wc = 3.0 * (rc * rc)
    return ((xa + xb) * wa + (0.5 * (d2 + d4) - d3) * wc) * rcp(wa + wb + wc)


def face_flux(du, df, f2, f3, alpha):
    e = [alpha * d for d in du]
    p = [df[k] + e[k] for k in range(4)]
    m = [None] + [df[k] - e[k] for k in range(1, 5)]
    linear = 3.0 * (f2 + f3) - e[2] + 0.5 * (p[1] - m[3])
    return linear - correction(p[0], p[1], p[2], p[3]) + correction(m[4], m[3], m[2], m[1])


def sweep(cells, fluxes, alpha, first, last):
    du, df = {}, {}
    out = {}
    for j in range(first, last + 1):
        for k in range(j, j + 5):
            if k not in du:
                du[k] = cells(k + 1) - cells(k)
                df[k] = fluxes(k + 1) - fluxes(k)
        out[j] = face_flux(
            [du[k] for k in range(j, j + 5)],
            [df[k] for k in range(j, j + 5)],
            fluxes(j + 2),
            fluxes(j + 3),
            alpha(j),
        )
    return out


def memo(load):
    return functools.lru_cache(maxsize=None)(load)


def thermo(u):
    g = [u[k] if GAS[k] == 1.0 else u[k] * float(GAS[k]) for k in range(9)]
    s2 = g[2] + g[6] + g[7]
    s3 = g[3] + g[4]
    gas = (g[0] + g[1]) + (g[5] + g[8]) + (s2 + s3)
    heat = 2.5 * gas + (0.5 * s2 - s3)
    bond = 1.5 * (u[4] - u[2]) + 12.0 * u[3] + 0.25 * u[5] + 0.02 * u[6] - 0.45 * u[7]
    rho = ((u[0] + u[1]) + (u[2] + u[3])) + ((u[4] + u[5]) + (u[6] + u[7])) + u[8]
    back = 1.0 / rho
    cold = 1.0 / heat
    motion = 0.5 * (u[9] * u[9] + u[10] * u[10] + u[11] * u[11]) * back
    temperature = (u[12] - motion - bond) * cold
    pressure = gas * temperature
    sound = jnp.sqrt((1.0 + gas * cold) * pressure * back)
    return back, pressure, sound


def for_components(dim, body):
    special = 8 + dim

    def step(i, _):
        body(i + jnp.where(i >= special, 1, 0).astype(jnp.int32), 0)
        return 0

    lax.fori_loop(0, NCOMP - 2, step, 0)
    body(special, 1)
    body(NCOMP - 1, 2)


def flux_of(u, speed, pressure, kind):
    if kind == 0:
        return u * speed
    if kind == 1:
        return u * speed + SCALE * pressure()
    return (u + pressure()) * speed


def own_thermo(planes, width_y, u_ref, x_refs, y_refs, z_refs, tmp):
    def own(i, _):
        for k in range(2):
            p = i * 2 + k
            here = pl.ds(pl.multiple_of(p * ROWS, ROWS), ROWS)
            u = [u_ref[c, here, :] for c in range(NCOMP)]
            back, pressure, sound = thermo(u)
            back, sound = SCALE * back, SCALE * sound
            across = pl.ds(p, width_y, stride=planes)
            for d, where in ((0, here), (1, across), (2, here)):
                speed = u[9 + d] * back
                for n, value in enumerate((speed, pressure, jnp.abs(speed) + sound)):
                    if d == 2:
                        tmp[n, where, :] = value
                    else:
                        (x_refs, y_refs)[d][n][where, :] = value
        return 0

    lax.fori_loop(0, planes // 2, own, 0)
    for n in range(3):
        z_refs[n][pl.ds(ROWS, tmp.shape[2]), :] = tmp[n].T


def inner_kernel(
    planes, width_y, width_z, u_ref, uz_ref,
    ux, px, ax, uy, py, ay, uz, pz, az, accx, accy, accz, alx, aly, alz, tmp,
):
    groups = planes // ROWS
    zvecs = width_z // ROWS
    own_thermo(planes, width_y, u_ref, (ux, px, ax), (uy, py, ay), (uz, pz, az), tmp)

    def xvec(ref):
        return lambda i: ref[pl.ds((i - HALO) * ROWS, ROWS), :]

    def yvec(ref, g):
        return lambda i: ref[pl.ds((i - HALO) * planes + g * ROWS, ROWS), :]

    def zvec(ref):
        return lambda i: ref[pl.ds(ROWS - HALO + i, ROWS, stride=zvecs), :]

    largest(xvec(ax), range(HALO, planes - HALO + 1), alx, lambda j: j * ROWS)
    for g in range(groups):
        largest(yvec(ay, g), range(HALO, width_y - HALO + 1), aly,
                lambda j: j * planes + g * ROWS)
    largest(zvec(az), range(HALO, zvecs - HALO + 1), alz, lambda j: j * ROWS)

    def inner(n, cells, speed, pressure, kind, alpha, put):
        cells = memo(cells)
        fluxes = memo(lambda i: flux_of(cells(i), speed(i), lambda: pressure(i), kind))
        out = sweep(cells, fluxes, alpha, HALO, n - HALO)
        put(HALO - 1, out[HALO])
        for i in range(HALO, n - HALO):
            put(i, out[i + 1] - out[i])
        put(n - HALO, out[n - HALO])

    def x_body(c, kind):
        def put(i, value):
            accx[c, pl.ds(i * ROWS, ROWS), :] = value
        inner(planes, lambda i: u_ref[c, pl.ds((i - HALO) * ROWS, ROWS), :], xvec(ux), xvec(px),
              kind, lambda j: alx[pl.ds(j * ROWS, ROWS), :], put)

    for_components(1, x_body)

    def z_body(c, kind):
        def put(i, value):
            accz[c, pl.ds(i, ROWS, stride=zvecs), :] = value
        inner(zvecs, lambda i: uz_ref[c, pl.ds(ROWS - HALO + i, ROWS, stride=zvecs), :],
              zvec(uz), zvec(pz), kind, lambda j: alz[pl.ds(j * ROWS, ROWS), :], put)

    for_components(3, z_body)

    def y_body(c, kind):
        for g in range(groups):
            def put(i, value, g=g):
                accy[c, pl.ds(g * ROWS * width_y + i, ROWS, stride=width_y), :] = value
            def cell(i, g=g):
                return u_ref[c, pl.ds(g * ROWS * width_y + i - HALO, ROWS, stride=width_y), :]
            inner(width_y, cell, yvec(uy, g), yvec(py, g), kind,
                  lambda j: aly[pl.ds(j * planes + g * ROWS, ROWS), :], put)

    for_components(2, y_body)


def largest(speed, faces, ref, place):
    values = memo(speed)
    for j in faces:
        top = values(j)
        for k in range(1, 6):
            top = jnp.maximum(top, values(j + k))
        ref[pl.ds(place(j), ROWS), :] = top


def outer_kernel(
    stage, planes, width_y, width_z, x_msgs, place,
    u_ref, uz_ref, start_ref, fresh_ref, xlo_ref, xhi_ref, ylo_ref, yhi_ref, zall_ref,
    ux, px, ax, uy, py, ay, uz, pz, az, accx, accy, accz, *refs,
):
    groups = planes // ROWS
    zvecs = width_z // ROWS
    tube, tubes = place[0], place[1]
    last = stage == 3
    refs = list(refs)
    new_ref = refs.pop(0)
    if not last:
        newz_ref = refs.pop(0)
        xmsg_refs = [refs.pop(0) for _ in range(x_msgs)]
        ymsg_lo, ymsg_hi, zmsg = [refs.pop(0) for _ in range(3)]
    xh, gx, gy, gz, alx, aly, alz, edgex, edgey, edgez = refs

    def ghosts(c, _):
        for k in range(HALO):
            here = pl.ds(k * ROWS, ROWS)
            lo = jnp.where(tube == 0, u_ref[c, pl.ds(0, ROWS), :], xlo_ref[c, here, :])
            hi = jnp.where(tube == tubes - 1, fresh_ref[c], xhi_ref[c, here, :])
            xh[c, here, :] = lo
            xh[c, pl.ds((HALO + k) * ROWS, ROWS), :] = hi
        return 0

    lax.fori_loop(0, NCOMP, ghosts, 0)

    def ghost_thermo(u, d, ref, row):
        back, pressure, sound = thermo(u)
        speed = u[9 + d] * (SCALE * back)
        for n, value in enumerate((speed, pressure, jnp.abs(speed) + SCALE * sound)):
            ref[n, pl.ds(row, ROWS), :] = value

    for k in range(2 * HALO):
        ghost_thermo([xh[c, pl.ds(k * ROWS, ROWS), :] for c in range(NCOMP)], 0, gx, k * ROWS)
    for ref, offset in ((ylo_ref, 0), (yhi_ref, HALO)):
        def ghost_y(k, _, ref=ref, offset=offset):
            for g in range(groups):
                row = pl.multiple_of(k * planes + g * ROWS, ROWS)
                u = [ref[c, pl.ds(row, ROWS), :] for c in range(NCOMP)]
                ghost_thermo(u, 1, gy, pl.multiple_of(offset * planes + row, ROWS))
            return 0
        lax.fori_loop(0, HALO, ghost_y, 0)
    zlo, zhi = place[5], place[6]
    ghost_thermo([zall_ref[zlo, c] for c in range(NCOMP)], 2, gz, 0)
    ghost_thermo([zall_ref[zhi, c] for c in range(NCOMP)], 2, gz, ROWS)

    def xvec(ref, n):
        def load(i):
            if HALO <= i < planes + HALO:
                return ref[pl.ds((i - HALO) * ROWS, ROWS), :]
            return gx[n, pl.ds((i if i < HALO else i - planes) * ROWS, ROWS), :]
        return load

    def yvec(ref, n, g):
        def load(i):
            if HALO <= i < width_y + HALO:
                return ref[pl.ds((i - HALO) * planes + g * ROWS, ROWS), :]
            return gy[n, pl.ds((i if i < HALO else i - width_y) * planes + g * ROWS, ROWS), :]
        return load

    row = lax.broadcasted_iota(jnp.int32, (ROWS, planes * width_y), 0)

    def joined(i, load, lo, hi):
        value = load(pl.ds(ROWS - HALO + i, ROWS, stride=zvecs))
        if i < HALO:
            return jnp.where(row == 0, lo(pl.ds(HALO + i, 1)), value)
        if i >= zvecs + HALO:
            return jnp.where(row == ROWS - 1, hi(pl.ds(i - zvecs - HALO, 1)), value)
        return value

    def zvec(ref, n):
        def load(i):
            return joined(i, lambda s: ref[s, :], lambda s: gz[n, s, :],
                          lambda s: gz[n, pl.ds(ROWS + s.start, 1), :])
        return load

    def ends(n):
        return list(range(HALO)) + list(range(n - HALO + 1, n + 1))

    largest(xvec(ax, 2), ends(planes), alx, lambda j: j * ROWS)
    for g in range(groups):
        largest(yvec(ay, 2, g), ends(width_y), aly, lambda j: j * planes + g * ROWS)
    largest(zvec(az, 2), ends(zvecs), alz, lambda j: j * ROWS)

    def outer(n, cells, speed, pressure, kind, alpha, given, put):
        cells = memo(cells)
        fluxes = memo(lambda i: flux_of(cells(i), speed(i), lambda: pressure(i), kind))
        out = sweep(cells, fluxes, alpha, 0, HALO - 1)
        out[HALO] = given(HALO - 1)
        for i in range(HALO):
            put(i, out[i + 1] - out[i])
        out = sweep(cells, fluxes, alpha, n - HALO + 1, n)
        out[n - HALO] = given(n - HALO)
        for i in range(n - HALO, n):
            put(i, out[i + 1] - out[i])

    def x_body(c, kind):
        def cell(i):
            if HALO <= i < planes + HALO:
                return u_ref[c, pl.ds((i - HALO) * ROWS, ROWS), :]
            return xh[c, pl.ds((i if i < HALO else i - planes) * ROWS, ROWS), :]
        def put(i, value):
            edgex[c, pl.ds((i if i < HALO else i - planes + 2 * HALO) * ROWS, ROWS), :] = value
        outer(planes, cell, xvec(ux, 0), xvec(px, 1), kind,
              lambda j: alx[pl.ds(j * ROWS, ROWS), :],
              lambda i: accx[c, pl.ds(i * ROWS, ROWS), :], put)

    for_components(1, x_body)

    def z_body(c, kind):
        def cell(i):
            return joined(i, lambda s: uz_ref[c, s, :], lambda s: zall_ref[zlo, c, s, :],
                          lambda s: zall_ref[zhi, c, s, :])
        def put(i, value):
            edgez[c, pl.ds(i, ROWS, stride=zvecs), :] = value
        outer(zvecs, cell, zvec(uz, 0), zvec(pz, 1), kind,
              lambda j: alz[pl.ds(j * ROWS, ROWS), :],
              lambda i: accz[c, pl.ds(i, ROWS, stride=zvecs), :], put)

    for_components(3, z_body)

    def y_body(c, kind):
        for g in range(groups):
            base = g * ROWS * width_y
            def cell(i, g=g, base=base):
                if HALO <= i < width_y + HALO:
                    return u_ref[c, pl.ds(base + i - HALO, ROWS, stride=width_y), :]
                if i < HALO:
                    return ylo_ref[c, pl.ds(i * planes + g * ROWS, ROWS), :]
                return yhi_ref[c, pl.ds((i - HALO - width_y) * planes + g * ROWS, ROWS), :]
            def put(i, value, base=base):
                edgey[c, pl.ds(base + i, ROWS, stride=width_y), :] = value
            outer(width_y, cell, yvec(uy, 0, g), yvec(py, 1, g), kind,
                  lambda j: aly[pl.ds(j * planes + g * ROWS, ROWS), :],
                  lambda i: accy[c, pl.ds(base + i, ROWS, stride=width_y), :], put)

    for_components(2, y_body)

    def between(n, rows, width):
        position = lax.broadcasted_iota(jnp.int32, (rows, width), 0) % n
        return (position >= HALO) & (position < n - HALO)

    inside_y = between(width_y, planes * width_y, width_z)
    inside_z = between(zvecs, width_z, planes * width_y)

    def combine(c, _):
        change_z = jnp.where(inside_z, accz[c], edgez[c]).T
        change_y = jnp.where(inside_y, accy[c], edgey[c])
        low, high = HALO * ROWS, (planes - HALO) * ROWS
        change_x = jnp.concatenate([
            edgex[c, pl.ds(0, low), :], accx[c, pl.ds(low, high - low), :],
            edgex[c, pl.ds(low, low), :]], axis=0)
        change = FLUX_FACTOR * (change_x + change_y + change_z)
        if stage == 1:
            value = u_ref[c] + change
        elif stage == 2:
            value = 0.75 * start_ref[c] + 0.25 * (u_ref[c] + change)
        else:
            value = (1.0 / 3.0) * start_ref[c] + (2.0 / 3.0) * (u_ref[c] + change)
        new_ref[c] = value
        if not last:
            newz_ref[c, pl.ds(ROWS, width_z), :] = value.T
        return 0

    lax.fori_loop(0, NCOMP, combine, 0)
    if not last:
        messages(planes, width_y, width_z, place, new_ref, newz_ref, xmsg_refs,
                 ymsg_lo, ymsg_hi, zmsg)


def messages(planes, width_y, width_z, place, u_ref, uz_ref, xmsg_refs, ylo, yhi, zmsg):
    def body(c, _):
        for n, ref in enumerate(xmsg_refs):
            begin = place[2 + n]
            for k in range(HALO):
                rows = pl.ds(pl.multiple_of((begin + k) * ROWS, ROWS), ROWS)
                ref[c, pl.ds(k * ROWS, ROWS), :] = u_ref[c, rows, :]
        for k in range(HALO):
            for g in range(planes // ROWS):
                there = pl.ds(k * planes + g * ROWS, ROWS)
                base = g * ROWS * width_y + k
                yhi[c, there, :] = u_ref[c, pl.ds(base, ROWS, stride=width_y), :]
                ylo[c, there, :] = u_ref[
                    c, pl.ds(base + width_y - HALO, ROWS, stride=width_y), :]
        zmsg[c, pl.ds(0, HALO), :] = uz_ref[c, pl.ds(ROWS, HALO), :]
        zmsg[c, pl.ds(HALO, HALO), :] = uz_ref[c, pl.ds(ROWS + width_z - HALO, HALO), :]
        return 0

    lax.fori_loop(0, NCOMP, body, 0)


def assemble_kernel(
    planes, width_y, width_z, x_msgs, place, state_ref, ahead_ref, fresh_ref, u_ref, uz_ref, *refs,
):
    refs = list(refs)
    xmsg_refs = [refs.pop(0) for _ in range(x_msgs)]
    ymsg_lo, ymsg_hi, zmsg, joined = refs
    tube, tubes, shift = place[0], place[1], place[4]
    total = planes + ahead_ref.shape[1] // ROWS

    def body(c, _):
        joined[pl.ds(0, planes * ROWS), :] = state_ref[c]
        fresh = fresh_ref[c]
        for i in range(planes, total):
            value = ahead_ref[c, pl.ds((i - planes) * ROWS, ROWS), :]
            joined[pl.ds(i * ROWS, ROWS), :] = jnp.where(tube == tubes - 1, fresh, value)
        for i in range(planes):
            u_ref[c, pl.ds(i * ROWS, ROWS), :] = joined[
                pl.ds(pl.multiple_of((shift + i) * ROWS, ROWS), ROWS), :]
        uz_ref[c, pl.ds(ROWS, width_z), :] = u_ref[c].T
        return 0

    lax.fori_loop(0, NCOMP, body, 0)
    messages(planes, width_y, width_z, place, u_ref, uz_ref, xmsg_refs,
             ymsg_lo, ymsg_hi, zmsg)


def powers_of(back):
    a = jnp.exp(-0.5 * back)
    b = jnp.exp(-0.3 * back)
    a2 = a * a
    a3 = a2 * a
    a4 = a2 * a2
    a6 = a3 * a3
    a8 = a4 * a4
    return {0.5: a, 0.3: b, 1.0: a2, 1.5: a3, 3.0: a6, 4.0: a8, 4.5: a8 * a, 5.0: a8 * a2,
            6.0: a6 * a6, 0.8: a * b}


def react(conc, internal, size):
    s2 = conc[2] + conc[6] + conc[7]
    s3 = conc[3] + conc[4]
    heat = 2.5 * (((conc[0] + conc[1]) + (conc[5] + conc[8])) + (s2 + s3)) + (0.5 * s2 - s3)
    bond = None
    for k in range(9):
        if FORMATION[k]:
            term = float(FORMATION[k] * MOLAR[k]) * conc[k]
            bond = term if bond is None else bond + term
    boltzmann = powers_of(heat / (internal - bond))
    pairs = {}
    omega = [None] * 9

    def add(k, value):
        omega[k] = value if omega[k] is None else omega[k] + value

    def sub(k, value):
        omega[k] = -value if omega[k] is None else omega[k] - value

    def rate(j):
        names = REACTANTS[j]
        key = tuple(sorted(names))
        if key not in pairs:
            value = conc[names[0]] * conc[names[1]]
            if len(names) == 3:
                base = tuple(sorted(names[:2]))
                if base not in pairs:
                    pairs[base] = value
                value = pairs[base] * conc[8]
            pairs[key] = value
        return (PREFACTOR[j] * boltzmann[BARRIER[j]]) * pairs[key]

    j = 0
    while j < len(REACTANTS):
        value = rate(j)
        back = j + 1 < len(REACTANTS) and REACTANTS[j + 1] == PRODUCTS[j] \
            and PRODUCTS[j + 1] == REACTANTS[j]
        if back:
            value = value - rate(j + 1)
        for k in range(9):
            times = PRODUCTS[j].count(k) - REACTANTS[j].count(k)
            if times == 0:
                continue
            amount = value if abs(times) == 1 else value + value
            if times > 0:
                add(k, amount)
            else:
                sub(k, amount)
        j += 2 if back else 1
    return [conc[k] + size * omega[k] for k in range(9)]


def chemistry_kernel(planes, span, third_ref, counts_ref, out_ref):
    for c in range(9, NCOMP):
        out_ref[c] = third_ref[c]

    def block(i, _):
        rows = [
            pl.ds(pl.multiple_of((i * span + k) * ROWS, ROWS), ROWS) for k in range(span)
        ]
        counts = [counts_ref[r, :] for r in rows]
        sizes = [TIME_STEP / n.astype(jnp.float32) for n in counts]
        most = counts[0]
        for n in counts[1:]:
            most = jnp.maximum(most, n)
        turns = jnp.max(most)
        conc, internal = [], []
        for r in rows:
            u = [third_ref[c, r, :] for c in range(NCOMP)]
            rho = ((u[0] + u[1]) + (u[2] + u[3])) + ((u[4] + u[5]) + (u[6] + u[7])) + u[8]
            internal.append(
                u[12] - 0.5 * (u[9] * u[9] + u[10] * u[10] + u[11] * u[11]) / rho)
            conc.append([u[k] * float(GAS[k]) for k in range(9)])

        def advance(index, carry):
            new = []
            for k in range(span):
                moved = react(carry[k], internal[k], sizes[k])
                keep = index < counts[k]
                new.append([jnp.where(keep, m, o) for m, o in zip(moved, carry[k])])
            return new

        conc = lax.fori_loop(0, turns, advance, conc)
        for k in range(span):
            for c in range(9):
                out_ref[c, rows[k], :] = conc[k][c] * float(MOLAR[c])
        return 0

    lax.fori_loop(0, planes // span, block, 0)


def shape(*dims):
    return jax.ShapeDtypeStruct(dims, jnp.float32)


def call(kernel, out_shape, scratch, n_in, scalars=True):
    vmem = pl.BlockSpec(memory_space=pltpu.VMEM)
    specs = [vmem] * n_in
    if scalars:
        specs[0] = pl.BlockSpec(memory_space=pltpu.SMEM)
    return pl.pallas_call(
        kernel,
        out_shape=out_shape,
        in_specs=specs,
        out_specs=jax.tree.map(lambda _: vmem, out_shape),
        scratch_shapes=[pltpu.VMEM(dims, jnp.float32) for dims in scratch],
        compiler_params=pltpu.CompilerParams(vmem_limit_bytes=16 * 1024 * 1024),
    )


def moved(value, axis, steps, closed):
    count = lax.axis_size(axis)
    pairs = [(i, (i + steps) % count) for i in range(count) if closed or 0 <= i + steps < count]
    return lax.ppermute(value, axis, pairs)


def on_device(state, fresh, substeps, shift):
    comps, planes, width_y, width_z = state.shape
    cross = planes * width_y
    zvecs = width_z // ROWS
    tubes = lax.axis_size("tube")
    tube = lax.axis_index("tube")
    slabs = lax.axis_size("gz")
    swap = tubes == 2
    x_msgs = 1 if swap else 2
    begins = [jnp.where(tube == 0, planes - HALO, 0), 0] if swap else [0, planes - HALO]
    place = jnp.stack([
        tube.astype(jnp.int32), jnp.int32(tubes), jnp.asarray(begins[0], jnp.int32),
        jnp.asarray(begins[1], jnp.int32), shift.astype(jnp.int32),
        (lax.axis_index("gz") - 1) % slabs, (lax.axis_index("gz") + 1) % slabs])

    full = shape(comps, cross, width_z)
    fullz = shape(comps, width_z + 2 * ROWS, cross)
    xs = shape(comps, HALO * ROWS, width_z)
    ys = shape(comps, HALO * planes, width_z)
    zs = shape(comps, ROWS, cross)
    sent = (full, fullz) + (xs,) * x_msgs + (ys, ys, zs)
    flat = state.reshape(comps, cross, width_z)

    def shifted(reach):
        def branch():
            ahead = moved(flat[:, :reach * width_y], "tube", -1, False)
            return call(
                functools.partial(assemble_kernel, planes, width_y, width_z, x_msgs),
                sent, [((planes + reach) * ROWS, width_z)], 4,
            )(place, flat, ahead, fresh)
        return branch

    pieces = 4
    size = SMAX // pieces
    start, uz, *msgs = lax.switch(
        (shift.astype(jnp.int32) - 1) // size, [shifted((n + 1) * size) for n in range(pieces)])

    in_x, in_y, in_z = shape(cross, width_z), shape(cross, width_z), shape(
        width_z + 2 * ROWS, cross)
    inner_out = (in_x,) * 3 + (in_y,) * 3 + (in_z,) * 3 + (full, full, shape(comps, width_z, cross))
    al = [((planes + 1) * ROWS, width_z), ((width_y + 1) * planes, width_z),
          ((zvecs + 1) * ROWS, cross)]
    inner_scratch = al + [(3, cross, width_z)]
    outer_scratch = [
        (comps, 2 * HALO * ROWS, width_z), (3, 2 * HALO * ROWS, width_z),
        (3, 2 * HALO * planes, width_z), (3, 2 * ROWS, cross),
        *al, (comps, 2 * HALO * ROWS, width_z), (comps, cross, width_z), (comps, width_z, cross)]
    current = start
    for stage in (1, 2, 3):
        xmsg, (ylo, yhi, zmsg) = msgs[:x_msgs], msgs[x_msgs:]
        zall = lax.all_gather(zmsg, "gz")
        ylo = moved(ylo, "gy", 1, True)
        yhi = moved(yhi, "gy", -1, True)
        if swap:
            xlo = xhi = lax.ppermute(xmsg[0], "tube", [(0, 1), (1, 0)])
        else:
            xhi = moved(xmsg[0], "tube", -1, False)
            xlo = moved(xmsg[1], "tube", 1, False)
        inner = call(
            functools.partial(inner_kernel, planes, width_y, width_z),
            inner_out, inner_scratch, 2, False)(current, uz)
        current, *rest = call(
            functools.partial(outer_kernel, stage, planes, width_y, width_z, x_msgs),
            (full,) if stage == 3 else sent, outer_scratch, 10 + len(inner_out),
        )(place, current, uz, start, fresh, xlo, xhi, ylo, yhi, zall, *inner)
        if stage < 3:
            uz, *msgs = rest

    vmem = pl.BlockSpec(memory_space=pltpu.VMEM)
    reacted = pl.pallas_call(
        functools.partial(chemistry_kernel, planes, 4),
        out_shape=full,
        in_specs=[vmem, vmem],
        out_specs=vmem,
        compiler_params=pltpu.CompilerParams(vmem_limit_bytes=16 * 1024 * 1024),
    )(current, substeps.reshape(cross, width_z))
    return reacted.reshape(state.shape)


def solution(mesh):
    return jax.shard_map(
        on_device,
        mesh=mesh,
        in_specs=(P(None, "tube", "gy", "gz"), P(None, "gy", "gz"), P("tube", "gy", "gz"), P()),
        out_specs=P(None, "tube", "gy", "gz"),
        check_vma=False,
    )
```

```python
import functools

import jax
import jax.numpy as jnp
import numpy as np
from jax import lax
from jax.experimental import pallas as pl
from jax.experimental.pallas import tpu as pltpu
from jax.sharding import PartitionSpec as P

SMAX = 12
HALO = 3
NCOMP = 13
ROWS = 8
SCALE = 0.25
TIME_STEP = 0.05
FLUX_FACTOR = -TIME_STEP / (6.0 * SCALE)

MOLAR = np.array([2.016, 31.998, 18.015, 1.008, 15.999, 17.007, 33.006, 34.014, 28.014]) / 18.015
GAS = 1.0 / MOLAR
FORMATION = np.array([0.0, 0.0, -1.5, 12.0, 1.5, 0.25, 0.02, -0.45, 0.0])
REACTANTS = [
    (3, 1), (4, 5), (4, 0), (3, 5), (0, 5), (2, 3), (4, 2), (5, 5), (0, 8), (3, 3, 8), (4, 4, 8),
    (3, 4, 8), (3, 5, 8), (3, 1, 8), (6, 3), (6, 3), (6, 4), (6, 5), (6, 6), (7, 8), (7, 3),
]
PRODUCTS = [
    (4, 5), (3, 1), (3, 5), (4, 0), (2, 3), (0, 5), (5, 5), (4, 2), (3, 3), (0,), (1,),
    (5,), (2,), (6,), (0, 1), (5, 5), (1, 5), (2, 1), (7, 1), (5, 5), (2, 5),
]
PREFACTOR = [
    30.0, 8.0, 20.0, 6.0, 25.0, 10.0, 12.0, 5.0, 4.0, 20.0, 15.0,
    18.0, 22.0, 25.0, 30.0, 25.0, 20.0, 30.0, 10.0, 6.0, 15.0,
]
BARRIER = [
    4.0, 1.0, 3.0, 1.5, 1.5, 4.5, 4.0, 1.5, 6.0, 0.5, 0.5,
    0.5, 0.5, 0.3, 0.8, 0.5, 0.3, 0.3, 0.5, 5.0, 1.5,
]

KAPPA = 0.609375
EPS = 3.0 * SCALE * SCALE * 1e-6


def rcp(x):
    return pl.reciprocal(x, approx=True)


def correction(d1, d2, d3, d4):
    k2 = KAPPA * (d2 * d2) + EPS
    k3 = KAPPA * (d3 * d3) + EPS
    xa = d1 - 1.375 * d2
    xb = d3 - 0.625 * d2
    xc = d4 - 1.375 * d3
    ra = rcp(xa * xa + k2)
    rb = rcp(xb * xb + k2)
    rc = rcp(xc * xc + k3)
    wa = ra * ra
    wb = 6.0 * (rb * rb)
    wc = 3.0 * (rc * rc)
    return ((xa + xb) * wa + (0.5 * (d2 + d4) - d3) * wc) * rcp(wa + wb + wc)


def face_flux(du, df, f2, f3, alpha):
    e = [alpha * d for d in du]
    p = [df[k] + e[k] for k in range(4)]
    m = [None] + [df[k] - e[k] for k in range(1, 5)]
    linear = 3.0 * (f2 + f3) - e[2] + 0.5 * (p[1] - m[3])
    return linear - correction(p[0], p[1], p[2], p[3]) + correction(m[4], m[3], m[2], m[1])


def sweep(cells, fluxes, alpha, first, last):
    du, df = {}, {}
    out = {}
    for j in range(first, last + 1):
        for k in range(j, j + 5):
            if k not in du:
                du[k] = cells(k + 1) - cells(k)
                df[k] = fluxes(k + 1) - fluxes(k)
        out[j] = face_flux(
            [du[k] for k in range(j, j + 5)],
            [df[k] for k in range(j, j + 5)],
            fluxes(j + 2),
            fluxes(j + 3),
            alpha(j),
        )
    return out


def memo(load):
    return functools.lru_cache(maxsize=None)(load)


def thermo(u):
    g = [u[k] if GAS[k] == 1.0 else u[k] * float(GAS[k]) for k in range(9)]
    s2 = g[2] + g[6] + g[7]
    s3 = g[3] + g[4]
    gas = (g[0] + g[1]) + (g[5] + g[8]) + (s2 + s3)
    heat = 2.5 * gas + (0.5 * s2 - s3)
    bond = 1.5 * (u[4] - u[2]) + 12.0 * u[3] + 0.25 * u[5] + 0.02 * u[6] - 0.45 * u[7]
    rho = ((u[0] + u[1]) + (u[2] + u[3])) + ((u[4] + u[5]) + (u[6] + u[7])) + u[8]
    back = 1.0 / rho
    cold = 1.0 / heat
    motion = 0.5 * (u[9] * u[9] + u[10] * u[10] + u[11] * u[11]) * back
    temperature = (u[12] - motion - bond) * cold
    pressure = gas * temperature
    sound = jnp.sqrt((1.0 + gas * cold) * pressure * back)
    return back, pressure, sound


def for_components(dim, body):
    special = 8 + dim
    generic = NCOMP - 2

    def nth(i):
        i = jnp.maximum(i, 0)
        return i + jnp.where(i >= special, 1, 0).astype(jnp.int32)

    def step(i, _):
        body(nth(i), 0, lambda n: nth(i - n))
        return 0

    lax.fori_loop(0, generic, step, 0)
    order = [k for k in range(NCOMP - 1) if k != special] + [special, NCOMP - 1]
    for turn in (generic, generic + 1):
        body(order[turn], turn - generic + 1, lambda n, turn=turn: order[turn - n])
    return order


def flux_of(u, speed, pressure, kind):
    if kind == 0:
        return u * speed
    if kind == 1:
        return u * speed + SCALE * pressure()
    return (u + pressure()) * speed


def own_thermo(planes, width_y, u_ref, x_refs, y_refs, z_refs, tmp):
    span = planes // 2

    def own(i, _):
        for k in range(span):
            p = i * span + k
            here = pl.ds(pl.multiple_of(p * ROWS, ROWS), ROWS)
            u = [u_ref[c, here, :] for c in range(NCOMP)]
            back, pressure, sound = thermo(u)
            back, sound = SCALE * back, SCALE * sound
            across = pl.ds(p, width_y, stride=planes)
            for d, where in ((0, here), (1, across), (2, here)):
                speed = u[9 + d] * back
                for n, value in enumerate((speed, pressure, jnp.abs(speed) + sound)):
                    if d == 2:
                        tmp[n, where, :] = value
                    else:
                        (x_refs, y_refs)[d][n][where, :] = value
        return 0

    lax.fori_loop(0, planes // span, own, 0)
    for n in range(3):
        z_refs[n][pl.ds(ROWS, tmp.shape[2]), :] = tmp[n].T


def inner_kernel(
    planes, width_y, width_z, u_ref, uz_ref,
    ux, px, ax, uy, py, ay, uz, pz, az, accx, accy, accz, alx, aly, alz, tmp,
):
    groups = planes // ROWS
    zvecs = width_z // ROWS
    own_thermo(planes, width_y, u_ref, (ux, px, ax), (uy, py, ay), (uz, pz, az), tmp)

    def xvec(ref):
        return lambda i: ref[pl.ds((i - HALO) * ROWS, ROWS), :]

    def yvec(ref, g):
        return lambda i: ref[pl.ds((i - HALO) * planes + g * ROWS, ROWS), :]

    def zvec(ref):
        return lambda i: ref[pl.ds(ROWS - HALO + i, ROWS, stride=zvecs), :]

    largest(xvec(ax), range(HALO, planes - HALO + 1), alx, lambda j: j * ROWS)
    for g in range(groups):
        largest(yvec(ay, g), range(HALO, width_y - HALO + 1), aly,
                lambda j: j * planes + g * ROWS)
    largest(zvec(az), range(HALO, zvecs - HALO + 1), alz, lambda j: j * ROWS)

    def inner(n, cells, speed, pressure, kind, alpha, put):
        cells = memo(cells)
        fluxes = memo(lambda i: flux_of(cells(i), speed(i), lambda: pressure(i), kind))
        out = sweep(cells, fluxes, alpha, HALO, n - HALO)
        put(HALO - 1, out[HALO])
        for i in range(HALO, n - HALO):
            put(i, out[i + 1] - out[i])
        put(n - HALO, out[n - HALO])

    def x_body(c, kind, before):
        def put(i, value):
            accx[c, pl.ds(i * ROWS, ROWS), :] = value
        inner(planes, lambda i: u_ref[c, pl.ds((i - HALO) * ROWS, ROWS), :], xvec(ux), xvec(px),
              kind, lambda j: alx[pl.ds(j * ROWS, ROWS), :], put)

    for_components(1, x_body)

    def z_body(c, kind, before):
        def put(i, value):
            accz[c, pl.ds(i, ROWS, stride=zvecs), :] = value
        inner(zvecs, lambda i: uz_ref[c, pl.ds(ROWS - HALO + i, ROWS, stride=zvecs), :],
              zvec(uz), zvec(pz), kind, lambda j: alz[pl.ds(j * ROWS, ROWS), :], put)

    for_components(3, z_body)

    def y_body(c, kind, before):
        for g in range(groups):
            def put(i, value, g=g):
                accy[c, pl.ds(g * ROWS * width_y + i, ROWS, stride=width_y), :] = value
            def cell(i, g=g):
                return u_ref[c, pl.ds(g * ROWS * width_y + i - HALO, ROWS, stride=width_y), :]
            inner(width_y, cell, yvec(uy, g), yvec(py, g), kind,
                  lambda j: aly[pl.ds(j * planes + g * ROWS, ROWS), :], put)

    for_components(2, y_body)


def largest(speed, faces, ref, place):
    values = memo(speed)
    for j in faces:
        top = values(j)
        for k in range(1, 6):
            top = jnp.maximum(top, values(j + k))
        ref[pl.ds(place(j), ROWS), :] = top


def outer_kernel(
    stage, planes, width_y, width_z, x_msgs, place,
    u_ref, uz_ref, start_ref, fresh_ref, xlo_ref, xhi_ref, ylo_ref, yhi_ref, zlo_ref, zhi_ref,
    ux, px, ax, uy, py, ay, uz, pz, az, accx, accy, accz, *refs,
):
    groups = planes // ROWS
    zvecs = width_z // ROWS
    tube, tubes = place[0], place[1]
    last = stage == 3
    refs = list(refs)
    new_ref = refs.pop(0)
    if not last:
        newz_ref = refs.pop(0)
        xmsg_refs = [refs.pop(0) for _ in range(x_msgs)]
        ymsg_lo, ymsg_hi, zmsg_lo, zmsg_hi = [refs.pop(0) for _ in range(4)]
    xh, gx, gy, gz, alx, aly, alz, edgex, edgey, edgez, changez = refs

    def ghosts(c, _):
        for k in range(HALO):
            here = pl.ds(k * ROWS, ROWS)
            lo = jnp.where(tube == 0, u_ref[c, pl.ds(0, ROWS), :], xlo_ref[c, here, :])
            hi = jnp.where(tube == tubes - 1, fresh_ref[c], xhi_ref[c, here, :])
            xh[c, here, :] = lo
            xh[c, pl.ds((HALO + k) * ROWS, ROWS), :] = hi
        return 0

    lax.fori_loop(0, NCOMP, ghosts, 0)

    def ghost_thermo(u, d, ref, row):
        back, pressure, sound = thermo(u)
        speed = u[9 + d] * (SCALE * back)
        for n, value in enumerate((speed, pressure, jnp.abs(speed) + SCALE * sound)):
            ref[n, pl.ds(row, ROWS), :] = value

    for k in range(2 * HALO):
        ghost_thermo([xh[c, pl.ds(k * ROWS, ROWS), :] for c in range(NCOMP)], 0, gx, k * ROWS)
    for ref, offset in ((ylo_ref, 0), (yhi_ref, HALO)):
        for k in range(HALO):
            for g in range(groups):
                row = k * planes + g * ROWS
                u = [ref[c, pl.ds(row, ROWS), :] for c in range(NCOMP)]
                ghost_thermo(u, 1, gy, offset * planes + row)
    ghost_thermo([zlo_ref[c] for c in range(NCOMP)], 2, gz, 0)
    ghost_thermo([zhi_ref[c] for c in range(NCOMP)], 2, gz, ROWS)

    def xvec(ref, n):
        def load(i):
            if HALO <= i < planes + HALO:
                return ref[pl.ds((i - HALO) * ROWS, ROWS), :]
            return gx[n, pl.ds((i if i < HALO else i - planes) * ROWS, ROWS), :]
        return load

    def yvec(ref, n, g):
        def load(i):
            if HALO <= i < width_y + HALO:
                return ref[pl.ds((i - HALO) * planes + g * ROWS, ROWS), :]
            return gy[n, pl.ds((i if i < HALO else i - width_y) * planes + g * ROWS, ROWS), :]
        return load

    row = lax.broadcasted_iota(jnp.int32, (ROWS, planes * width_y), 0)

    def joined(i, load, lo, hi):
        value = load(pl.ds(ROWS - HALO + i, ROWS, stride=zvecs))
        if i < HALO:
            return jnp.where(row == 0, lo(pl.ds(ROWS - HALO + i, 1)), value)
        if i >= zvecs + HALO:
            return jnp.where(row == ROWS - 1, hi(pl.ds(i - zvecs - HALO, 1)), value)
        return value

    def zvec(ref, n):
        def load(i):
            return joined(i, lambda s: ref[s, :], lambda s: gz[n, s, :],
                          lambda s: gz[n, pl.ds(ROWS + s.start, 1), :])
        return load

    def ends(n):
        return list(range(HALO)) + list(range(n - HALO + 1, n + 1))

    largest(xvec(ax, 2), ends(planes), alx, lambda j: j * ROWS)
    for g in range(groups):
        largest(yvec(ay, 2, g), ends(width_y), aly, lambda j: j * planes + g * ROWS)
    largest(zvec(az, 2), ends(zvecs), alz, lambda j: j * ROWS)

    def outer(n, cells, speed, pressure, kind, alpha, given, put):
        cells = memo(cells)
        fluxes = memo(lambda i: flux_of(cells(i), speed(i), lambda: pressure(i), kind))
        out = sweep(cells, fluxes, alpha, 0, HALO - 1)
        out[HALO] = given(HALO - 1)
        for i in range(HALO):
            put(i, out[i + 1] - out[i])
        out = sweep(cells, fluxes, alpha, n - HALO + 1, n)
        out[n - HALO] = given(n - HALO)
        for i in range(n - HALO, n):
            put(i, out[i + 1] - out[i])

    def between(n, rows, width):
        position = lax.broadcasted_iota(jnp.int32, (rows, width), 0) % n
        return (position >= HALO) & (position < n - HALO)

    inside_y = between(width_y, ROWS, width_z)
    inside_z = between(zvecs, width_z, planes * width_y)

    def z_body(c, kind, before):
        def cell(i):
            return joined(i, lambda s: uz_ref[c, s, :], lambda s: zlo_ref[c, s, :],
                          lambda s: zhi_ref[c, s, :])
        def put(i, value):
            edgez[c, pl.ds(i, ROWS, stride=zvecs), :] = value
        outer(zvecs, cell, zvec(uz, 0), zvec(pz, 1), kind,
              lambda j: alz[pl.ds(j * ROWS, ROWS), :],
              lambda i: accz[c, pl.ds(i, ROWS, stride=zvecs), :], put)

    for_components(3, z_body)

    def x_body(c, kind, before):
        changez[c] = jnp.where(inside_z, accz[c], edgez[c]).T

        def cell(i):
            if HALO <= i < planes + HALO:
                return u_ref[c, pl.ds((i - HALO) * ROWS, ROWS), :]
            return xh[c, pl.ds((i if i < HALO else i - planes) * ROWS, ROWS), :]
        def put(i, value):
            edgex[c, pl.ds((i if i < HALO else i - planes + 2 * HALO) * ROWS, ROWS), :] = value
        outer(planes, cell, xvec(ux, 0), xvec(px, 1), kind,
              lambda j: alx[pl.ds(j * ROWS, ROWS), :],
              lambda i: accx[c, pl.ds(i * ROWS, ROWS), :], put)

    for_components(1, x_body)

    def update(c):
        for p in range(planes):
            here = pl.ds(p * ROWS, ROWS)
            change = changez[c, here, :] + jnp.where(inside_y, accy[c, here, :], edgey[c, here, :])
            if HALO <= p < planes - HALO:
                change = change + accx[c, here, :]
            else:
                k = p if p < HALO else p - planes + 2 * HALO
                change = change + edgex[c, pl.ds(k * ROWS, ROWS), :]
            value = u_ref[c, here, :] + FLUX_FACTOR * change
            if stage == 2:
                value = 0.75 * start_ref[c, here, :] + 0.25 * value
            elif stage == 3:
                value = (1.0 / 3.0) * start_ref[c, here, :] + (2.0 / 3.0) * value
            new_ref[c, here, :] = value

    def pass_on(c):
        if not last:
            newz_ref[c, pl.ds(ROWS, width_z), :] = new_ref[c].T
            messages(c, planes, width_y, width_z, place, new_ref, newz_ref, xmsg_refs,
                     ymsg_lo, ymsg_hi, zmsg_lo, zmsg_hi)

    def y_body(c, kind, before):
        pass_on(before(2))
        update(before(1))
        for g in range(groups):
            base = g * ROWS * width_y
            def cell(i, g=g, base=base):
                if HALO <= i < width_y + HALO:
                    return u_ref[c, pl.ds(base + i - HALO, ROWS, stride=width_y), :]
                if i < HALO:
                    return ylo_ref[c, pl.ds(i * planes + g * ROWS, ROWS), :]
                return yhi_ref[c, pl.ds((i - HALO - width_y) * planes + g * ROWS, ROWS), :]
            def put(i, value, base=base):
                edgey[c, pl.ds(base + i, ROWS, stride=width_y), :] = value
            outer(width_y, cell, yvec(uy, 0, g), yvec(py, 1, g), kind,
                  lambda j: aly[pl.ds(j * planes + g * ROWS, ROWS), :],
                  lambda i: accy[c, pl.ds(base + i, ROWS, stride=width_y), :], put)

    order = for_components(2, y_body)
    pass_on(order[-2])
    update(order[-1])
    pass_on(order[-1])


def messages(c, planes, width_y, width_z, place, u_ref, uz_ref, xmsg_refs, ylo, yhi, zlo, zhi):
    for n, ref in enumerate(xmsg_refs):
        begin = place[2 + n]
        for k in range(HALO):
            rows = pl.ds(pl.multiple_of((begin + k) * ROWS, ROWS), ROWS)
            ref[c, pl.ds(k * ROWS, ROWS), :] = u_ref[c, rows, :]
    for k in range(HALO):
        for g in range(planes // ROWS):
            there = pl.ds(k * planes + g * ROWS, ROWS)
            base = g * ROWS * width_y + k
            yhi[c, there, :] = u_ref[c, pl.ds(base, ROWS, stride=width_y), :]
            ylo[c, there, :] = u_ref[c, pl.ds(base + width_y - HALO, ROWS, stride=width_y), :]
    zhi[c] = uz_ref[c, pl.ds(ROWS, ROWS), :]
    zlo[c] = uz_ref[c, pl.ds(width_z, ROWS), :]


def assemble_kernel(
    planes, width_y, width_z, x_msgs, place, state_ref, ahead_ref, fresh_ref, u_ref, uz_ref, *refs,
):
    refs = list(refs)
    xmsg_refs = [refs.pop(0) for _ in range(x_msgs)]
    ymsg_lo, ymsg_hi, zmsg_lo, zmsg_hi = refs
    tube, tubes, shift = place[0], place[1], place[4]
    reach = ahead_ref.shape[1] // ROWS

    def pass_on(c):
        uz_ref[c, pl.ds(ROWS, width_z), :] = u_ref[c].T
        messages(c, planes, width_y, width_z, place, u_ref, uz_ref, xmsg_refs,
                 ymsg_lo, ymsg_hi, zmsg_lo, zmsg_hi)

    def body(c, _):
        pass_on(jnp.maximum(c - 1, 0))
        fresh = fresh_ref[c]
        for i in range(planes):
            source = shift + i
            own = jnp.minimum(source, planes - 1)
            value = state_ref[c, pl.ds(pl.multiple_of(own * ROWS, ROWS), ROWS), :]
            if i >= planes - reach:
                beyond = jnp.clip(source - planes, 0, reach - 1)
                other = ahead_ref[c, pl.ds(pl.multiple_of(beyond * ROWS, ROWS), ROWS), :]
                other = jnp.where(tube == tubes - 1, fresh, other)
                value = jnp.where(source >= planes, other, value)
            u_ref[c, pl.ds(i * ROWS, ROWS), :] = value
        return 0

    lax.fori_loop(0, NCOMP, body, 0)
    pass_on(NCOMP - 1)


def powers_of(back):
    a = jnp.exp(-0.5 * back)
    b = jnp.exp(-0.3 * back)
    a2 = a * a
    a3 = a2 * a
    a4 = a2 * a2
    a6 = a3 * a3
    a8 = a4 * a4
    return {0.5: a, 0.3: b, 1.0: a2, 1.5: a3, 3.0: a6, 4.0: a8, 4.5: a8 * a, 5.0: a8 * a2,
            6.0: a6 * a6, 0.8: a * b}


def react(conc, internal, size):
    s2 = conc[2] + conc[6] + conc[7]
    s3 = conc[3] + conc[4]
    heat = 2.5 * (((conc[0] + conc[1]) + (conc[5] + conc[8])) + (s2 + s3)) + (0.5 * s2 - s3)
    bond = None
    for k in range(9):
        if FORMATION[k]:
            term = float(FORMATION[k] * MOLAR[k]) * conc[k]
            bond = term if bond is None else bond + term
    boltzmann = powers_of(heat / (internal - bond))
    pairs = {}
    omega = [None] * 9

    def add(k, value):
        omega[k] = value if omega[k] is None else omega[k] + value

    def sub(k, value):
        omega[k] = -value if omega[k] is None else omega[k] - value

    def rate(j):
        names = REACTANTS[j]
        key = tuple(sorted(names))
        if key not in pairs:
            value = conc[names[0]] * conc[names[1]]
            if len(names) == 3:
                base = tuple(sorted(names[:2]))
                if base not in pairs:
                    pairs[base] = value
                value = pairs[base] * conc[8]
            pairs[key] = value
        return (PREFACTOR[j] * boltzmann[BARRIER[j]]) * pairs[key]

    j = 0
    while j < len(REACTANTS):
        value = rate(j)
        back = j + 1 < len(REACTANTS) and REACTANTS[j + 1] == PRODUCTS[j] \
            and PRODUCTS[j + 1] == REACTANTS[j]
        if back:
            value = value - rate(j + 1)
        for k in range(9):
            times = PRODUCTS[j].count(k) - REACTANTS[j].count(k)
            if times == 0:
                continue
            amount = value if abs(times) == 1 else value + value
            if times > 0:
                add(k, amount)
            else:
                sub(k, amount)
        j += 2 if back else 1
    return [conc[k] + size * omega[k] for k in range(9)]


def chemistry_kernel(planes, span, third_ref, counts_ref, out_ref):
    for c in range(9, NCOMP):
        out_ref[c] = third_ref[c]

    def block(i, _):
        rows = [
            pl.ds(pl.multiple_of((i * span + k) * ROWS, ROWS), ROWS) for k in range(span)
        ]
        counts = [counts_ref[r, :] for r in rows]
        sizes = [TIME_STEP / n.astype(jnp.float32) for n in counts]
        most = counts[0]
        for n in counts[1:]:
            most = jnp.maximum(most, n)
        turns = jnp.max(most)
        conc, internal = [], []
        for r in rows:
            u = [third_ref[c, r, :] for c in range(NCOMP)]
            rho = ((u[0] + u[1]) + (u[2] + u[3])) + ((u[4] + u[5]) + (u[6] + u[7])) + u[8]
            internal.append(
                u[12] - 0.5 * (u[9] * u[9] + u[10] * u[10] + u[11] * u[11]) / rho)
            conc.append([u[k] * float(GAS[k]) for k in range(9)])

        def advance(index, carry):
            new = []
            for k in range(span):
                moved = react(carry[k], internal[k], sizes[k])
                keep = index < counts[k]
                new.append([jnp.where(keep, m, o) for m, o in zip(moved, carry[k])])
            return new

        conc = lax.fori_loop(0, turns, advance, conc)
        for k in range(span):
            for c in range(9):
                out_ref[c, rows[k], :] = conc[k][c] * float(MOLAR[c])
        return 0

    lax.fori_loop(0, planes // span, block, 0)


def shape(*dims):
    return jax.ShapeDtypeStruct(dims, jnp.float32)


def call(kernel, out_shape, scratch, n_in, scalars=True):
    vmem = pl.BlockSpec(memory_space=pltpu.VMEM)
    specs = [vmem] * n_in
    if scalars:
        specs[0] = pl.BlockSpec(memory_space=pltpu.SMEM)
    return pl.pallas_call(
        kernel,
        out_shape=out_shape,
        in_specs=specs,
        out_specs=jax.tree.map(lambda _: vmem, out_shape),
        scratch_shapes=[pltpu.VMEM(dims, jnp.float32) for dims in scratch],
        compiler_params=pltpu.CompilerParams(vmem_limit_bytes=16 * 1024 * 1024),
    )


def moved(value, axis, steps, closed):
    count = lax.axis_size(axis)
    pairs = [(i, (i + steps) % count) for i in range(count) if closed or 0 <= i + steps < count]
    return lax.ppermute(value, axis, pairs)


def on_device(state, fresh, substeps, shift):
    comps, planes, width_y, width_z = state.shape
    cross = planes * width_y
    zvecs = width_z // ROWS
    tubes = lax.axis_size("tube")
    tube = lax.axis_index("tube")
    swap = tubes == 2
    x_msgs = 1 if swap else 2
    begins = [jnp.where(tube == 0, planes - HALO, 0), 0] if swap else [0, planes - HALO]
    place = jnp.stack([
        tube.astype(jnp.int32), jnp.int32(tubes), jnp.asarray(begins[0], jnp.int32),
        jnp.asarray(begins[1], jnp.int32), shift.astype(jnp.int32)])

    full = shape(comps, cross, width_z)
    fullz = shape(comps, width_z + 2 * ROWS, cross)
    xs = shape(comps, HALO * ROWS, width_z)
    ys = shape(comps, HALO * planes, width_z)
    zs = shape(comps, ROWS, cross)
    sent = (full, fullz) + (xs,) * x_msgs + (ys, ys, zs, zs)
    flat = state.reshape(comps, cross, width_z)

    def shifted(reach):
        def branch():
            ahead = moved(flat[:, :reach * width_y], "tube", -1, False)
            return call(
                functools.partial(assemble_kernel, planes, width_y, width_z, x_msgs),
                sent, [], 4,
            )(place, flat, ahead, fresh)
        return branch

    pieces = 4
    size = SMAX // pieces
    start, uz, *msgs = lax.switch(
        (shift.astype(jnp.int32) - 1) // size, [shifted((n + 1) * size) for n in range(pieces)])

    in_x, in_y, in_z = shape(cross, width_z), shape(cross, width_z), shape(
        width_z + 2 * ROWS, cross)
    inner_out = (in_x,) * 3 + (in_y,) * 3 + (in_z,) * 3 + (full, full, shape(comps, width_z, cross))
    al = [((planes + 1) * ROWS, width_z), ((width_y + 1) * planes, width_z),
          ((zvecs + 1) * ROWS, cross)]
    inner_scratch = al + [(3, cross, width_z)]
    outer_scratch = [
        (comps, 2 * HALO * ROWS, width_z), (3, 2 * HALO * ROWS, width_z),
        (3, 2 * HALO * planes, width_z), (3, 2 * ROWS, cross),
        *al, (comps, 2 * HALO * ROWS, width_z), (comps, cross, width_z), (comps, width_z, cross),
        (comps, cross, width_z)]
    current = start
    for stage in (1, 2, 3):
        xmsg, (ylo, yhi, zlo, zhi) = msgs[:x_msgs], msgs[x_msgs:]
        ylo = moved(ylo, "gy", 1, True)
        yhi = moved(yhi, "gy", -1, True)
        if swap:
            xlo = xhi = lax.ppermute(xmsg[0], "tube", [(0, 1), (1, 0)])
        else:
            xhi = moved(xmsg[0], "tube", -1, False)
            xlo = moved(xmsg[1], "tube", 1, False)
        zlo = moved(zlo, "gz", 1, True)
        zhi = moved(zhi, "gz", -1, True)
        inner = call(
            functools.partial(inner_kernel, planes, width_y, width_z),
            inner_out, inner_scratch, 2, False)(current, uz)
        current, *rest = call(
            functools.partial(outer_kernel, stage, planes, width_y, width_z, x_msgs),
            (full,) if stage == 3 else sent, outer_scratch, 11 + len(inner_out),
        )(place, current, uz, start, fresh, xlo, xhi, ylo, yhi, zlo, zhi, *inner)
        if stage < 3:
            uz, *msgs = rest

    vmem = pl.BlockSpec(memory_space=pltpu.VMEM)
    reacted = pl.pallas_call(
        functools.partial(chemistry_kernel, planes, 4),
        out_shape=full,
        in_specs=[vmem, vmem],
        out_specs=vmem,
        compiler_params=pltpu.CompilerParams(vmem_limit_bytes=16 * 1024 * 1024),
    )(current, substeps.reshape(cross, width_z))
    return reacted.reshape(state.shape)


def solution(mesh):
    return jax.shard_map(
        on_device,
        mesh=mesh,
        in_specs=(P(None, "tube", "gy", "gz"), P(None, "gy", "gz"), P("tube", "gy", "gz"), P()),
        out_specs=P(None, "tube", "gy", "gz"),
        check_vma=False,
    )
```

```python
import functools

import jax
import jax.numpy as jnp
import numpy as np
from jax import lax
from jax.experimental import pallas as pl
from jax.experimental.pallas import tpu as pltpu
from jax.sharding import PartitionSpec as P

SMAX = 12
HALO = 3
NCOMP = 13
ROWS = 8
SCALE = 0.25
TIME_STEP = 0.05
FLUX_FACTOR = -TIME_STEP / (6.0 * SCALE)

MOLAR = np.array([2.016, 31.998, 18.015, 1.008, 15.999, 17.007, 33.006, 34.014, 28.014]) / 18.015
GAS = 1.0 / MOLAR
FORMATION = np.array([0.0, 0.0, -1.5, 12.0, 1.5, 0.25, 0.02, -0.45, 0.0])
REACTANTS = [
    (3, 1), (4, 5), (4, 0), (3, 5), (0, 5), (2, 3), (4, 2), (5, 5), (0, 8), (3, 3, 8), (4, 4, 8),
    (3, 4, 8), (3, 5, 8), (3, 1, 8), (6, 3), (6, 3), (6, 4), (6, 5), (6, 6), (7, 8), (7, 3),
]
PRODUCTS = [
    (4, 5), (3, 1), (3, 5), (4, 0), (2, 3), (0, 5), (5, 5), (4, 2), (3, 3), (0,), (1,),
    (5,), (2,), (6,), (0, 1), (5, 5), (1, 5), (2, 1), (7, 1), (5, 5), (2, 5),
]
PREFACTOR = [
    30.0, 8.0, 20.0, 6.0, 25.0, 10.0, 12.0, 5.0, 4.0, 20.0, 15.0,
    18.0, 22.0, 25.0, 30.0, 25.0, 20.0, 30.0, 10.0, 6.0, 15.0,
]
BARRIER = [
    4.0, 1.0, 3.0, 1.5, 1.5, 4.5, 4.0, 1.5, 6.0, 0.5, 0.5,
    0.5, 0.5, 0.3, 0.8, 0.5, 0.3, 0.3, 0.5, 5.0, 1.5,
]

KAPPA = 0.609375
EPS = 3.0 * SCALE * SCALE * 1e-6


def rcp(x):
    return pl.reciprocal(x, approx=True)


def correction(d1, d2, d3, d4):
    k2 = KAPPA * (d2 * d2) + EPS
    k3 = KAPPA * (d3 * d3) + EPS
    xa = d1 - 1.375 * d2
    xb = d3 - 0.625 * d2
    xc = d4 - 1.375 * d3
    ra = rcp(xa * xa + k2)
    rb = rcp(xb * xb + k2)
    rc = rcp(xc * xc + k3)
    wa = ra * ra
    wb = 6.0 * (rb * rb)
    wc = 3.0 * (rc * rc)
    return ((xa + xb) * wa + (0.5 * (d2 + d4) - d3) * wc) * rcp(wa + wb + wc)


def face_flux(du, df, f2, f3, alpha):
    e = [alpha * d for d in du]
    p = [df[k] + e[k] for k in range(4)]
    m = [None] + [df[k] - e[k] for k in range(1, 5)]
    linear = 3.0 * (f2 + f3) - e[2] + 0.5 * (p[1] - m[3])
    return linear - correction(p[0], p[1], p[2], p[3]) + correction(m[4], m[3], m[2], m[1])


def sweep(cells, fluxes, alpha, first, last):
    du, df = {}, {}
    out = {}
    for j in range(first, last + 1):
        for k in range(j, j + 5):
            if k not in du:
                du[k] = cells(k + 1) - cells(k)
                df[k] = fluxes(k + 1) - fluxes(k)
        out[j] = face_flux(
            [du[k] for k in range(j, j + 5)],
            [df[k] for k in range(j, j + 5)],
            fluxes(j + 2),
            fluxes(j + 3),
            alpha(j),
        )
    return out


def memo(load):
    return functools.lru_cache(maxsize=None)(load)


def thermo(u):
    g = [u[k] if GAS[k] == 1.0 else u[k] * float(GAS[k]) for k in range(9)]
    s2 = g[2] + g[6] + g[7]
    s3 = g[3] + g[4]
    gas = (g[0] + g[1]) + (g[5] + g[8]) + (s2 + s3)
    heat = 2.5 * gas + (0.5 * s2 - s3)
    bond = 1.5 * (u[4] - u[2]) + 12.0 * u[3] + 0.25 * u[5] + 0.02 * u[6] - 0.45 * u[7]
    rho = ((u[0] + u[1]) + (u[2] + u[3])) + ((u[4] + u[5]) + (u[6] + u[7])) + u[8]
    back = 1.0 / rho
    cold = 1.0 / heat
    motion = 0.5 * (u[9] * u[9] + u[10] * u[10] + u[11] * u[11]) * back
    temperature = (u[12] - motion - bond) * cold
    pressure = gas * temperature
    sound = jnp.sqrt((1.0 + gas * cold) * pressure * back)
    return back, pressure, sound


def for_components(body):
    def step(c, _):
        body(c, (0, 0, 0), lambda n: jnp.maximum(c - n, 0))
        return 0

    lax.fori_loop(0, 9, step, 0)
    kinds = [(1, 0, 0), (0, 1, 0), (0, 0, 1), (2, 2, 2)]
    for c in range(9, NCOMP):
        body(c, kinds[c - 9], lambda n, c=c: c - n)


def flux_of(u, speed, pressure, kind):
    if kind == 0:
        return u * speed
    if kind == 1:
        return u * speed + SCALE * pressure()
    return (u + pressure()) * speed


def own_thermo(planes, width_y, u_ref, x_refs, y_refs, z_refs, tmp):
    span = planes // 2

    def own(i, _):
        for k in range(span):
            p = i * span + k
            here = pl.ds(pl.multiple_of(p * ROWS, ROWS), ROWS)
            u = [u_ref[c, here, :] for c in range(NCOMP)]
            back, pressure, sound = thermo(u)
            back, sound = SCALE * back, SCALE * sound
            across = pl.ds(p, width_y, stride=planes)
            for d, where in ((0, here), (1, across), (2, here)):
                speed = u[9 + d] * back
                for n, value in enumerate((speed, pressure, jnp.abs(speed) + sound)):
                    if d == 2:
                        tmp[n, where, :] = value
                    else:
                        (x_refs, y_refs)[d][n][where, :] = value
        return 0

    lax.fori_loop(0, planes // span, own, 0)
    for n in range(3):
        z_refs[n][pl.ds(ROWS, tmp.shape[2]), :] = tmp[n].T


def inner_kernel(
    planes, width_y, width_z, u_ref, uz_ref,
    ux, px, ax, uy, py, ay, uz, pz, az, accx, accy, accz, alx, aly, alz, tmp,
):
    groups = planes // ROWS
    zvecs = width_z // ROWS
    own_thermo(planes, width_y, u_ref, (ux, px, ax), (uy, py, ay), (uz, pz, az), tmp)

    def xvec(ref):
        return lambda i: ref[pl.ds((i - HALO) * ROWS, ROWS), :]

    def yvec(ref, g):
        return lambda i: ref[pl.ds((i - HALO) * planes + g * ROWS, ROWS), :]

    def zvec(ref):
        return lambda i: ref[pl.ds(ROWS - HALO + i, ROWS, stride=zvecs), :]

    largest(xvec(ax), range(HALO, planes - HALO + 1), alx, lambda j: j * ROWS)
    for g in range(groups):
        largest(yvec(ay, g), range(HALO, width_y - HALO + 1), aly,
                lambda j: j * planes + g * ROWS)
    largest(zvec(az), range(HALO, zvecs - HALO + 1), alz, lambda j: j * ROWS)

    def inner(n, cells, speed, pressure, kind, alpha, put):
        cells = memo(cells)
        fluxes = memo(lambda i: flux_of(cells(i), speed(i), lambda: pressure(i), kind))
        out = sweep(cells, fluxes, alpha, HALO, n - HALO)
        put(HALO - 1, out[HALO])
        for i in range(HALO, n - HALO):
            put(i, out[i + 1] - out[i])
        put(n - HALO, out[n - HALO])

    def x_body(c, kind):
        def put(i, value):
            accx[c, pl.ds(i * ROWS, ROWS), :] = value
        inner(planes, lambda i: u_ref[c, pl.ds((i - HALO) * ROWS, ROWS), :], xvec(ux), xvec(px),
              kind, lambda j: alx[pl.ds(j * ROWS, ROWS), :], put)

    def z_body(c, kind):
        def put(i, value):
            accz[c, pl.ds(i, ROWS, stride=zvecs), :] = value
        inner(zvecs, lambda i: uz_ref[c, pl.ds(ROWS - HALO + i, ROWS, stride=zvecs), :],
              zvec(uz), zvec(pz), kind, lambda j: alz[pl.ds(j * ROWS, ROWS), :], put)

    def y_body(c, kind):
        for g in range(groups):
            def put(i, value, g=g):
                accy[c, pl.ds(g * ROWS * width_y + i, ROWS, stride=width_y), :] = value
            def cell(i, g=g):
                return u_ref[c, pl.ds(g * ROWS * width_y + i - HALO, ROWS, stride=width_y), :]
            inner(width_y, cell, yvec(uy, g), yvec(py, g), kind,
                  lambda j: aly[pl.ds(j * planes + g * ROWS, ROWS), :], put)

    def body(c, kinds, before):
        x_body(c, kinds[0])
        z_body(c, kinds[2])
        y_body(c, kinds[1])

    for_components(body)


def largest(speed, faces, ref, place):
    values = memo(speed)
    for j in faces:
        top = values(j)
        for k in range(1, 6):
            top = jnp.maximum(top, values(j + k))
        ref[pl.ds(place(j), ROWS), :] = top


def outer_kernel(
    stage, planes, width_y, width_z, x_msgs, place,
    u_ref, uz_ref, start_ref, fresh_ref, xlo_ref, xhi_ref, ylo_ref, yhi_ref, zlo_ref, zhi_ref,
    ux, px, ax, uy, py, ay, uz, pz, az, accx, accy, accz, *refs,
):
    groups = planes // ROWS
    zvecs = width_z // ROWS
    tube, tubes = place[0], place[1]
    last = stage == 3
    refs = list(refs)
    new_ref = refs.pop(0)
    if not last:
        newz_ref = refs.pop(0)
        xmsg_refs = [refs.pop(0) for _ in range(x_msgs)]
        ymsg_lo, ymsg_hi, zmsg_lo, zmsg_hi = [refs.pop(0) for _ in range(4)]
    xh, gx, gy, gz, alx, aly, alz, edgex, edgey, edgez, changez = refs

    def ghosts(c, _):
        for k in range(HALO):
            here = pl.ds(k * ROWS, ROWS)
            lo = jnp.where(tube == 0, u_ref[c, pl.ds(0, ROWS), :], xlo_ref[c, here, :])
            hi = jnp.where(tube == tubes - 1, fresh_ref[c], xhi_ref[c, here, :])
            xh[c, here, :] = lo
            xh[c, pl.ds((HALO + k) * ROWS, ROWS), :] = hi
        return 0

    lax.fori_loop(0, NCOMP, ghosts, 0)

    def ghost_thermo(u, d, ref, row):
        back, pressure, sound = thermo(u)
        speed = u[9 + d] * (SCALE * back)
        for n, value in enumerate((speed, pressure, jnp.abs(speed) + SCALE * sound)):
            ref[n, pl.ds(row, ROWS), :] = value

    for k in range(2 * HALO):
        ghost_thermo([xh[c, pl.ds(k * ROWS, ROWS), :] for c in range(NCOMP)], 0, gx, k * ROWS)
    for ref, offset in ((ylo_ref, 0), (yhi_ref, HALO)):
        for k in range(HALO):
            for g in range(groups):
                row = k * planes + g * ROWS
                u = [ref[c, pl.ds(row, ROWS), :] for c in range(NCOMP)]
                ghost_thermo(u, 1, gy, offset * planes + row)
    ghost_thermo([zlo_ref[c] for c in range(NCOMP)], 2, gz, 0)
    ghost_thermo([zhi_ref[c] for c in range(NCOMP)], 2, gz, ROWS)

    def xvec(ref, n):
        def load(i):
            if HALO <= i < planes + HALO:
                return ref[pl.ds((i - HALO) * ROWS, ROWS), :]
            return gx[n, pl.ds((i if i < HALO else i - planes) * ROWS, ROWS), :]
        return load

    def yvec(ref, n, g):
        def load(i):
            if HALO <= i < width_y + HALO:
                return ref[pl.ds((i - HALO) * planes + g * ROWS, ROWS), :]
            return gy[n, pl.ds((i if i < HALO else i - width_y) * planes + g * ROWS, ROWS), :]
        return load

    row = lax.broadcasted_iota(jnp.int32, (ROWS, planes * width_y), 0)

    def joined(i, load, lo, hi):
        value = load(pl.ds(ROWS - HALO + i, ROWS, stride=zvecs))
        if i < HALO:
            return jnp.where(row == 0, lo(pl.ds(ROWS - HALO + i, 1)), value)
        if i >= zvecs + HALO:
            return jnp.where(row == ROWS - 1, hi(pl.ds(i - zvecs - HALO, 1)), value)
        return value

    def zvec(ref, n):
        def load(i):
            return joined(i, lambda s: ref[s, :], lambda s: gz[n, s, :],
                          lambda s: gz[n, pl.ds(ROWS + s.start, 1), :])
        return load

    def ends(n):
        return list(range(HALO)) + list(range(n - HALO + 1, n + 1))

    largest(xvec(ax, 2), ends(planes), alx, lambda j: j * ROWS)
    for g in range(groups):
        largest(yvec(ay, 2, g), ends(width_y), aly, lambda j: j * planes + g * ROWS)
    largest(zvec(az, 2), ends(zvecs), alz, lambda j: j * ROWS)

    def outer(n, cells, speed, pressure, kind, alpha, given, put):
        cells = memo(cells)
        fluxes = memo(lambda i: flux_of(cells(i), speed(i), lambda: pressure(i), kind))
        out = sweep(cells, fluxes, alpha, 0, HALO - 1)
        out[HALO] = given(HALO - 1)
        for i in range(HALO):
            put(i, out[i + 1] - out[i])
        out = sweep(cells, fluxes, alpha, n - HALO + 1, n)
        out[n - HALO] = given(n - HALO)
        for i in range(n - HALO, n):
            put(i, out[i + 1] - out[i])

    def between(n, rows, width):
        position = lax.broadcasted_iota(jnp.int32, (rows, width), 0) % n
        return (position >= HALO) & (position < n - HALO)

    inside_y = between(width_y, ROWS, width_z)
    inside_z = between(zvecs, width_z, planes * width_y)

    def z_body(c, kind):
        def cell(i):
            return joined(i, lambda s: uz_ref[c, s, :], lambda s: zlo_ref[c, s, :],
                          lambda s: zhi_ref[c, s, :])
        def put(i, value):
            edgez[c, pl.ds(i, ROWS, stride=zvecs), :] = value
        outer(zvecs, cell, zvec(uz, 0), zvec(pz, 1), kind,
              lambda j: alz[pl.ds(j * ROWS, ROWS), :],
              lambda i: accz[c, pl.ds(i, ROWS, stride=zvecs), :], put)

    def x_body(c, kind):
        def cell(i):
            if HALO <= i < planes + HALO:
                return u_ref[c, pl.ds((i - HALO) * ROWS, ROWS), :]
            return xh[c, pl.ds((i if i < HALO else i - planes) * ROWS, ROWS), :]
        def put(i, value):
            edgex[c, pl.ds((i if i < HALO else i - planes + 2 * HALO) * ROWS, ROWS), :] = value
        outer(planes, cell, xvec(ux, 0), xvec(px, 1), kind,
              lambda j: alx[pl.ds(j * ROWS, ROWS), :],
              lambda i: accx[c, pl.ds(i * ROWS, ROWS), :], put)

    def update(c):
        changez[...] = jnp.where(inside_z, accz[c], edgez[c]).T
        for p in range(planes):
            here = pl.ds(p * ROWS, ROWS)
            change = changez[here, :] + jnp.where(inside_y, accy[c, here, :], edgey[c, here, :])
            if HALO <= p < planes - HALO:
                change = change + accx[c, here, :]
            else:
                k = p if p < HALO else p - planes + 2 * HALO
                change = change + edgex[c, pl.ds(k * ROWS, ROWS), :]
            value = u_ref[c, here, :] + FLUX_FACTOR * change
            if stage == 2:
                value = 0.75 * start_ref[c, here, :] + 0.25 * value
            elif stage == 3:
                value = (1.0 / 3.0) * start_ref[c, here, :] + (2.0 / 3.0) * value
            new_ref[c, here, :] = value

    def pass_on(c):
        if not last:
            newz_ref[c, pl.ds(ROWS, width_z), :] = new_ref[c].T
            messages(c, planes, width_y, width_z, place, new_ref, newz_ref, xmsg_refs,
                     ymsg_lo, ymsg_hi, zmsg_lo, zmsg_hi)

    def y_body(c, kind):
        for g in range(groups):
            base = g * ROWS * width_y
            def cell(i, g=g, base=base):
                if HALO <= i < width_y + HALO:
                    return u_ref[c, pl.ds(base + i - HALO, ROWS, stride=width_y), :]
                if i < HALO:
                    return ylo_ref[c, pl.ds(i * planes + g * ROWS, ROWS), :]
                return yhi_ref[c, pl.ds((i - HALO - width_y) * planes + g * ROWS, ROWS), :]
            def put(i, value, base=base):
                edgey[c, pl.ds(base + i, ROWS, stride=width_y), :] = value
            outer(width_y, cell, yvec(uy, 0, g), yvec(py, 1, g), kind,
                  lambda j: aly[pl.ds(j * planes + g * ROWS, ROWS), :],
                  lambda i: accy[c, pl.ds(base + i, ROWS, stride=width_y), :], put)

    def body(c, kinds, before):
        pass_on(before(2))
        update(before(1))
        z_body(c, kinds[2])
        x_body(c, kinds[0])
        y_body(c, kinds[1])

    for_components(body)
    pass_on(NCOMP - 2)
    update(NCOMP - 1)
    pass_on(NCOMP - 1)


def messages(c, planes, width_y, width_z, place, u_ref, uz_ref, xmsg_refs, ylo, yhi, zlo, zhi):
    for n, ref in enumerate(xmsg_refs):
        begin = place[2 + n]
        for k in range(HALO):
            rows = pl.ds(pl.multiple_of((begin + k) * ROWS, ROWS), ROWS)
            ref[c, pl.ds(k * ROWS, ROWS), :] = u_ref[c, rows, :]
    for k in range(HALO):
        for g in range(planes // ROWS):
            there = pl.ds(k * planes + g * ROWS, ROWS)
            base = g * ROWS * width_y + k
            yhi[c, there, :] = u_ref[c, pl.ds(base, ROWS, stride=width_y), :]
            ylo[c, there, :] = u_ref[c, pl.ds(base + width_y - HALO, ROWS, stride=width_y), :]
    zhi[c] = uz_ref[c, pl.ds(ROWS, ROWS), :]
    zlo[c] = uz_ref[c, pl.ds(width_z, ROWS), :]


def assemble_kernel(
    planes, width_y, width_z, x_msgs, place, state_ref, ahead_ref, fresh_ref, u_ref, uz_ref, *refs,
):
    refs = list(refs)
    xmsg_refs = [refs.pop(0) for _ in range(x_msgs)]
    ymsg_lo, ymsg_hi, zmsg_lo, zmsg_hi = refs
    tube, tubes, shift = place[0], place[1], place[4]
    reach = ahead_ref.shape[1] // ROWS

    def pass_on(c):
        uz_ref[c, pl.ds(ROWS, width_z), :] = u_ref[c].T
        messages(c, planes, width_y, width_z, place, u_ref, uz_ref, xmsg_refs,
                 ymsg_lo, ymsg_hi, zmsg_lo, zmsg_hi)

    for c in range(NCOMP):
        if c:
            pass_on(c - 1)
        fresh = fresh_ref[c]
        for i in range(planes):
            source = shift + i
            own = jnp.minimum(source, planes - 1)
            value = state_ref[c, pl.ds(pl.multiple_of(own * ROWS, ROWS), ROWS), :]
            if i >= planes - reach:
                beyond = jnp.clip(source - planes, 0, reach - 1)
                other = ahead_ref[c, pl.ds(pl.multiple_of(beyond * ROWS, ROWS), ROWS), :]
                other = jnp.where(tube == tubes - 1, fresh, other)
                value = jnp.where(source >= planes, other, value)
            u_ref[c, pl.ds(i * ROWS, ROWS), :] = value
    pass_on(NCOMP - 1)


def powers_of(back):
    a = jnp.exp(-0.5 * back)
    b = jnp.exp(-0.3 * back)
    a2 = a * a
    a3 = a2 * a
    a4 = a2 * a2
    a6 = a3 * a3
    a8 = a4 * a4
    return {0.5: a, 0.3: b, 1.0: a2, 1.5: a3, 3.0: a6, 4.0: a8, 4.5: a8 * a, 5.0: a8 * a2,
            6.0: a6 * a6, 0.8: a * b}


def react(conc, internal, size):
    s2 = conc[2] + conc[6] + conc[7]
    s3 = conc[3] + conc[4]
    heat = 2.5 * (((conc[0] + conc[1]) + (conc[5] + conc[8])) + (s2 + s3)) + (0.5 * s2 - s3)
    bond = None
    for k in range(9):
        if FORMATION[k]:
            term = float(FORMATION[k] * MOLAR[k]) * conc[k]
            bond = term if bond is None else bond + term
    boltzmann = powers_of(heat / (internal - bond))
    pairs = {}
    omega = [None] * 9

    def add(k, value):
        omega[k] = value if omega[k] is None else omega[k] + value

    def sub(k, value):
        omega[k] = -value if omega[k] is None else omega[k] - value

    def rate(j):
        names = REACTANTS[j]
        key = tuple(sorted(names))
        if key not in pairs:
            value = conc[names[0]] * conc[names[1]]
            if len(names) == 3:
                base = tuple(sorted(names[:2]))
                if base not in pairs:
                    pairs[base] = value
                value = pairs[base] * conc[8]
            pairs[key] = value
        return (PREFACTOR[j] * boltzmann[BARRIER[j]]) * pairs[key]

    j = 0
    while j < len(REACTANTS):
        value = rate(j)
        back = j + 1 < len(REACTANTS) and REACTANTS[j + 1] == PRODUCTS[j] \
            and PRODUCTS[j + 1] == REACTANTS[j]
        if back:
            value = value - rate(j + 1)
        for k in range(9):
            times = PRODUCTS[j].count(k) - REACTANTS[j].count(k)
            if times == 0:
                continue
            amount = value if abs(times) == 1 else value + value
            if times > 0:
                add(k, amount)
            else:
                sub(k, amount)
        j += 2 if back else 1
    return [conc[k] + size * omega[k] for k in range(9)]


def chemistry_kernel(planes, span, third_ref, counts_ref, out_ref):
    for c in range(9, NCOMP):
        out_ref[c] = third_ref[c]

    def block(i, _):
        rows = [
            pl.ds(pl.multiple_of((i * span + k) * ROWS, ROWS), ROWS) for k in range(span)
        ]
        counts = [counts_ref[r, :] for r in rows]
        sizes = [TIME_STEP / n.astype(jnp.float32) for n in counts]
        most = counts[0]
        for n in counts[1:]:
            most = jnp.maximum(most, n)
        turns = jnp.max(most)
        conc, internal = [], []
        for r in rows:
            u = [third_ref[c, r, :] for c in range(NCOMP)]
            rho = ((u[0] + u[1]) + (u[2] + u[3])) + ((u[4] + u[5]) + (u[6] + u[7])) + u[8]
            internal.append(
                u[12] - 0.5 * (u[9] * u[9] + u[10] * u[10] + u[11] * u[11]) / rho)
            conc.append([u[k] * float(GAS[k]) for k in range(9)])

        def advance(index, carry):
            new = []
            for k in range(span):
                moved = react(carry[k], internal[k], sizes[k])
                keep = index < counts[k]
                new.append([jnp.where(keep, m, o) for m, o in zip(moved, carry[k])])
            return new

        conc = lax.fori_loop(0, turns, advance, conc)
        for k in range(span):
            for c in range(9):
                out_ref[c, rows[k], :] = conc[k][c] * float(MOLAR[c])
        return 0

    lax.fori_loop(0, planes // span, block, 0)


def shape(*dims):
    return jax.ShapeDtypeStruct(dims, jnp.float32)


def call(kernel, out_shape, scratch, n_in, scalars=True):
    vmem = pl.BlockSpec(memory_space=pltpu.VMEM)
    specs = [vmem] * n_in
    if scalars:
        specs[0] = pl.BlockSpec(memory_space=pltpu.SMEM)
    return pl.pallas_call(
        kernel,
        out_shape=out_shape,
        in_specs=specs,
        out_specs=jax.tree.map(lambda _: vmem, out_shape),
        scratch_shapes=[pltpu.VMEM(dims, jnp.float32) for dims in scratch],
        compiler_params=pltpu.CompilerParams(vmem_limit_bytes=16 * 1024 * 1024),
    )


def moved(value, axis, steps, closed):
    count = lax.axis_size(axis)
    pairs = [(i, (i + steps) % count) for i in range(count) if closed or 0 <= i + steps < count]
    return lax.ppermute(value, axis, pairs)


def on_device(state, fresh, substeps, shift):
    comps, planes, width_y, width_z = state.shape
    cross = planes * width_y
    zvecs = width_z // ROWS
    tubes = lax.axis_size("tube")
    tube = lax.axis_index("tube")
    swap = tubes == 2
    x_msgs = 1 if swap else 2
    begins = [jnp.where(tube == 0, planes - HALO, 0), 0] if swap else [0, planes - HALO]
    place = jnp.stack([
        tube.astype(jnp.int32), jnp.int32(tubes), jnp.asarray(begins[0], jnp.int32),
        jnp.asarray(begins[1], jnp.int32), shift.astype(jnp.int32)])

    full = shape(comps, cross, width_z)
    fullz = shape(comps, width_z + 2 * ROWS, cross)
    xs = shape(comps, HALO * ROWS, width_z)
    ys = shape(comps, HALO * planes, width_z)
    zs = shape(comps, ROWS, cross)
    sent = (full, fullz) + (xs,) * x_msgs + (ys, ys, zs, zs)
    flat = state.reshape(comps, cross, width_z)

    def shifted(reach):
        def branch():
            ahead = moved(flat[:, :reach * width_y], "tube", -1, False)
            return call(
                functools.partial(assemble_kernel, planes, width_y, width_z, x_msgs),
                sent, [], 4,
            )(place, flat, ahead, fresh)
        return branch

    pieces = 4
    size = SMAX // pieces
    start, uz, *msgs = lax.switch(
        (shift.astype(jnp.int32) - 1) // size, [shifted((n + 1) * size) for n in range(pieces)])

    in_x, in_y, in_z = shape(cross, width_z), shape(cross, width_z), shape(
        width_z + 2 * ROWS, cross)
    inner_out = (in_x,) * 3 + (in_y,) * 3 + (in_z,) * 3 + (full, full, shape(comps, width_z, cross))
    al = [((planes + 1) * ROWS, width_z), ((width_y + 1) * planes, width_z),
          ((zvecs + 1) * ROWS, cross)]
    inner_scratch = al + [(3, cross, width_z)]
    outer_scratch = [
        (comps, 2 * HALO * ROWS, width_z), (3, 2 * HALO * ROWS, width_z),
        (3, 2 * HALO * planes, width_z), (3, 2 * ROWS, cross),
        *al, (comps, 2 * HALO * ROWS, width_z), (comps, cross, width_z), (comps, width_z, cross),
        (cross, width_z)]
    current = start
    for stage in (1, 2, 3):
        xmsg, (ylo, yhi, zlo, zhi) = msgs[:x_msgs], msgs[x_msgs:]
        ylo = moved(ylo, "gy", 1, True)
        yhi = moved(yhi, "gy", -1, True)
        if swap:
            xlo = xhi = lax.ppermute(xmsg[0], "tube", [(0, 1), (1, 0)])
        else:
            xhi = moved(xmsg[0], "tube", -1, False)
            xlo = moved(xmsg[1], "tube", 1, False)
        zlo = moved(zlo, "gz", 1, True)
        zhi = moved(zhi, "gz", -1, True)
        inner = call(
            functools.partial(inner_kernel, planes, width_y, width_z),
            inner_out, inner_scratch, 2, False)(current, uz)
        current, *rest = call(
            functools.partial(outer_kernel, stage, planes, width_y, width_z, x_msgs),
            (full,) if stage == 3 else sent, outer_scratch, 11 + len(inner_out),
        )(place, current, uz, start, fresh, xlo, xhi, ylo, yhi, zlo, zhi, *inner)
        if stage < 3:
            uz, *msgs = rest

    vmem = pl.BlockSpec(memory_space=pltpu.VMEM)
    reacted = pl.pallas_call(
        functools.partial(chemistry_kernel, planes, 4),
        out_shape=full,
        in_specs=[vmem, vmem],
        out_specs=vmem,
        compiler_params=pltpu.CompilerParams(vmem_limit_bytes=16 * 1024 * 1024),
    )(current, substeps.reshape(cross, width_z))
    return reacted.reshape(state.shape)


def solution(mesh):
    return jax.shard_map(
        on_device,
        mesh=mesh,
        in_specs=(P(None, "tube", "gy", "gz"), P(None, "gy", "gz"), P("tube", "gy", "gz"), P()),
        out_specs=P(None, "tube", "gy", "gz"),
        check_vma=False,
    )
```

```python
import functools

import jax
import jax.numpy as jnp
import numpy as np
from jax import lax
from jax.experimental import pallas as pl
from jax.experimental.pallas import tpu as pltpu
from jax.sharding import PartitionSpec as P

SMAX = 12
HALO = 3
NCOMP = 13
ROWS = 8
SCALE = 0.25
TIME_STEP = 0.05
FLUX_FACTOR = -TIME_STEP / (6.0 * SCALE)

MOLAR = np.array([2.016, 31.998, 18.015, 1.008, 15.999, 17.007, 33.006, 34.014, 28.014]) / 18.015
GAS = 1.0 / MOLAR
FORMATION = np.array([0.0, 0.0, -1.5, 12.0, 1.5, 0.25, 0.02, -0.45, 0.0])
REACTANTS = [
    (3, 1), (4, 5), (4, 0), (3, 5), (0, 5), (2, 3), (4, 2), (5, 5), (0, 8), (3, 3, 8), (4, 4, 8),
    (3, 4, 8), (3, 5, 8), (3, 1, 8), (6, 3), (6, 3), (6, 4), (6, 5), (6, 6), (7, 8), (7, 3),
]
PRODUCTS = [
    (4, 5), (3, 1), (3, 5), (4, 0), (2, 3), (0, 5), (5, 5), (4, 2), (3, 3), (0,), (1,),
    (5,), (2,), (6,), (0, 1), (5, 5), (1, 5), (2, 1), (7, 1), (5, 5), (2, 5),
]
PREFACTOR = [
    30.0, 8.0, 20.0, 6.0, 25.0, 10.0, 12.0, 5.0, 4.0, 20.0, 15.0,
    18.0, 22.0, 25.0, 30.0, 25.0, 20.0, 30.0, 10.0, 6.0, 15.0,
]
BARRIER = [
    4.0, 1.0, 3.0, 1.5, 1.5, 4.5, 4.0, 1.5, 6.0, 0.5, 0.5,
    0.5, 0.5, 0.3, 0.8, 0.5, 0.3, 0.3, 0.5, 5.0, 1.5,
]

KAPPA = 0.609375
EPS = 3.0 * SCALE * SCALE * 1e-6


def rcp(x):
    return pl.reciprocal(x, approx=True)


def correction(d1, d2, d3, d4):
    k2 = KAPPA * (d2 * d2) + EPS
    k3 = KAPPA * (d3 * d3) + EPS
    xa = d1 - 1.375 * d2
    xb = d3 - 0.625 * d2
    xc = d4 - 1.375 * d3
    ra = rcp(xa * xa + k2)
    rb = rcp(xb * xb + k2)
    rc = rcp(xc * xc + k3)
    wa = ra * ra
    wb = 6.0 * (rb * rb)
    wc = 3.0 * (rc * rc)
    return ((xa + xb) * wa + (0.5 * (d2 + d4) - d3) * wc) * rcp(wa + wb + wc)


def face_flux(du, df, f2, f3, alpha):
    e = [alpha * d for d in du]
    p = [df[k] + e[k] for k in range(4)]
    m = [None] + [df[k] - e[k] for k in range(1, 5)]
    linear = 3.0 * (f2 + f3) - e[2] + 0.5 * (p[1] - m[3])
    return linear - correction(p[0], p[1], p[2], p[3]) + correction(m[4], m[3], m[2], m[1])


def sweep(cells, fluxes, alpha, first, last):
    du, df = {}, {}
    out = {}
    for j in range(first, last + 1):
        for k in range(j, j + 5):
            if k not in du:
                du[k] = cells(k + 1) - cells(k)
                df[k] = fluxes(k + 1) - fluxes(k)
        out[j] = face_flux(
            [du[k] for k in range(j, j + 5)],
            [df[k] for k in range(j, j + 5)],
            fluxes(j + 2),
            fluxes(j + 3),
            alpha(j),
        )
    return out


def memo(load):
    return functools.lru_cache(maxsize=None)(load)


def thermo(u):
    g = [u[k] if GAS[k] == 1.0 else u[k] * float(GAS[k]) for k in range(9)]
    s2 = g[2] + g[6] + g[7]
    s3 = g[3] + g[4]
    gas = (g[0] + g[1]) + (g[5] + g[8]) + (s2 + s3)
    heat = 2.5 * gas + (0.5 * s2 - s3)
    bond = 1.5 * (u[4] - u[2]) + 12.0 * u[3] + 0.25 * u[5] + 0.02 * u[6] - 0.45 * u[7]
    rho = ((u[0] + u[1]) + (u[2] + u[3])) + ((u[4] + u[5]) + (u[6] + u[7])) + u[8]
    back = 1.0 / rho
    cold = 1.0 / heat
    motion = 0.5 * (u[9] * u[9] + u[10] * u[10] + u[11] * u[11]) * back
    temperature = (u[12] - motion - bond) * cold
    pressure = gas * temperature
    sound = jnp.sqrt((1.0 + gas * cold) * pressure * back)
    return back, pressure, sound


def for_components(body):
    def step(c, _):
        body(c, (0, 0, 0), lambda n: jnp.maximum(c - n, 0))
        return 0

    lax.fori_loop(0, 9, step, 0)
    kinds = [(1, 0, 0), (0, 1, 0), (0, 0, 1), (2, 2, 2)]
    for c in range(9, NCOMP):
        body(c, kinds[c - 9], lambda n, c=c: c - n)


def flux_of(u, speed, pressure, kind):
    if kind == 0:
        return u * speed
    if kind == 1:
        return u * speed + SCALE * pressure()
    return (u + pressure()) * speed


def own_thermo(planes, width_y, u_ref, x_refs, y_refs, z_refs, tmp):
    span = planes // 2

    def own(i, _):
        for k in range(span):
            p = i * span + k
            here = pl.ds(pl.multiple_of(p * ROWS, ROWS), ROWS)
            u = [u_ref[c, here, :] for c in range(NCOMP)]
            back, pressure, sound = thermo(u)
            back, sound = SCALE * back, SCALE * sound
            across = pl.ds(p, width_y, stride=planes)
            for d, where in ((0, here), (1, across), (2, here)):
                speed = u[9 + d] * back
                for n, value in enumerate((speed, pressure, jnp.abs(speed) + sound)):
                    if d == 2:
                        tmp[n, where, :] = value
                    else:
                        (x_refs, y_refs)[d][n][where, :] = value
        return 0

    lax.fori_loop(0, planes // span, own, 0)
    for n in range(3):
        z_refs[n][pl.ds(ROWS, tmp.shape[2]), :] = tmp[n].T


def inner_kernel(
    planes, width_y, width_z, u_ref, uz_ref,
    ux, px, ax, uy, py, ay, uz, pz, az, accx, accy, accz, alx, aly, alz, tmp,
):
    groups = planes // ROWS
    zvecs = width_z // ROWS
    own_thermo(planes, width_y, u_ref, (ux, px, ax), (uy, py, ay), (uz, pz, az), tmp)

    def xvec(ref):
        return lambda i: ref[pl.ds((i - HALO) * ROWS, ROWS), :]

    def yvec(ref, g):
        return lambda i: ref[pl.ds((i - HALO) * planes + g * ROWS, ROWS), :]

    def zvec(ref):
        return lambda i: ref[pl.ds(ROWS - HALO + i, ROWS, stride=zvecs), :]

    largest(xvec(ax), range(HALO, planes - HALO + 1), alx, lambda j: j * ROWS)
    for g in range(groups):
        largest(yvec(ay, g), range(HALO, width_y - HALO + 1), aly,
                lambda j: j * planes + g * ROWS)
    largest(zvec(az), range(HALO, zvecs - HALO + 1), alz, lambda j: j * ROWS)

    def inner(n, cells, speed, pressure, kind, alpha, put):
        cells = memo(cells)
        fluxes = memo(lambda i: flux_of(cells(i), speed(i), lambda: pressure(i), kind))
        out = sweep(cells, fluxes, alpha, HALO, n - HALO)
        put(HALO - 1, out[HALO])
        for i in range(HALO, n - HALO):
            put(i, out[i + 1] - out[i])
        put(n - HALO, out[n - HALO])

    def x_body(c, kind):
        def put(i, value):
            accx[c, pl.ds(i * ROWS, ROWS), :] = value
        inner(planes, lambda i: u_ref[c, pl.ds((i - HALO) * ROWS, ROWS), :], xvec(ux), xvec(px),
              kind, lambda j: alx[pl.ds(j * ROWS, ROWS), :], put)

    def z_body(c, kind):
        def put(i, value):
            accz[c, pl.ds(i, ROWS, stride=zvecs), :] = value
        inner(zvecs, lambda i: uz_ref[c, pl.ds(ROWS - HALO + i, ROWS, stride=zvecs), :],
              zvec(uz), zvec(pz), kind, lambda j: alz[pl.ds(j * ROWS, ROWS), :], put)

    def y_body(c, kind):
        for g in range(groups):
            def put(i, value, g=g):
                accy[c, pl.ds(g * ROWS * width_y + i, ROWS, stride=width_y), :] = value
            def cell(i, g=g):
                return u_ref[c, pl.ds(g * ROWS * width_y + i - HALO, ROWS, stride=width_y), :]
            inner(width_y, cell, yvec(uy, g), yvec(py, g), kind,
                  lambda j: aly[pl.ds(j * planes + g * ROWS, ROWS), :], put)

    def body(c, kinds, before):
        x_body(c, kinds[0])
        z_body(c, kinds[2])
        y_body(c, kinds[1])

    for_components(body)


def largest(speed, faces, ref, place):
    values = memo(speed)
    for j in faces:
        top = values(j)
        for k in range(1, 6):
            top = jnp.maximum(top, values(j + k))
        ref[pl.ds(place(j), ROWS), :] = top


def outer_kernel(
    stage, planes, width_y, width_z, x_msgs, place,
    u_ref, uz_ref, start_ref, fresh_ref, xlo_ref, xhi_ref, y0_ref, y1_ref, z0_ref, z1_ref,
    ux, px, ax, uy, py, ay, uz, pz, az, accx, accy, accz, *refs,
):
    groups = planes // ROWS
    zvecs = width_z // ROWS
    tube, tubes = place[0], place[1]
    last = stage == 3
    refs = list(refs)
    new_ref = refs.pop(0)
    if not last:
        newz_ref = refs.pop(0)
        xmsg_refs = [refs.pop(0) for _ in range(x_msgs)]
        ymsgs, zmsgs = [refs.pop(0) for _ in range(2)], [refs.pop(0) for _ in range(2)]
    xh, gx, gy, gz, alx, aly, alz, edgex, edgey, edgez, changez = refs

    def lower_y(c, rows):
        return jnp.where(place[5] == 0, y1_ref[c, rows, :], y0_ref[c, rows, :])

    def upper_y(c, rows):
        return jnp.where(place[5] == 0, y0_ref[c, rows, :], y1_ref[c, rows, :])

    def lower_z(c, rows):
        return jnp.where(place[6] == 0, z1_ref[c, rows, :], z0_ref[c, rows, :])

    def upper_z(c, rows):
        return jnp.where(place[6] == 0, z0_ref[c, rows, :], z1_ref[c, rows, :])

    def ghosts(c, _):
        for k in range(HALO):
            here = pl.ds(k * ROWS, ROWS)
            lo = jnp.where(tube == 0, u_ref[c, pl.ds(0, ROWS), :], xlo_ref[c, here, :])
            hi = jnp.where(tube == tubes - 1, fresh_ref[c], xhi_ref[c, here, :])
            xh[c, here, :] = lo
            xh[c, pl.ds((HALO + k) * ROWS, ROWS), :] = hi
        return 0

    lax.fori_loop(0, NCOMP, ghosts, 0)

    def ghost_thermo(u, d, ref, row):
        back, pressure, sound = thermo(u)
        speed = u[9 + d] * (SCALE * back)
        for n, value in enumerate((speed, pressure, jnp.abs(speed) + SCALE * sound)):
            ref[n, pl.ds(row, ROWS), :] = value

    for k in range(2 * HALO):
        ghost_thermo([xh[c, pl.ds(k * ROWS, ROWS), :] for c in range(NCOMP)], 0, gx, k * ROWS)
    for load, offset in ((lower_y, 0), (upper_y, HALO)):
        for k in range(HALO):
            for g in range(groups):
                row = k * planes + g * ROWS
                u = [load(c, pl.ds(row, ROWS)) for c in range(NCOMP)]
                ghost_thermo(u, 1, gy, offset * planes + row)
    ghost_thermo([lower_z(c, pl.ds(0, ROWS)) for c in range(NCOMP)], 2, gz, 0)
    ghost_thermo([upper_z(c, pl.ds(0, ROWS)) for c in range(NCOMP)], 2, gz, ROWS)

    def xvec(ref, n):
        def load(i):
            if HALO <= i < planes + HALO:
                return ref[pl.ds((i - HALO) * ROWS, ROWS), :]
            return gx[n, pl.ds((i if i < HALO else i - planes) * ROWS, ROWS), :]
        return load

    def yvec(ref, n, g):
        def load(i):
            if HALO <= i < width_y + HALO:
                return ref[pl.ds((i - HALO) * planes + g * ROWS, ROWS), :]
            return gy[n, pl.ds((i if i < HALO else i - width_y) * planes + g * ROWS, ROWS), :]
        return load

    row = lax.broadcasted_iota(jnp.int32, (ROWS, planes * width_y), 0)

    def joined(i, load, lo, hi):
        value = load(pl.ds(ROWS - HALO + i, ROWS, stride=zvecs))
        if i < HALO:
            return jnp.where(row == 0, lo(pl.ds(ROWS - HALO + i, 1)), value)
        if i >= zvecs + HALO:
            return jnp.where(row == ROWS - 1, hi(pl.ds(i - zvecs - HALO, 1)), value)
        return value

    def zvec(ref, n):
        def load(i):
            return joined(i, lambda s: ref[s, :], lambda s: gz[n, s, :],
                          lambda s: gz[n, pl.ds(ROWS + s.start, 1), :])
        return load

    def ends(n):
        return list(range(HALO)) + list(range(n - HALO + 1, n + 1))

    largest(xvec(ax, 2), ends(planes), alx, lambda j: j * ROWS)
    for g in range(groups):
        largest(yvec(ay, 2, g), ends(width_y), aly, lambda j: j * planes + g * ROWS)
    largest(zvec(az, 2), ends(zvecs), alz, lambda j: j * ROWS)

    def outer(n, cells, speed, pressure, kind, alpha, given, put):
        cells = memo(cells)
        fluxes = memo(lambda i: flux_of(cells(i), speed(i), lambda: pressure(i), kind))
        out = sweep(cells, fluxes, alpha, 0, HALO - 1)
        out[HALO] = given(HALO - 1)
        for i in range(HALO):
            put(i, out[i + 1] - out[i])
        out = sweep(cells, fluxes, alpha, n - HALO + 1, n)
        out[n - HALO] = given(n - HALO)
        for i in range(n - HALO, n):
            put(i, out[i + 1] - out[i])

    def between(n, rows, width):
        position = lax.broadcasted_iota(jnp.int32, (rows, width), 0) % n
        return (position >= HALO) & (position < n - HALO)

    inside_y = between(width_y, ROWS, width_z)
    inside_z = between(zvecs, width_z, planes * width_y)

    def z_body(c, kind):
        def cell(i):
            return joined(i, lambda s: uz_ref[c, s, :], lambda s: lower_z(c, s),
                          lambda s: upper_z(c, s))
        def put(i, value):
            edgez[c, pl.ds(i, ROWS, stride=zvecs), :] = value
        outer(zvecs, cell, zvec(uz, 0), zvec(pz, 1), kind,
              lambda j: alz[pl.ds(j * ROWS, ROWS), :],
              lambda i: accz[c, pl.ds(i, ROWS, stride=zvecs), :], put)

    def x_body(c, kind):
        def cell(i):
            if HALO <= i < planes + HALO:
                return u_ref[c, pl.ds((i - HALO) * ROWS, ROWS), :]
            return xh[c, pl.ds((i if i < HALO else i - planes) * ROWS, ROWS), :]
        def put(i, value):
            edgex[c, pl.ds((i if i < HALO else i - planes + 2 * HALO) * ROWS, ROWS), :] = value
        outer(planes, cell, xvec(ux, 0), xvec(px, 1), kind,
              lambda j: alx[pl.ds(j * ROWS, ROWS), :],
              lambda i: accx[c, pl.ds(i * ROWS, ROWS), :], put)

    def update(c):
        changez[...] = jnp.where(inside_z, accz[c], edgez[c]).T
        for p in range(planes):
            here = pl.ds(p * ROWS, ROWS)
            change = changez[here, :] + jnp.where(inside_y, accy[c, here, :], edgey[c, here, :])
            if HALO <= p < planes - HALO:
                change = change + accx[c, here, :]
            else:
                k = p if p < HALO else p - planes + 2 * HALO
                change = change + edgex[c, pl.ds(k * ROWS, ROWS), :]
            value = u_ref[c, here, :] + FLUX_FACTOR * change
            if stage == 2:
                value = 0.75 * start_ref[c, here, :] + 0.25 * value
            elif stage == 3:
                value = (1.0 / 3.0) * start_ref[c, here, :] + (2.0 / 3.0) * value
            new_ref[c, here, :] = value

    def pass_on(c):
        if not last:
            newz_ref[c, pl.ds(ROWS, width_z), :] = new_ref[c].T
            messages(c, planes, width_y, width_z, place, new_ref, newz_ref, xmsg_refs,
                     ymsgs, zmsgs)

    def y_body(c, kind):
        for g in range(groups):
            base = g * ROWS * width_y
            def cell(i, g=g, base=base):
                if HALO <= i < width_y + HALO:
                    return u_ref[c, pl.ds(base + i - HALO, ROWS, stride=width_y), :]
                if i < HALO:
                    return lower_y(c, pl.ds(i * planes + g * ROWS, ROWS))
                return upper_y(c, pl.ds((i - HALO - width_y) * planes + g * ROWS, ROWS))
            def put(i, value, base=base):
                edgey[c, pl.ds(base + i, ROWS, stride=width_y), :] = value
            outer(width_y, cell, yvec(uy, 0, g), yvec(py, 1, g), kind,
                  lambda j: aly[pl.ds(j * planes + g * ROWS, ROWS), :],
                  lambda i: accy[c, pl.ds(base + i, ROWS, stride=width_y), :], put)

    def body(c, kinds, before):
        pass_on(before(2))
        update(before(1))
        z_body(c, kinds[2])
        x_body(c, kinds[0])
        y_body(c, kinds[1])

    for_components(body)
    pass_on(NCOMP - 2)
    update(NCOMP - 1)
    pass_on(NCOMP - 1)


def messages(c, planes, width_y, width_z, place, u_ref, uz_ref, xmsg_refs, ymsgs, zmsgs):
    for n, ref in enumerate(xmsg_refs):
        begin = place[2 + n]
        for k in range(HALO):
            rows = pl.ds(pl.multiple_of((begin + k) * ROWS, ROWS), ROWS)
            ref[c, pl.ds(k * ROWS, ROWS), :] = u_ref[c, rows, :]
    for n in range(2):
        upper = place[5] == n
        for k in range(HALO):
            for g in range(planes // ROWS):
                base = g * ROWS * width_y + k
                low = u_ref[c, pl.ds(base, ROWS, stride=width_y), :]
                high = u_ref[c, pl.ds(base + width_y - HALO, ROWS, stride=width_y), :]
                ymsgs[n][c, pl.ds(k * planes + g * ROWS, ROWS), :] = jnp.where(upper, high, low)
        begin = pl.multiple_of(jnp.where(place[6] == n, width_z, ROWS), ROWS)
        zmsgs[n][c] = uz_ref[c, pl.ds(begin, ROWS), :]


def assemble_kernel(
    planes, width_y, width_z, x_msgs, place, state_ref, ahead_ref, fresh_ref, u_ref, uz_ref, *refs,
):
    refs = list(refs)
    xmsg_refs = [refs.pop(0) for _ in range(x_msgs)]
    ymsgs, zmsgs = refs[:2], refs[2:]
    tube, tubes, shift = place[0], place[1], place[4]
    reach = ahead_ref.shape[1] // ROWS

    def pass_on(c):
        uz_ref[c, pl.ds(ROWS, width_z), :] = u_ref[c].T
        messages(c, planes, width_y, width_z, place, u_ref, uz_ref, xmsg_refs,
                 ymsgs, zmsgs)

    for c in range(NCOMP):
        if c:
            pass_on(c - 1)
        fresh = fresh_ref[c]
        for i in range(planes):
            source = shift + i
            own = jnp.minimum(source, planes - 1)
            value = state_ref[c, pl.ds(pl.multiple_of(own * ROWS, ROWS), ROWS), :]
            if i >= planes - reach:
                beyond = jnp.clip(source - planes, 0, reach - 1)
                other = ahead_ref[c, pl.ds(pl.multiple_of(beyond * ROWS, ROWS), ROWS), :]
                other = jnp.where(tube == tubes - 1, fresh, other)
                value = jnp.where(source >= planes, other, value)
            u_ref[c, pl.ds(i * ROWS, ROWS), :] = value
    pass_on(NCOMP - 1)


def powers_of(back):
    a = jnp.exp(-0.5 * back)
    b = jnp.exp(-0.3 * back)
    a2 = a * a
    a3 = a2 * a
    a4 = a2 * a2
    a6 = a3 * a3
    a8 = a4 * a4
    return {0.5: a, 0.3: b, 1.0: a2, 1.5: a3, 3.0: a6, 4.0: a8, 4.5: a8 * a, 5.0: a8 * a2,
            6.0: a6 * a6, 0.8: a * b}


def react(conc, internal, size):
    s2 = conc[2] + conc[6] + conc[7]
    s3 = conc[3] + conc[4]
    heat = 2.5 * (((conc[0] + conc[1]) + (conc[5] + conc[8])) + (s2 + s3)) + (0.5 * s2 - s3)
    bond = None
    for k in range(9):
        if FORMATION[k]:
            term = float(FORMATION[k] * MOLAR[k]) * conc[k]
            bond = term if bond is None else bond + term
    boltzmann = powers_of(heat / (internal - bond))
    pairs = {}
    omega = [None] * 9

    def add(k, value):
        omega[k] = value if omega[k] is None else omega[k] + value

    def sub(k, value):
        omega[k] = -value if omega[k] is None else omega[k] - value

    def rate(j):
        names = REACTANTS[j]
        key = tuple(sorted(names))
        if key not in pairs:
            value = conc[names[0]] * conc[names[1]]
            if len(names) == 3:
                base = tuple(sorted(names[:2]))
                if base not in pairs:
                    pairs[base] = value
                value = pairs[base] * conc[8]
            pairs[key] = value
        return (PREFACTOR[j] * boltzmann[BARRIER[j]]) * pairs[key]

    j = 0
    while j < len(REACTANTS):
        value = rate(j)
        back = j + 1 < len(REACTANTS) and REACTANTS[j + 1] == PRODUCTS[j] \
            and PRODUCTS[j + 1] == REACTANTS[j]
        if back:
            value = value - rate(j + 1)
        for k in range(9):
            times = PRODUCTS[j].count(k) - REACTANTS[j].count(k)
            if times == 0:
                continue
            amount = value if abs(times) == 1 else value + value
            if times > 0:
                add(k, amount)
            else:
                sub(k, amount)
        j += 2 if back else 1
    return [conc[k] + size * omega[k] for k in range(9)]


def chemistry_kernel(planes, span, third_ref, counts_ref, out_ref):
    for c in range(9, NCOMP):
        out_ref[c] = third_ref[c]

    def block(i, _):
        rows = [
            pl.ds(pl.multiple_of((i * span + k) * ROWS, ROWS), ROWS) for k in range(span)
        ]
        counts = [counts_ref[r, :] for r in rows]
        sizes = [TIME_STEP / n.astype(jnp.float32) for n in counts]
        most = counts[0]
        for n in counts[1:]:
            most = jnp.maximum(most, n)
        turns = jnp.max(most)
        conc, internal = [], []
        for r in rows:
            u = [third_ref[c, r, :] for c in range(NCOMP)]
            rho = ((u[0] + u[1]) + (u[2] + u[3])) + ((u[4] + u[5]) + (u[6] + u[7])) + u[8]
            internal.append(
                u[12] - 0.5 * (u[9] * u[9] + u[10] * u[10] + u[11] * u[11]) / rho)
            conc.append([u[k] * float(GAS[k]) for k in range(9)])

        def advance(index, carry):
            new = []
            for k in range(span):
                moved = react(carry[k], internal[k], sizes[k])
                keep = index < counts[k]
                new.append([jnp.where(keep, m, o) for m, o in zip(moved, carry[k])])
            return new

        conc = lax.fori_loop(0, turns, advance, conc)
        for k in range(span):
            for c in range(9):
                out_ref[c, rows[k], :] = conc[k][c] * float(MOLAR[c])
        return 0

    lax.fori_loop(0, planes // span, block, 0)


def shape(*dims):
    return jax.ShapeDtypeStruct(dims, jnp.float32)


def call(kernel, out_shape, scratch, n_in, scalars=True):
    vmem = pl.BlockSpec(memory_space=pltpu.VMEM)
    specs = [vmem] * n_in
    if scalars:
        specs[0] = pl.BlockSpec(memory_space=pltpu.SMEM)
    return pl.pallas_call(
        kernel,
        out_shape=out_shape,
        in_specs=specs,
        out_specs=jax.tree.map(lambda _: vmem, out_shape),
        scratch_shapes=[pltpu.VMEM(dims, jnp.float32) for dims in scratch],
        compiler_params=pltpu.CompilerParams(vmem_limit_bytes=16 * 1024 * 1024),
    )


def moved(value, axis, steps):
    count = lax.axis_size(axis)
    pairs = [(i, i + steps) for i in range(count) if 0 <= i + steps < count]
    return lax.ppermute(value, axis, pairs)


def swapped(value, axis, which):
    count = lax.axis_size(axis)
    assert count % 2 == 0
    step = 1 - 2 * which
    return lax.ppermute(
        value, axis, [(i, (i + (step if i % 2 == 0 else -step)) % count) for i in range(count)])


def on_device(state, fresh, substeps, shift):
    comps, planes, width_y, width_z = state.shape
    cross = planes * width_y
    zvecs = width_z // ROWS
    tubes = lax.axis_size("tube")
    tube = lax.axis_index("tube")
    swap = tubes == 2
    x_msgs = 1 if swap else 2
    begins = [jnp.where(tube == 0, planes - HALO, 0), 0] if swap else [0, planes - HALO]
    place = jnp.stack([
        tube.astype(jnp.int32), jnp.int32(tubes), jnp.asarray(begins[0], jnp.int32),
        jnp.asarray(begins[1], jnp.int32), shift.astype(jnp.int32),
        lax.axis_index("gy") % 2, lax.axis_index("gz") % 2])

    full = shape(comps, cross, width_z)
    fullz = shape(comps, width_z + 2 * ROWS, cross)
    xs = shape(comps, HALO * ROWS, width_z)
    ys = shape(comps, HALO * planes, width_z)
    zs = shape(comps, ROWS, cross)
    sent = (full, fullz) + (xs,) * x_msgs + (ys, ys, zs, zs)
    flat = state.reshape(comps, cross, width_z)

    def shifted(reach):
        def branch():
            ahead = moved(flat[:, :reach * width_y], "tube", -1)
            return call(
                functools.partial(assemble_kernel, planes, width_y, width_z, x_msgs),
                sent, [], 4,
            )(place, flat, ahead, fresh)
        return branch

    pieces = SMAX
    size = SMAX // pieces
    start, uz, *msgs = lax.switch(
        (shift.astype(jnp.int32) - 1) // size, [shifted((n + 1) * size) for n in range(pieces)])

    in_x, in_y, in_z = shape(cross, width_z), shape(cross, width_z), shape(
        width_z + 2 * ROWS, cross)
    inner_out = (in_x,) * 3 + (in_y,) * 3 + (in_z,) * 3 + (full, full, shape(comps, width_z, cross))
    al = [((planes + 1) * ROWS, width_z), ((width_y + 1) * planes, width_z),
          ((zvecs + 1) * ROWS, cross)]
    inner_scratch = al + [(3, cross, width_z)]
    outer_scratch = [
        (comps, 2 * HALO * ROWS, width_z), (3, 2 * HALO * ROWS, width_z),
        (3, 2 * HALO * planes, width_z), (3, 2 * ROWS, cross),
        *al, (comps, 2 * HALO * ROWS, width_z), (comps, cross, width_z), (comps, width_z, cross),
        (cross, width_z)]
    current = start
    for stage in (1, 2, 3):
        xmsg, (y0, y1, z0, z1) = msgs[:x_msgs], msgs[x_msgs:]
        y1 = swapped(y1, "gy", 1)
        if swap:
            xlo = xhi = lax.ppermute(xmsg[0], "tube", [(0, 1), (1, 0)])
        else:
            xhi = moved(xmsg[0], "tube", -1)
            xlo = moved(xmsg[1], "tube", 1)
        z1 = swapped(z1, "gz", 1)
        z0 = swapped(z0, "gz", 0)
        y0 = swapped(y0, "gy", 0)
        inner = call(
            functools.partial(inner_kernel, planes, width_y, width_z),
            inner_out, inner_scratch, 2, False)(current, uz)
        current, *rest = call(
            functools.partial(outer_kernel, stage, planes, width_y, width_z, x_msgs),
            (full,) if stage == 3 else sent, outer_scratch, 11 + len(inner_out),
        )(place, current, uz, start, fresh, xlo, xhi, y0, y1, z0, z1, *inner)
        if stage < 3:
            uz, *msgs = rest

    vmem = pl.BlockSpec(memory_space=pltpu.VMEM)
    reacted = pl.pallas_call(
        functools.partial(chemistry_kernel, planes, 4),
        out_shape=full,
        in_specs=[vmem, vmem],
        out_specs=vmem,
        compiler_params=pltpu.CompilerParams(vmem_limit_bytes=16 * 1024 * 1024),
    )(current, substeps.reshape(cross, width_z))
    return reacted.reshape(state.shape)


def solution(mesh):
    return jax.shard_map(
        on_device,
        mesh=mesh,
        in_specs=(P(None, "tube", "gy", "gz"), P(None, "gy", "gz"), P("tube", "gy", "gz"), P()),
        out_specs=P(None, "tube", "gy", "gz"),
        check_vma=False,
    )
```

```python
import functools

import jax
import jax.numpy as jnp
import numpy as np
from jax import lax
from jax.experimental import pallas as pl
from jax.experimental.pallas import tpu as pltpu
from jax.sharding import PartitionSpec as P

SMAX = 12
HALO = 3
NCOMP = 13
ROWS = 8
SCALE = 0.25
TIME_STEP = 0.05
FLUX_FACTOR = -TIME_STEP / (6.0 * SCALE)

MOLAR = np.array([2.016, 31.998, 18.015, 1.008, 15.999, 17.007, 33.006, 34.014, 28.014]) / 18.015
GAS = 1.0 / MOLAR
FORMATION = np.array([0.0, 0.0, -1.5, 12.0, 1.5, 0.25, 0.02, -0.45, 0.0])
REACTANTS = [
    (3, 1), (4, 5), (4, 0), (3, 5), (0, 5), (2, 3), (4, 2), (5, 5), (0, 8), (3, 3, 8), (4, 4, 8),
    (3, 4, 8), (3, 5, 8), (3, 1, 8), (6, 3), (6, 3), (6, 4), (6, 5), (6, 6), (7, 8), (7, 3),
]
PRODUCTS = [
    (4, 5), (3, 1), (3, 5), (4, 0), (2, 3), (0, 5), (5, 5), (4, 2), (3, 3), (0,), (1,),
    (5,), (2,), (6,), (0, 1), (5, 5), (1, 5), (2, 1), (7, 1), (5, 5), (2, 5),
]
PREFACTOR = [
    30.0, 8.0, 20.0, 6.0, 25.0, 10.0, 12.0, 5.0, 4.0, 20.0, 15.0,
    18.0, 22.0, 25.0, 30.0, 25.0, 20.0, 30.0, 10.0, 6.0, 15.0,
]
BARRIER = [
    4.0, 1.0, 3.0, 1.5, 1.5, 4.5, 4.0, 1.5, 6.0, 0.5, 0.5,
    0.5, 0.5, 0.3, 0.8, 0.5, 0.3, 0.3, 0.5, 5.0, 1.5,
]

KAPPA = 0.609375
EPS = 3.0 * SCALE * SCALE * 1e-6


def rcp(x):
    return pl.reciprocal(x, approx=True)


def correction(d1, d2, d3, d4):
    k2 = KAPPA * (d2 * d2) + EPS
    k3 = KAPPA * (d3 * d3) + EPS
    xa = d1 - 1.375 * d2
    xb = d3 - 0.625 * d2
    xc = d4 - 1.375 * d3
    ra = rcp(xa * xa + k2)
    rb = rcp(xb * xb + k2)
    rc = rcp(xc * xc + k3)
    wa = ra * ra
    wb = 6.0 * (rb * rb)
    wc = 3.0 * (rc * rc)
    return ((xa + xb) * wa + (0.5 * (d2 + d4) - d3) * wc) * rcp(wa + wb + wc)


def face_flux(du, df, f2, f3, alpha):
    e = [alpha * d for d in du]
    p = [df[k] + e[k] for k in range(4)]
    m = [None] + [df[k] - e[k] for k in range(1, 5)]
    linear = 3.0 * (f2 + f3) - e[2] + 0.5 * (p[1] - m[3])
    return linear - correction(p[0], p[1], p[2], p[3]) + correction(m[4], m[3], m[2], m[1])


def sweep(cells, fluxes, alpha, first, last):
    du, df = {}, {}
    out = {}
    for j in range(first, last + 1):
        for k in range(j, j + 5):
            if k not in du:
                du[k] = cells(k + 1) - cells(k)
                df[k] = fluxes(k + 1) - fluxes(k)
        out[j] = face_flux(
            [du[k] for k in range(j, j + 5)],
            [df[k] for k in range(j, j + 5)],
            fluxes(j + 2),
            fluxes(j + 3),
            alpha(j),
        )
    return out


def memo(load):
    return functools.lru_cache(maxsize=None)(load)


def thermo(u):
    g = [u[k] if GAS[k] == 1.0 else u[k] * float(GAS[k]) for k in range(9)]
    s2 = g[2] + g[6] + g[7]
    s3 = g[3] + g[4]
    gas = (g[0] + g[1]) + (g[5] + g[8]) + (s2 + s3)
    heat = 2.5 * gas + (0.5 * s2 - s3)
    bond = 1.5 * (u[4] - u[2]) + 12.0 * u[3] + 0.25 * u[5] + 0.02 * u[6] - 0.45 * u[7]
    rho = ((u[0] + u[1]) + (u[2] + u[3])) + ((u[4] + u[5]) + (u[6] + u[7])) + u[8]
    back = 1.0 / rho
    cold = 1.0 / heat
    motion = 0.5 * (u[9] * u[9] + u[10] * u[10] + u[11] * u[11]) * back
    temperature = (u[12] - motion - bond) * cold
    pressure = gas * temperature
    sound = jnp.sqrt((1.0 + gas * cold) * pressure * back)
    return back, pressure, sound


def for_components(body):
    together = 3

    def step(i, _):
        for k in range(together):
            c = i * together + k
            body(c, (0, 0, 0), lambda n, c=c: jnp.maximum(c - n, 0))
        return 0

    lax.fori_loop(0, 9 // together, step, 0)
    kinds = [(1, 0, 0), (0, 1, 0), (0, 0, 1), (2, 2, 2)]
    for c in range(9, NCOMP):
        body(c, kinds[c - 9], lambda n, c=c: c - n)


def flux_of(u, speed, pressure, kind):
    if kind == 0:
        return u * speed
    if kind == 1:
        return u * speed + SCALE * pressure()
    return (u + pressure()) * speed


def own_thermo(planes, width_y, u_ref, x_refs, y_refs, z_refs, tmp):
    span = planes // 2

    def own(i, _):
        for k in range(span):
            p = i * span + k
            here = pl.ds(pl.multiple_of(p * ROWS, ROWS), ROWS)
            u = [u_ref[c, here, :] for c in range(NCOMP)]
            back, pressure, sound = thermo(u)
            back, sound = SCALE * back, SCALE * sound
            across = pl.ds(p, width_y, stride=planes)
            for d, where in ((0, here), (1, across), (2, here)):
                speed = u[9 + d] * back
                for n, value in enumerate((speed, pressure, jnp.abs(speed) + sound)):
                    if d == 2:
                        tmp[n, where, :] = value
                    else:
                        (x_refs, y_refs)[d][n][where, :] = value
        return 0

    lax.fori_loop(0, planes // span, own, 0)
    for n in range(3):
        z_refs[n][pl.ds(ROWS, tmp.shape[2]), :] = tmp[n].T


def inner_kernel(
    planes, width_y, width_z, u_ref, uz_ref,
    ux, px, ax, uy, py, ay, uz, pz, az, accx, accy, accz, alx, aly, alz, tmp,
):
    groups = planes // ROWS
    zvecs = width_z // ROWS
    own_thermo(planes, width_y, u_ref, (ux, px, ax), (uy, py, ay), (uz, pz, az), tmp)

    def xvec(ref):
        return lambda i: ref[pl.ds((i - HALO) * ROWS, ROWS), :]

    def yvec(ref, g):
        return lambda i: ref[pl.ds((i - HALO) * planes + g * ROWS, ROWS), :]

    def zvec(ref):
        return lambda i: ref[pl.ds(ROWS - HALO + i, ROWS, stride=zvecs), :]

    largest(xvec(ax), range(HALO, planes - HALO + 1), alx, lambda j: j * ROWS)
    for g in range(groups):
        largest(yvec(ay, g), range(HALO, width_y - HALO + 1), aly,
                lambda j: j * planes + g * ROWS)
    largest(zvec(az), range(HALO, zvecs - HALO + 1), alz, lambda j: j * ROWS)

    def inner(n, cells, speed, pressure, kind, alpha, put):
        cells = memo(cells)
        fluxes = memo(lambda i: flux_of(cells(i), speed(i), lambda: pressure(i), kind))
        out = sweep(cells, fluxes, alpha, HALO, n - HALO)
        put(HALO - 1, out[HALO])
        for i in range(HALO, n - HALO):
            put(i, out[i + 1] - out[i])
        put(n - HALO, out[n - HALO])

    def x_body(c, kind):
        def put(i, value):
            accx[c, pl.ds(i * ROWS, ROWS), :] = value
        inner(planes, lambda i: u_ref[c, pl.ds((i - HALO) * ROWS, ROWS), :], xvec(ux), xvec(px),
              kind, lambda j: alx[pl.ds(j * ROWS, ROWS), :], put)

    def z_body(c, kind):
        def put(i, value):
            accz[c, pl.ds(i, ROWS, stride=zvecs), :] = value
        inner(zvecs, lambda i: uz_ref[c, pl.ds(ROWS - HALO + i, ROWS, stride=zvecs), :],
              zvec(uz), zvec(pz), kind, lambda j: alz[pl.ds(j * ROWS, ROWS), :], put)

    def y_body(c, kind):
        for g in range(groups):
            def put(i, value, g=g):
                accy[c, pl.ds(g * ROWS * width_y + i, ROWS, stride=width_y), :] = value
            def cell(i, g=g):
                return u_ref[c, pl.ds(g * ROWS * width_y + i - HALO, ROWS, stride=width_y), :]
            inner(width_y, cell, yvec(uy, g), yvec(py, g), kind,
                  lambda j: aly[pl.ds(j * planes + g * ROWS, ROWS), :], put)

    def body(c, kinds, before):
        x_body(c, kinds[0])
        z_body(c, kinds[2])
        y_body(c, kinds[1])

    for_components(body)


def largest(speed, faces, ref, place):
    values = memo(speed)
    for j in faces:
        top = values(j)
        for k in range(1, 6):
            top = jnp.maximum(top, values(j + k))
        ref[pl.ds(place(j), ROWS), :] = top


def outer_kernel(
    stage, planes, width_y, width_z, x_msgs, place,
    u_ref, uz_ref, start_ref, fresh_ref, xlo_ref, xhi_ref, y0_ref, y1_ref, z0_ref, z1_ref,
    ux, px, ax, uy, py, ay, uz, pz, az, accx, accy, accz, *refs,
):
    groups = planes // ROWS
    zvecs = width_z // ROWS
    tube, tubes = place[0], place[1]
    last = stage == 3
    refs = list(refs)
    new_ref = refs.pop(0)
    if not last:
        newz_ref = refs.pop(0)
        xmsg_refs = [refs.pop(0) for _ in range(x_msgs)]
        ymsgs, zmsgs = [refs.pop(0) for _ in range(2)], [refs.pop(0) for _ in range(2)]
    xh, gx, gy, gz, alx, aly, alz, edgex, edgey, edgez, changez = refs

    def lower_y(c, rows):
        return jnp.where(place[5] == 0, y1_ref[c, rows, :], y0_ref[c, rows, :])

    def upper_y(c, rows):
        return jnp.where(place[5] == 0, y0_ref[c, rows, :], y1_ref[c, rows, :])

    def lower_z(c, rows):
        return jnp.where(place[6] == 0, z1_ref[c, rows, :], z0_ref[c, rows, :])

    def upper_z(c, rows):
        return jnp.where(place[6] == 0, z0_ref[c, rows, :], z1_ref[c, rows, :])

    def ghosts(c, _):
        for k in range(HALO):
            here = pl.ds(k * ROWS, ROWS)
            lo = jnp.where(tube == 0, u_ref[c, pl.ds(0, ROWS), :], xlo_ref[c, here, :])
            hi = jnp.where(tube == tubes - 1, fresh_ref[c], xhi_ref[c, here, :])
            xh[c, here, :] = lo
            xh[c, pl.ds((HALO + k) * ROWS, ROWS), :] = hi
        return 0

    lax.fori_loop(0, NCOMP, ghosts, 0)

    def ghost_thermo(u, d, ref, row):
        back, pressure, sound = thermo(u)
        speed = u[9 + d] * (SCALE * back)
        for n, value in enumerate((speed, pressure, jnp.abs(speed) + SCALE * sound)):
            ref[n, pl.ds(row, ROWS), :] = value

    for k in range(2 * HALO):
        ghost_thermo([xh[c, pl.ds(k * ROWS, ROWS), :] for c in range(NCOMP)], 0, gx, k * ROWS)
    for load, offset in ((lower_y, 0), (upper_y, HALO)):
        for k in range(HALO):
            for g in range(groups):
                row = k * planes + g * ROWS
                u = [load(c, pl.ds(row, ROWS)) for c in range(NCOMP)]
                ghost_thermo(u, 1, gy, offset * planes + row)
    ghost_thermo([lower_z(c, pl.ds(0, ROWS)) for c in range(NCOMP)], 2, gz, 0)
    ghost_thermo([upper_z(c, pl.ds(0, ROWS)) for c in range(NCOMP)], 2, gz, ROWS)

    def xvec(ref, n):
        def load(i):
            if HALO <= i < planes + HALO:
                return ref[pl.ds((i - HALO) * ROWS, ROWS), :]
            return gx[n, pl.ds((i if i < HALO else i - planes) * ROWS, ROWS), :]
        return load

    def yvec(ref, n, g):
        def load(i):
            if HALO <= i < width_y + HALO:
                return ref[pl.ds((i - HALO) * planes + g * ROWS, ROWS), :]
            return gy[n, pl.ds((i if i < HALO else i - width_y) * planes + g * ROWS, ROWS), :]
        return load

    row = lax.broadcasted_iota(jnp.int32, (ROWS, planes * width_y), 0)

    def joined(i, load, lo, hi):
        value = load(pl.ds(ROWS - HALO + i, ROWS, stride=zvecs))
        if i < HALO:
            return jnp.where(row == 0, lo(pl.ds(ROWS - HALO + i, 1)), value)
        if i >= zvecs + HALO:
            return jnp.where(row == ROWS - 1, hi(pl.ds(i - zvecs - HALO, 1)), value)
        return value

    def zvec(ref, n):
        def load(i):
            return joined(i, lambda s: ref[s, :], lambda s: gz[n, s, :],
                          lambda s: gz[n, pl.ds(ROWS + s.start, 1), :])
        return load

    def ends(n):
        return list(range(HALO)) + list(range(n - HALO + 1, n + 1))

    largest(xvec(ax, 2), ends(planes), alx, lambda j: j * ROWS)
    for g in range(groups):
        largest(yvec(ay, 2, g), ends(width_y), aly, lambda j: j * planes + g * ROWS)
    largest(zvec(az, 2), ends(zvecs), alz, lambda j: j * ROWS)

    def outer(n, cells, speed, pressure, kind, alpha, given, put):
        cells = memo(cells)
        fluxes = memo(lambda i: flux_of(cells(i), speed(i), lambda: pressure(i), kind))
        out = sweep(cells, fluxes, alpha, 0, HALO - 1)
        out[HALO] = given(HALO - 1)
        for i in range(HALO):
            put(i, out[i + 1] - out[i])
        out = sweep(cells, fluxes, alpha, n - HALO + 1, n)
        out[n - HALO] = given(n - HALO)
        for i in range(n - HALO, n):
            put(i, out[i + 1] - out[i])

    def between(n, rows, width):
        position = lax.broadcasted_iota(jnp.int32, (rows, width), 0) % n
        return (position >= HALO) & (position < n - HALO)

    inside_y = between(width_y, ROWS, width_z)
    inside_z = between(zvecs, width_z, planes * width_y)

    def z_body(c, kind):
        def cell(i):
            return joined(i, lambda s: uz_ref[c, s, :], lambda s: lower_z(c, s),
                          lambda s: upper_z(c, s))
        def put(i, value):
            edgez[c, pl.ds(i, ROWS, stride=zvecs), :] = value
        outer(zvecs, cell, zvec(uz, 0), zvec(pz, 1), kind,
              lambda j: alz[pl.ds(j * ROWS, ROWS), :],
              lambda i: accz[c, pl.ds(i, ROWS, stride=zvecs), :], put)

    def x_body(c, kind):
        def cell(i):
            if HALO <= i < planes + HALO:
                return u_ref[c, pl.ds((i - HALO) * ROWS, ROWS), :]
            return xh[c, pl.ds((i if i < HALO else i - planes) * ROWS, ROWS), :]
        def put(i, value):
            edgex[c, pl.ds((i if i < HALO else i - planes + 2 * HALO) * ROWS, ROWS), :] = value
        outer(planes, cell, xvec(ux, 0), xvec(px, 1), kind,
              lambda j: alx[pl.ds(j * ROWS, ROWS), :],
              lambda i: accx[c, pl.ds(i * ROWS, ROWS), :], put)

    def update(c):
        changez[...] = jnp.where(inside_z, accz[c], edgez[c]).T
        for p in range(planes):
            here = pl.ds(p * ROWS, ROWS)
            change = changez[here, :] + jnp.where(inside_y, accy[c, here, :], edgey[c, here, :])
            if HALO <= p < planes - HALO:
                change = change + accx[c, here, :]
            else:
                k = p if p < HALO else p - planes + 2 * HALO
                change = change + edgex[c, pl.ds(k * ROWS, ROWS), :]
            value = u_ref[c, here, :] + FLUX_FACTOR * change
            if stage == 2:
                value = 0.75 * start_ref[c, here, :] + 0.25 * value
            elif stage == 3:
                value = (1.0 / 3.0) * start_ref[c, here, :] + (2.0 / 3.0) * value
            new_ref[c, here, :] = value

    def pass_on(c):
        if not last:
            newz_ref[c, pl.ds(ROWS, width_z), :] = new_ref[c].T
            messages(c, planes, width_y, width_z, place, new_ref, newz_ref, xmsg_refs,
                     ymsgs, zmsgs)

    def y_body(c, kind):
        for g in range(groups):
            base = g * ROWS * width_y
            def cell(i, g=g, base=base):
                if HALO <= i < width_y + HALO:
                    return u_ref[c, pl.ds(base + i - HALO, ROWS, stride=width_y), :]
                if i < HALO:
                    return lower_y(c, pl.ds(i * planes + g * ROWS, ROWS))
                return upper_y(c, pl.ds((i - HALO - width_y) * planes + g * ROWS, ROWS))
            def put(i, value, base=base):
                edgey[c, pl.ds(base + i, ROWS, stride=width_y), :] = value
            outer(width_y, cell, yvec(uy, 0, g), yvec(py, 1, g), kind,
                  lambda j: aly[pl.ds(j * planes + g * ROWS, ROWS), :],
                  lambda i: accy[c, pl.ds(base + i, ROWS, stride=width_y), :], put)

    def body(c, kinds, before):
        pass_on(before(2))
        update(before(1))
        z_body(c, kinds[2])
        x_body(c, kinds[0])
        y_body(c, kinds[1])

    for_components(body)
    pass_on(NCOMP - 2)
    update(NCOMP - 1)
    pass_on(NCOMP - 1)


def messages(c, planes, width_y, width_z, place, u_ref, uz_ref, xmsg_refs, ymsgs, zmsgs):
    for n, ref in enumerate(xmsg_refs):
        begin = place[2 + n]
        for k in range(HALO):
            rows = pl.ds(pl.multiple_of((begin + k) * ROWS, ROWS), ROWS)
            ref[c, pl.ds(k * ROWS, ROWS), :] = u_ref[c, rows, :]
    for n in range(2):
        upper = place[5] == n
        for k in range(HALO):
            for g in range(planes // ROWS):
                base = g * ROWS * width_y + k
                low = u_ref[c, pl.ds(base, ROWS, stride=width_y), :]
                high = u_ref[c, pl.ds(base + width_y - HALO, ROWS, stride=width_y), :]
                ymsgs[n][c, pl.ds(k * planes + g * ROWS, ROWS), :] = jnp.where(upper, high, low)
        begin = pl.multiple_of(jnp.where(place[6] == n, width_z, ROWS), ROWS)
        zmsgs[n][c] = uz_ref[c, pl.ds(begin, ROWS), :]


def assemble_kernel(
    planes, width_y, width_z, x_msgs, place, state_ref, ahead_ref, fresh_ref, u_ref, uz_ref, *refs,
):
    refs = list(refs)
    xmsg_refs = [refs.pop(0) for _ in range(x_msgs)]
    ymsgs, zmsgs = refs[:2], refs[2:]
    tube, tubes, shift = place[0], place[1], place[4]
    reach = ahead_ref.shape[1] // ROWS

    def pass_on(c):
        uz_ref[c, pl.ds(ROWS, width_z), :] = u_ref[c].T
        messages(c, planes, width_y, width_z, place, u_ref, uz_ref, xmsg_refs,
                 ymsgs, zmsgs)

    for c in range(NCOMP):
        if c:
            pass_on(c - 1)
        fresh = fresh_ref[c]
        for i in range(planes):
            source = shift + i
            own = jnp.minimum(source, planes - 1)
            value = state_ref[c, pl.ds(pl.multiple_of(own * ROWS, ROWS), ROWS), :]
            if i >= planes - reach:
                beyond = jnp.clip(source - planes, 0, reach - 1)
                other = ahead_ref[c, pl.ds(pl.multiple_of(beyond * ROWS, ROWS), ROWS), :]
                other = jnp.where(tube == tubes - 1, fresh, other)
                value = jnp.where(source >= planes, other, value)
            u_ref[c, pl.ds(i * ROWS, ROWS), :] = value
    pass_on(NCOMP - 1)


def powers_of(back):
    a = jnp.exp(-0.5 * back)
    b = jnp.exp(-0.3 * back)
    a2 = a * a
    a3 = a2 * a
    a4 = a2 * a2
    a6 = a3 * a3
    a8 = a4 * a4
    return {0.5: a, 0.3: b, 1.0: a2, 1.5: a3, 3.0: a6, 4.0: a8, 4.5: a8 * a, 5.0: a8 * a2,
            6.0: a6 * a6, 0.8: a * b}


def react(conc, internal, size):
    s2 = conc[2] + conc[6] + conc[7]
    s3 = conc[3] + conc[4]
    heat = 2.5 * (((conc[0] + conc[1]) + (conc[5] + conc[8])) + (s2 + s3)) + (0.5 * s2 - s3)
    bond = None
    for k in range(9):
        if FORMATION[k]:
            term = float(FORMATION[k] * MOLAR[k]) * conc[k]
            bond = term if bond is None else bond + term
    boltzmann = powers_of(heat / (internal - bond))
    pairs = {}
    omega = [None] * 9

    def add(k, value):
        omega[k] = value if omega[k] is None else omega[k] + value

    def sub(k, value):
        omega[k] = -value if omega[k] is None else omega[k] - value

    def rate(j):
        names = REACTANTS[j]
        key = tuple(sorted(names))
        if key not in pairs:
            value = conc[names[0]] * conc[names[1]]
            if len(names) == 3:
                base = tuple(sorted(names[:2]))
                if base not in pairs:
                    pairs[base] = value
                value = pairs[base] * conc[8]
            pairs[key] = value
        return (PREFACTOR[j] * boltzmann[BARRIER[j]]) * pairs[key]

    j = 0
    while j < len(REACTANTS):
        value = rate(j)
        back = j + 1 < len(REACTANTS) and REACTANTS[j + 1] == PRODUCTS[j] \
            and PRODUCTS[j + 1] == REACTANTS[j]
        if back:
            value = value - rate(j + 1)
        for k in range(9):
            times = PRODUCTS[j].count(k) - REACTANTS[j].count(k)
            if times == 0:
                continue
            amount = value if abs(times) == 1 else value + value
            if times > 0:
                add(k, amount)
            else:
                sub(k, amount)
        j += 2 if back else 1
    return [conc[k] + size * omega[k] for k in range(9)]


def chemistry_kernel(planes, span, third_ref, counts_ref, out_ref, made, sems):
    blocks = planes // span
    kept = pltpu.make_async_copy(
        third_ref.at[pl.ds(9, NCOMP - 9)], out_ref.at[pl.ds(9, NCOMP - 9)], sems.at[blocks])
    kept.start()
    copies = [kept]
    for i in reversed(range(blocks)):
        rows = [pl.ds((i * span + k) * ROWS, ROWS) for k in range(span)]
        counts = [counts_ref[r, :] for r in rows]
        sizes = [TIME_STEP / n.astype(jnp.float32) for n in counts]
        most = counts[0]
        for n in counts[1:]:
            most = jnp.maximum(most, n)
        turns = jnp.max(most)
        conc, internal = [], []
        for r in rows:
            u = [third_ref[c, r, :] for c in range(NCOMP)]
            rho = ((u[0] + u[1]) + (u[2] + u[3])) + ((u[4] + u[5]) + (u[6] + u[7])) + u[8]
            internal.append(
                u[12] - 0.5 * (u[9] * u[9] + u[10] * u[10] + u[11] * u[11]) / rho)
            conc.append([u[k] * float(GAS[k]) for k in range(9)])

        def advance(index, carry, counts=counts, sizes=sizes, internal=internal):
            new = []
            for k in range(span):
                moved = react(carry[k], internal[k], sizes[k])
                keep = index < counts[k]
                new.append([jnp.where(keep, m, o) for m, o in zip(moved, carry[k])])
            return new

        conc = lax.fori_loop(0, turns, advance, conc)
        for k in range(span):
            for c in range(9):
                made[c, rows[k], :] = conc[k][c] * float(MOLAR[c])
        block = pl.ds(i * span * ROWS, span * ROWS)
        copy = pltpu.make_async_copy(
            made.at[:, block], out_ref.at[pl.ds(0, 9), block], sems.at[i])
        copy.start()
        copies.append(copy)
    for copy in copies:
        copy.wait()


def shape(*dims):
    return jax.ShapeDtypeStruct(dims, jnp.float32)


def call(kernel, out_shape, scratch, n_in, scalars=True):
    vmem = pl.BlockSpec(memory_space=pltpu.VMEM)
    specs = [vmem] * n_in
    if scalars:
        specs[0] = pl.BlockSpec(memory_space=pltpu.SMEM)
    return pl.pallas_call(
        kernel,
        out_shape=out_shape,
        in_specs=specs,
        out_specs=jax.tree.map(lambda _: vmem, out_shape),
        scratch_shapes=[pltpu.VMEM(dims, jnp.float32) for dims in scratch],
        compiler_params=pltpu.CompilerParams(vmem_limit_bytes=16 * 1024 * 1024),
    )


def moved(value, axis, steps):
    count = lax.axis_size(axis)
    pairs = [(i, i + steps) for i in range(count) if 0 <= i + steps < count]
    return lax.ppermute(value, axis, pairs)


def swapped(value, axis, which):
    count = lax.axis_size(axis)
    assert count % 2 == 0
    step = 1 - 2 * which
    return lax.ppermute(
        value, axis, [(i, (i + (step if i % 2 == 0 else -step)) % count) for i in range(count)])


def on_device(state, fresh, substeps, shift):
    comps, planes, width_y, width_z = state.shape
    cross = planes * width_y
    zvecs = width_z // ROWS
    tubes = lax.axis_size("tube")
    tube = lax.axis_index("tube")
    swap = tubes == 2
    x_msgs = 1 if swap else 2
    begins = [jnp.where(tube == 0, planes - HALO, 0), 0] if swap else [0, planes - HALO]
    place = jnp.stack([
        tube.astype(jnp.int32), jnp.int32(tubes), jnp.asarray(begins[0], jnp.int32),
        jnp.asarray(begins[1], jnp.int32), shift.astype(jnp.int32),
        lax.axis_index("gy") % 2, lax.axis_index("gz") % 2])

    full = shape(comps, cross, width_z)
    fullz = shape(comps, width_z + 2 * ROWS, cross)
    xs = shape(comps, HALO * ROWS, width_z)
    ys = shape(comps, HALO * planes, width_z)
    zs = shape(comps, ROWS, cross)
    sent = (full, fullz) + (xs,) * x_msgs + (ys, ys, zs, zs)
    flat = state.reshape(comps, cross, width_z)

    def shifted(reach):
        def branch():
            ahead = moved(flat[:, :reach * width_y], "tube", -1)
            return call(
                functools.partial(assemble_kernel, planes, width_y, width_z, x_msgs),
                sent, [], 4,
            )(place, flat, ahead, fresh)
        return branch

    pieces = SMAX
    size = SMAX // pieces
    start, uz, *msgs = lax.switch(
        (shift.astype(jnp.int32) - 1) // size, [shifted((n + 1) * size) for n in range(pieces)])

    in_x, in_y, in_z = shape(cross, width_z), shape(cross, width_z), shape(
        width_z + 2 * ROWS, cross)
    inner_out = (in_x,) * 3 + (in_y,) * 3 + (in_z,) * 3 + (full, full, shape(comps, width_z, cross))
    al = [((planes + 1) * ROWS, width_z), ((width_y + 1) * planes, width_z),
          ((zvecs + 1) * ROWS, cross)]
    inner_scratch = al + [(3, cross, width_z)]
    outer_scratch = [
        (comps, 2 * HALO * ROWS, width_z), (3, 2 * HALO * ROWS, width_z),
        (3, 2 * HALO * planes, width_z), (3, 2 * ROWS, cross),
        *al, (comps, 2 * HALO * ROWS, width_z), (comps, cross, width_z), (comps, width_z, cross),
        (cross, width_z)]
    current = start
    for stage in (1, 2, 3):
        xmsg, (y0, y1, z0, z1) = msgs[:x_msgs], msgs[x_msgs:]
        y1 = swapped(y1, "gy", 1)
        if swap:
            xlo = xhi = lax.ppermute(xmsg[0], "tube", [(0, 1), (1, 0)])
        else:
            xhi = moved(xmsg[0], "tube", -1)
            xlo = moved(xmsg[1], "tube", 1)
        z1 = swapped(z1, "gz", 1)
        z0 = swapped(z0, "gz", 0)
        y0 = swapped(y0, "gy", 0)
        inner = call(
            functools.partial(inner_kernel, planes, width_y, width_z),
            inner_out, inner_scratch, 2, False)(current, uz)
        current, *rest = call(
            functools.partial(outer_kernel, stage, planes, width_y, width_z, x_msgs),
            (full,) if stage == 3 else sent, outer_scratch, 11 + len(inner_out),
        )(place, current, uz, start, fresh, xlo, xhi, y0, y1, z0, z1, *inner)
        if stage < 3:
            uz, *msgs = rest

    vmem = pl.BlockSpec(memory_space=pltpu.VMEM)
    span = 4
    reacted = pl.pallas_call(
        functools.partial(chemistry_kernel, planes, span),
        out_shape=full,
        in_specs=[vmem, vmem],
        out_specs=pl.BlockSpec(memory_space=pl.ANY),
        scratch_shapes=[pltpu.VMEM((9, cross, width_z), jnp.float32),
                        pltpu.SemaphoreType.DMA((planes // span + 1,))],
        compiler_params=pltpu.CompilerParams(vmem_limit_bytes=16 * 1024 * 1024),
    )(current, substeps.reshape(cross, width_z))
    return reacted.reshape(state.shape)


def solution(mesh):
    return jax.shard_map(
        on_device,
        mesh=mesh,
        in_specs=(P(None, "tube", "gy", "gz"), P(None, "gy", "gz"), P("tube", "gy", "gz"), P()),
        out_specs=P(None, "tube", "gy", "gz"),
        check_vma=False,
    )
```

```python
import functools

import jax
import jax.numpy as jnp
import numpy as np
from jax import lax
from jax.experimental import pallas as pl
from jax.experimental.pallas import tpu as pltpu
from jax.sharding import PartitionSpec as P

SMAX = 12
HALO = 3
NCOMP = 13
ROWS = 8
SCALE = 0.25
TIME_STEP = 0.05
FLUX_FACTOR = -TIME_STEP / (6.0 * SCALE)

MOLAR = np.array([2.016, 31.998, 18.015, 1.008, 15.999, 17.007, 33.006, 34.014, 28.014]) / 18.015
GAS = 1.0 / MOLAR
FORMATION = np.array([0.0, 0.0, -1.5, 12.0, 1.5, 0.25, 0.02, -0.45, 0.0])
REACTANTS = [
    (3, 1), (4, 5), (4, 0), (3, 5), (0, 5), (2, 3), (4, 2), (5, 5), (0, 8), (3, 3, 8), (4, 4, 8),
    (3, 4, 8), (3, 5, 8), (3, 1, 8), (6, 3), (6, 3), (6, 4), (6, 5), (6, 6), (7, 8), (7, 3),
]
PRODUCTS = [
    (4, 5), (3, 1), (3, 5), (4, 0), (2, 3), (0, 5), (5, 5), (4, 2), (3, 3), (0,), (1,),
    (5,), (2,), (6,), (0, 1), (5, 5), (1, 5), (2, 1), (7, 1), (5, 5), (2, 5),
]
PREFACTOR = [
    30.0, 8.0, 20.0, 6.0, 25.0, 10.0, 12.0, 5.0, 4.0, 20.0, 15.0,
    18.0, 22.0, 25.0, 30.0, 25.0, 20.0, 30.0, 10.0, 6.0, 15.0,
]
BARRIER = [
    4.0, 1.0, 3.0, 1.5, 1.5, 4.5, 4.0, 1.5, 6.0, 0.5, 0.5,
    0.5, 0.5, 0.3, 0.8, 0.5, 0.3, 0.3, 0.5, 5.0, 1.5,
]

KAPPA = 0.609375
SPAN = 4
EPS = 3.0 * SCALE * SCALE * 1e-6


def rcp(x):
    return pl.reciprocal(x, approx=True)


def correction(d1, d2, d3, d4):
    k2 = KAPPA * (d2 * d2) + EPS
    k3 = KAPPA * (d3 * d3) + EPS
    xa = d1 - 1.375 * d2
    xb = d3 - 0.625 * d2
    xc = d4 - 1.375 * d3
    ra = rcp(xa * xa + k2)
    rb = rcp(xb * xb + k2)
    rc = rcp(xc * xc + k3)
    wa = ra * ra
    wb = 6.0 * (rb * rb)
    wc = 3.0 * (rc * rc)
    return ((xa + xb) * wa + (0.5 * (d2 + d4) - d3) * wc) * rcp(wa + wb + wc)


def face_flux(du, df, f2, f3, alpha):
    e = [alpha * d for d in du]
    p = [df[k] + e[k] for k in range(4)]
    m = [None] + [df[k] - e[k] for k in range(1, 5)]
    linear = 3.0 * (f2 + f3) - e[2] + 0.5 * (p[1] - m[3])
    return linear - correction(p[0], p[1], p[2], p[3]) + correction(m[4], m[3], m[2], m[1])


def sweep(cells, fluxes, alpha, first, last):
    du, df = {}, {}
    out = {}
    for j in range(first, last + 1):
        for k in range(j, j + 5):
            if k not in du:
                du[k] = cells(k + 1) - cells(k)
                df[k] = fluxes(k + 1) - fluxes(k)
        out[j] = face_flux(
            [du[k] for k in range(j, j + 5)],
            [df[k] for k in range(j, j + 5)],
            fluxes(j + 2),
            fluxes(j + 3),
            alpha(j),
        )
    return out


def memo(load):
    return functools.lru_cache(maxsize=None)(load)


def thermo(u):
    g = [u[k] if GAS[k] == 1.0 else u[k] * float(GAS[k]) for k in range(9)]
    s2 = g[2] + g[6] + g[7]
    s3 = g[3] + g[4]
    gas = (g[0] + g[1]) + (g[5] + g[8]) + (s2 + s3)
    heat = 2.5 * gas + (0.5 * s2 - s3)
    bond = 1.5 * (u[4] - u[2]) + 12.0 * u[3] + 0.25 * u[5] + 0.02 * u[6] - 0.45 * u[7]
    rho = ((u[0] + u[1]) + (u[2] + u[3])) + ((u[4] + u[5]) + (u[6] + u[7])) + u[8]
    back = 1.0 / rho
    cold = 1.0 / heat
    motion = 0.5 * (u[9] * u[9] + u[10] * u[10] + u[11] * u[11]) * back
    temperature = (u[12] - motion - bond) * cold
    pressure = gas * temperature
    sound = jnp.sqrt((1.0 + gas * cold) * pressure * back)
    return back, pressure, sound


def for_components(body):
    together = 3

    def step(i, _):
        for k in range(together):
            c = i * together + k
            body(c, (0, 0, 0), lambda n, c=c: jnp.maximum(c - n, 0))
        return 0

    lax.fori_loop(0, 9 // together, step, 0)
    kinds = [(1, 0, 0), (0, 1, 0), (0, 0, 1), (2, 2, 2)]
    for c in range(9, NCOMP):
        body(c, kinds[c - 9], lambda n, c=c: c - n)


def flux_of(u, speed, pressure, kind):
    if kind == 0:
        return u * speed
    if kind == 1:
        return u * speed + SCALE * pressure()
    return (u + pressure()) * speed


def own_thermo(planes, width_y, u_ref, x_refs, y_refs, z_refs, tmp):
    span = planes // 2

    def own(i, _):
        for k in range(span):
            p = i * span + k
            here = pl.ds(pl.multiple_of(p * ROWS, ROWS), ROWS)
            u = [u_ref[c, here, :] for c in range(NCOMP)]
            back, pressure, sound = thermo(u)
            back, sound = SCALE * back, SCALE * sound
            across = pl.ds(p, width_y, stride=planes)
            for d, where in ((0, here), (1, across), (2, here)):
                speed = u[9 + d] * back
                for n, value in enumerate((speed, pressure, jnp.abs(speed) + sound)):
                    if d == 2:
                        tmp[n, where, :] = value
                    else:
                        (x_refs, y_refs)[d][n][where, :] = value
        return 0

    lax.fori_loop(0, planes // span, own, 0)
    for n in range(3):
        z_refs[n][pl.ds(ROWS, tmp.shape[2]), :] = tmp[n].T


def inner_kernel(
    planes, width_y, width_z, u_ref, uz_ref,
    ux, px, ax, uy, py, ay, uz, pz, az, accx, accy, accz, alx, aly, alz, tmp,
):
    groups = planes // ROWS
    zvecs = width_z // ROWS
    own_thermo(planes, width_y, u_ref, (ux, px, ax), (uy, py, ay), (uz, pz, az), tmp)

    def xvec(ref):
        return lambda i: ref[pl.ds((i - HALO) * ROWS, ROWS), :]

    def yvec(ref, g):
        return lambda i: ref[pl.ds((i - HALO) * planes + g * ROWS, ROWS), :]

    def zvec(ref):
        return lambda i: ref[pl.ds(ROWS - HALO + i, ROWS, stride=zvecs), :]

    largest(xvec(ax), range(HALO, planes - HALO + 1), alx, lambda j: j * ROWS)
    for g in range(groups):
        largest(yvec(ay, g), range(HALO, width_y - HALO + 1), aly,
                lambda j: j * planes + g * ROWS)
    largest(zvec(az), range(HALO, zvecs - HALO + 1), alz, lambda j: j * ROWS)

    def inner(n, cells, speed, pressure, kind, alpha, put):
        cells = memo(cells)
        fluxes = memo(lambda i: flux_of(cells(i), speed(i), lambda: pressure(i), kind))
        out = sweep(cells, fluxes, alpha, HALO, n - HALO)
        put(HALO - 1, out[HALO])
        for i in range(HALO, n - HALO):
            put(i, out[i + 1] - out[i])
        put(n - HALO, out[n - HALO])

    def x_body(c, kind):
        def put(i, value):
            accx[c, pl.ds(i * ROWS, ROWS), :] = value
        inner(planes, lambda i: u_ref[c, pl.ds((i - HALO) * ROWS, ROWS), :], xvec(ux), xvec(px),
              kind, lambda j: alx[pl.ds(j * ROWS, ROWS), :], put)

    def z_body(c, kind):
        def put(i, value):
            accz[c, pl.ds(i, ROWS, stride=zvecs), :] = value
        inner(zvecs, lambda i: uz_ref[c, pl.ds(ROWS - HALO + i, ROWS, stride=zvecs), :],
              zvec(uz), zvec(pz), kind, lambda j: alz[pl.ds(j * ROWS, ROWS), :], put)

    def y_body(c, kind):
        for g in range(groups):
            def put(i, value, g=g):
                accy[c, pl.ds(g * ROWS * width_y + i, ROWS, stride=width_y), :] = value
            def cell(i, g=g):
                return u_ref[c, pl.ds(g * ROWS * width_y + i - HALO, ROWS, stride=width_y), :]
            inner(width_y, cell, yvec(uy, g), yvec(py, g), kind,
                  lambda j: aly[pl.ds(j * planes + g * ROWS, ROWS), :], put)

    def body(c, kinds, before):
        x_body(c, kinds[0])
        z_body(c, kinds[2])
        y_body(c, kinds[1])

    for_components(body)


def largest(speed, faces, ref, place):
    values = memo(speed)
    for j in faces:
        top = values(j)
        for k in range(1, 6):
            top = jnp.maximum(top, values(j + k))
        ref[pl.ds(place(j), ROWS), :] = top


def outer_kernel(
    stage, planes, width_y, width_z, x_msgs, place,
    u_ref, uz_ref, start_ref, fresh_ref, xlo_ref, xhi_ref, y0_ref, y1_ref, z0_ref, z1_ref,
    ux, px, ax, uy, py, ay, uz, pz, az, accx, accy, accz, *refs,
):
    groups = planes // ROWS
    zvecs = width_z // ROWS
    tube, tubes = place[0], place[1]
    last = stage == 3
    refs = list(refs)
    if last:
        counts_ref, out_ref = refs.pop(0), refs.pop(0)
        new_ref, made, sems = refs[-3:]
        refs = refs[:-3]
        turns = trip_counts(planes, SPAN, counts_ref)
    else:
        new_ref = refs.pop(0)
        newz_ref = refs.pop(0)
        xmsg_refs = [refs.pop(0) for _ in range(x_msgs)]
        ymsgs, zmsgs = [refs.pop(0) for _ in range(2)], [refs.pop(0) for _ in range(2)]
    xh, gx, gy, gz, alx, aly, alz, edgex, edgey, edgez, changez = refs

    def lower_y(c, rows):
        return jnp.where(place[5] == 0, y1_ref[c, rows, :], y0_ref[c, rows, :])

    def upper_y(c, rows):
        return jnp.where(place[5] == 0, y0_ref[c, rows, :], y1_ref[c, rows, :])

    def lower_z(c, rows):
        return jnp.where(place[6] == 0, z1_ref[c, rows, :], z0_ref[c, rows, :])

    def upper_z(c, rows):
        return jnp.where(place[6] == 0, z0_ref[c, rows, :], z1_ref[c, rows, :])

    def ghosts(c, _):
        for k in range(HALO):
            here = pl.ds(k * ROWS, ROWS)
            lo = jnp.where(tube == 0, u_ref[c, pl.ds(0, ROWS), :], xlo_ref[c, here, :])
            hi = jnp.where(tube == tubes - 1, fresh_ref[c], xhi_ref[c, here, :])
            xh[c, here, :] = lo
            xh[c, pl.ds((HALO + k) * ROWS, ROWS), :] = hi
        return 0

    lax.fori_loop(0, NCOMP, ghosts, 0)

    def ghost_thermo(u, d, ref, row):
        back, pressure, sound = thermo(u)
        speed = u[9 + d] * (SCALE * back)
        for n, value in enumerate((speed, pressure, jnp.abs(speed) + SCALE * sound)):
            ref[n, pl.ds(row, ROWS), :] = value

    for k in range(2 * HALO):
        ghost_thermo([xh[c, pl.ds(k * ROWS, ROWS), :] for c in range(NCOMP)], 0, gx, k * ROWS)
    for load, offset in ((lower_y, 0), (upper_y, HALO)):
        for k in range(HALO):
            for g in range(groups):
                row = k * planes + g * ROWS
                u = [load(c, pl.ds(row, ROWS)) for c in range(NCOMP)]
                ghost_thermo(u, 1, gy, offset * planes + row)
    ghost_thermo([lower_z(c, pl.ds(0, ROWS)) for c in range(NCOMP)], 2, gz, 0)
    ghost_thermo([upper_z(c, pl.ds(0, ROWS)) for c in range(NCOMP)], 2, gz, ROWS)

    def xvec(ref, n):
        def load(i):
            if HALO <= i < planes + HALO:
                return ref[pl.ds((i - HALO) * ROWS, ROWS), :]
            return gx[n, pl.ds((i if i < HALO else i - planes) * ROWS, ROWS), :]
        return load

    def yvec(ref, n, g):
        def load(i):
            if HALO <= i < width_y + HALO:
                return ref[pl.ds((i - HALO) * planes + g * ROWS, ROWS), :]
            return gy[n, pl.ds((i if i < HALO else i - width_y) * planes + g * ROWS, ROWS), :]
        return load

    row = lax.broadcasted_iota(jnp.int32, (ROWS, planes * width_y), 0)

    def joined(i, load, lo, hi):
        value = load(pl.ds(ROWS - HALO + i, ROWS, stride=zvecs))
        if i < HALO:
            return jnp.where(row == 0, lo(pl.ds(ROWS - HALO + i, 1)), value)
        if i >= zvecs + HALO:
            return jnp.where(row == ROWS - 1, hi(pl.ds(i - zvecs - HALO, 1)), value)
        return value

    def zvec(ref, n):
        def load(i):
            return joined(i, lambda s: ref[s, :], lambda s: gz[n, s, :],
                          lambda s: gz[n, pl.ds(ROWS + s.start, 1), :])
        return load

    def ends(n):
        return list(range(HALO)) + list(range(n - HALO + 1, n + 1))

    largest(xvec(ax, 2), ends(planes), alx, lambda j: j * ROWS)
    for g in range(groups):
        largest(yvec(ay, 2, g), ends(width_y), aly, lambda j: j * planes + g * ROWS)
    largest(zvec(az, 2), ends(zvecs), alz, lambda j: j * ROWS)

    def outer(n, cells, speed, pressure, kind, alpha, given, put):
        cells = memo(cells)
        fluxes = memo(lambda i: flux_of(cells(i), speed(i), lambda: pressure(i), kind))
        out = sweep(cells, fluxes, alpha, 0, HALO - 1)
        out[HALO] = given(HALO - 1)
        for i in range(HALO):
            put(i, out[i + 1] - out[i])
        out = sweep(cells, fluxes, alpha, n - HALO + 1, n)
        out[n - HALO] = given(n - HALO)
        for i in range(n - HALO, n):
            put(i, out[i + 1] - out[i])

    def between(n, rows, width):
        position = lax.broadcasted_iota(jnp.int32, (rows, width), 0) % n
        return (position >= HALO) & (position < n - HALO)

    inside_y = between(width_y, ROWS, width_z)
    inside_z = between(zvecs, width_z, planes * width_y)

    def z_body(c, kind):
        def cell(i):
            return joined(i, lambda s: uz_ref[c, s, :], lambda s: lower_z(c, s),
                          lambda s: upper_z(c, s))
        def put(i, value):
            edgez[c, pl.ds(i, ROWS, stride=zvecs), :] = value
        outer(zvecs, cell, zvec(uz, 0), zvec(pz, 1), kind,
              lambda j: alz[pl.ds(j * ROWS, ROWS), :],
              lambda i: accz[c, pl.ds(i, ROWS, stride=zvecs), :], put)

    def x_body(c, kind):
        def cell(i):
            if HALO <= i < planes + HALO:
                return u_ref[c, pl.ds((i - HALO) * ROWS, ROWS), :]
            return xh[c, pl.ds((i if i < HALO else i - planes) * ROWS, ROWS), :]
        def put(i, value):
            edgex[c, pl.ds((i if i < HALO else i - planes + 2 * HALO) * ROWS, ROWS), :] = value
        outer(planes, cell, xvec(ux, 0), xvec(px, 1), kind,
              lambda j: alx[pl.ds(j * ROWS, ROWS), :],
              lambda i: accx[c, pl.ds(i * ROWS, ROWS), :], put)

    def update(c):
        changez[...] = jnp.where(inside_z, accz[c], edgez[c]).T
        for p in range(planes):
            here = pl.ds(p * ROWS, ROWS)
            change = changez[here, :] + jnp.where(inside_y, accy[c, here, :], edgey[c, here, :])
            if HALO <= p < planes - HALO:
                change = change + accx[c, here, :]
            else:
                k = p if p < HALO else p - planes + 2 * HALO
                change = change + edgex[c, pl.ds(k * ROWS, ROWS), :]
            value = u_ref[c, here, :] + FLUX_FACTOR * change
            if stage == 2:
                value = 0.75 * start_ref[c, here, :] + 0.25 * value
            elif stage == 3:
                value = (1.0 / 3.0) * start_ref[c, here, :] + (2.0 / 3.0) * value
            new_ref[c, here, :] = value

    def pass_on(c):
        if not last:
            newz_ref[c, pl.ds(ROWS, width_z), :] = new_ref[c].T
            messages(c, planes, width_y, width_z, place, new_ref, newz_ref, xmsg_refs,
                     ymsgs, zmsgs)

    def y_body(c, kind):
        for g in range(groups):
            base = g * ROWS * width_y
            def cell(i, g=g, base=base):
                if HALO <= i < width_y + HALO:
                    return u_ref[c, pl.ds(base + i - HALO, ROWS, stride=width_y), :]
                if i < HALO:
                    return lower_y(c, pl.ds(i * planes + g * ROWS, ROWS))
                return upper_y(c, pl.ds((i - HALO - width_y) * planes + g * ROWS, ROWS))
            def put(i, value, base=base):
                edgey[c, pl.ds(base + i, ROWS, stride=width_y), :] = value
            outer(width_y, cell, yvec(uy, 0, g), yvec(py, 1, g), kind,
                  lambda j: aly[pl.ds(j * planes + g * ROWS, ROWS), :],
                  lambda i: accy[c, pl.ds(base + i, ROWS, stride=width_y), :], put)

    def body(c, kinds, before):
        pass_on(before(2))
        update(before(1))
        z_body(c, kinds[2])
        x_body(c, kinds[0])
        y_body(c, kinds[1])

    for_components(body)
    pass_on(NCOMP - 2)
    update(NCOMP - 1)
    pass_on(NCOMP - 1)
    if last:
        chemistry(planes, SPAN, turns, new_ref, counts_ref, out_ref, made, sems)


def messages(c, planes, width_y, width_z, place, u_ref, uz_ref, xmsg_refs, ymsgs, zmsgs):
    for n, ref in enumerate(xmsg_refs):
        begin = place[2 + n]
        for k in range(HALO):
            rows = pl.ds(pl.multiple_of((begin + k) * ROWS, ROWS), ROWS)
            ref[c, pl.ds(k * ROWS, ROWS), :] = u_ref[c, rows, :]
    for n in range(2):
        upper = place[5] == n
        for k in range(HALO):
            for g in range(planes // ROWS):
                base = g * ROWS * width_y + k
                low = u_ref[c, pl.ds(base, ROWS, stride=width_y), :]
                high = u_ref[c, pl.ds(base + width_y - HALO, ROWS, stride=width_y), :]
                ymsgs[n][c, pl.ds(k * planes + g * ROWS, ROWS), :] = jnp.where(upper, high, low)
        begin = pl.multiple_of(jnp.where(place[6] == n, width_z, ROWS), ROWS)
        zmsgs[n][c] = uz_ref[c, pl.ds(begin, ROWS), :]


def assemble_kernel(
    planes, width_y, width_z, x_msgs, place, state_ref, ahead_ref, fresh_ref, u_ref, uz_ref, *refs,
):
    refs = list(refs)
    xmsg_refs = [refs.pop(0) for _ in range(x_msgs)]
    ymsgs, zmsgs = refs[:2], refs[2:]
    tube, tubes, shift = place[0], place[1], place[4]
    reach = ahead_ref.shape[1] // ROWS

    def pass_on(c):
        uz_ref[c, pl.ds(ROWS, width_z), :] = u_ref[c].T
        messages(c, planes, width_y, width_z, place, u_ref, uz_ref, xmsg_refs,
                 ymsgs, zmsgs)

    for c in range(NCOMP):
        if c:
            pass_on(c - 1)
        fresh = fresh_ref[c]
        for i in range(planes):
            source = shift + i
            own = jnp.minimum(source, planes - 1)
            value = state_ref[c, pl.ds(pl.multiple_of(own * ROWS, ROWS), ROWS), :]
            if i >= planes - reach:
                beyond = jnp.clip(source - planes, 0, reach - 1)
                other = ahead_ref[c, pl.ds(pl.multiple_of(beyond * ROWS, ROWS), ROWS), :]
                other = jnp.where(tube == tubes - 1, fresh, other)
                value = jnp.where(source >= planes, other, value)
            u_ref[c, pl.ds(i * ROWS, ROWS), :] = value
    pass_on(NCOMP - 1)


def powers_of(back):
    a = jnp.exp(-0.5 * back)
    b = jnp.exp(-0.3 * back)
    a2 = a * a
    a3 = a2 * a
    a4 = a2 * a2
    a6 = a3 * a3
    a8 = a4 * a4
    return {0.5: a, 0.3: b, 1.0: a2, 1.5: a3, 3.0: a6, 4.0: a8, 4.5: a8 * a, 5.0: a8 * a2,
            6.0: a6 * a6, 0.8: a * b}


def react(conc, internal, size):
    s2 = conc[2] + conc[6] + conc[7]
    s3 = conc[3] + conc[4]
    heat = 2.5 * (((conc[0] + conc[1]) + (conc[5] + conc[8])) + (s2 + s3)) + (0.5 * s2 - s3)
    bond = None
    for k in range(9):
        if FORMATION[k]:
            term = float(FORMATION[k] * MOLAR[k]) * conc[k]
            bond = term if bond is None else bond + term
    boltzmann = powers_of(heat / (internal - bond))
    pairs = {}
    omega = [None] * 9

    def add(k, value):
        omega[k] = value if omega[k] is None else omega[k] + value

    def sub(k, value):
        omega[k] = -value if omega[k] is None else omega[k] - value

    def rate(j):
        names = REACTANTS[j]
        key = tuple(sorted(names))
        if key not in pairs:
            value = conc[names[0]] * conc[names[1]]
            if len(names) == 3:
                base = tuple(sorted(names[:2]))
                if base not in pairs:
                    pairs[base] = value
                value = pairs[base] * conc[8]
            pairs[key] = value
        return (PREFACTOR[j] * boltzmann[BARRIER[j]]) * pairs[key]

    j = 0
    while j < len(REACTANTS):
        value = rate(j)
        back = j + 1 < len(REACTANTS) and REACTANTS[j + 1] == PRODUCTS[j] \
            and PRODUCTS[j + 1] == REACTANTS[j]
        if back:
            value = value - rate(j + 1)
        for k in range(9):
            times = PRODUCTS[j].count(k) - REACTANTS[j].count(k)
            if times == 0:
                continue
            amount = value if abs(times) == 1 else value + value
            if times > 0:
                add(k, amount)
            else:
                sub(k, amount)
        j += 2 if back else 1
    return [conc[k] + size * omega[k] for k in range(9)]


def trip_counts(planes, span, counts_ref):
    most = []
    for i in range(planes // span):
        top = counts_ref[pl.ds(i * span * ROWS, ROWS), :]
        for k in range(1, span):
            top = jnp.maximum(top, counts_ref[pl.ds((i * span + k) * ROWS, ROWS), :])
        most.append(jnp.max(top))
    return most


def chemistry(planes, span, turns, third_ref, counts_ref, out_ref, made, sems):
    blocks = planes // span
    kept = pltpu.make_async_copy(
        third_ref.at[pl.ds(9, NCOMP - 9)], out_ref.at[pl.ds(9, NCOMP - 9)], sems.at[blocks])
    kept.start()
    copies = [kept]
    for i in reversed(range(blocks)):
        rows = [pl.ds((i * span + k) * ROWS, ROWS) for k in range(span)]
        counts = [counts_ref[r, :] for r in rows]
        sizes = [TIME_STEP / n.astype(jnp.float32) for n in counts]
        conc, internal = [], []
        for r in rows:
            u = [third_ref[c, r, :] for c in range(NCOMP)]
            rho = ((u[0] + u[1]) + (u[2] + u[3])) + ((u[4] + u[5]) + (u[6] + u[7])) + u[8]
            internal.append(
                u[12] - 0.5 * (u[9] * u[9] + u[10] * u[10] + u[11] * u[11]) / rho)
            conc.append([u[k] * float(GAS[k]) for k in range(9)])

        def advance(index, carry, counts=counts, sizes=sizes, internal=internal):
            new = []
            for k in range(span):
                moved = react(carry[k], internal[k], sizes[k])
                keep = index < counts[k]
                new.append([jnp.where(keep, m, o) for m, o in zip(moved, carry[k])])
            return new

        conc = lax.fori_loop(0, turns[i], advance, conc)
        for k in range(span):
            for c in range(9):
                made[c, rows[k], :] = conc[k][c] * float(MOLAR[c])
        block = pl.ds(i * span * ROWS, span * ROWS)
        copy = pltpu.make_async_copy(
            made.at[:, block], out_ref.at[pl.ds(0, 9), block], sems.at[i])
        copy.start()
        copies.append(copy)
    for copy in copies:
        copy.wait()


def shape(*dims):
    return jax.ShapeDtypeStruct(dims, jnp.float32)


def call(kernel, out_shape, scratch, n_in, scalars=True, far=False):
    vmem = pl.BlockSpec(memory_space=pltpu.VMEM)
    specs = [vmem] * n_in
    if scalars:
        specs[0] = pl.BlockSpec(memory_space=pltpu.SMEM)
    out = pl.BlockSpec(memory_space=pl.ANY) if far else vmem
    return pl.pallas_call(
        kernel,
        out_shape=out_shape,
        in_specs=specs,
        out_specs=jax.tree.map(lambda _: out, out_shape),
        scratch_shapes=[
            pltpu.VMEM(s, jnp.float32) if isinstance(s, tuple) else s for s in scratch],
        compiler_params=pltpu.CompilerParams(vmem_limit_bytes=16 * 1024 * 1024),
    )


def moved(value, axis, steps):
    count = lax.axis_size(axis)
    pairs = [(i, i + steps) for i in range(count) if 0 <= i + steps < count]
    return lax.ppermute(value, axis, pairs)


def swapped(value, axis, which):
    count = lax.axis_size(axis)
    assert count % 2 == 0
    step = 1 - 2 * which
    return lax.ppermute(
        value, axis, [(i, (i + (step if i % 2 == 0 else -step)) % count) for i in range(count)])


def on_device(state, fresh, substeps, shift):
    comps, planes, width_y, width_z = state.shape
    cross = planes * width_y
    zvecs = width_z // ROWS
    tubes = lax.axis_size("tube")
    tube = lax.axis_index("tube")
    swap = tubes == 2
    x_msgs = 1 if swap else 2
    begins = [jnp.where(tube == 0, planes - HALO, 0), 0] if swap else [0, planes - HALO]
    place = jnp.stack([
        tube.astype(jnp.int32), jnp.int32(tubes), jnp.asarray(begins[0], jnp.int32),
        jnp.asarray(begins[1], jnp.int32), shift.astype(jnp.int32),
        lax.axis_index("gy") % 2, lax.axis_index("gz") % 2])

    full = shape(comps, cross, width_z)
    fullz = shape(comps, width_z + 2 * ROWS, cross)
    xs = shape(comps, HALO * ROWS, width_z)
    ys = shape(comps, HALO * planes, width_z)
    zs = shape(comps, ROWS, cross)
    sent = (full, fullz) + (xs,) * x_msgs + (ys, ys, zs, zs)
    flat = state.reshape(comps, cross, width_z)

    def shifted(reach):
        def branch():
            ahead = moved(flat[:, :reach * width_y], "tube", -1)
            return call(
                functools.partial(assemble_kernel, planes, width_y, width_z, x_msgs),
                sent, [], 4,
            )(place, flat, ahead, fresh)
        return branch

    pieces = SMAX
    size = SMAX // pieces
    start, uz, *msgs = lax.switch(
        (shift.astype(jnp.int32) - 1) // size, [shifted((n + 1) * size) for n in range(pieces)])

    in_x, in_y, in_z = shape(cross, width_z), shape(cross, width_z), shape(
        width_z + 2 * ROWS, cross)
    inner_out = (in_x,) * 3 + (in_y,) * 3 + (in_z,) * 3 + (full, full, shape(comps, width_z, cross))
    al = [((planes + 1) * ROWS, width_z), ((width_y + 1) * planes, width_z),
          ((zvecs + 1) * ROWS, cross)]
    inner_scratch = al + [(3, cross, width_z)]
    outer_scratch = [
        (comps, 2 * HALO * ROWS, width_z), (3, 2 * HALO * ROWS, width_z),
        (3, 2 * HALO * planes, width_z), (3, 2 * ROWS, cross),
        *al, (comps, 2 * HALO * ROWS, width_z), (comps, cross, width_z), (comps, width_z, cross),
        (cross, width_z)]
    current = start
    for stage in (1, 2, 3):
        xmsg, (y0, y1, z0, z1) = msgs[:x_msgs], msgs[x_msgs:]
        y1 = swapped(y1, "gy", 1)
        if swap:
            xlo = xhi = lax.ppermute(xmsg[0], "tube", [(0, 1), (1, 0)])
        else:
            xhi = moved(xmsg[0], "tube", -1)
            xlo = moved(xmsg[1], "tube", 1)
        z1 = swapped(z1, "gz", 1)
        z0 = swapped(z0, "gz", 0)
        y0 = swapped(y0, "gy", 0)
        inner = call(
            functools.partial(inner_kernel, planes, width_y, width_z),
            inner_out, inner_scratch, 2, False)(current, uz)
        last = stage == 3
        tail = (substeps.reshape(cross, width_z),) if last else ()
        far = [full.shape, (9, cross, width_z), pltpu.SemaphoreType.DMA((planes // SPAN + 1,))]
        current, *rest = call(
            functools.partial(outer_kernel, stage, planes, width_y, width_z, x_msgs),
            (full,) if last else sent, outer_scratch + far if last else outer_scratch,
            11 + len(inner_out) + len(tail), far=last,
        )(place, current, uz, start, fresh, xlo, xhi, y0, y1, z0, z1, *inner, *tail)
        if stage < 3:
            uz, *msgs = rest

    return current.reshape(state.shape)


def solution(mesh):
    return jax.shard_map(
        on_device,
        mesh=mesh,
        in_specs=(P(None, "tube", "gy", "gz"), P(None, "gy", "gz"), P("tube", "gy", "gz"), P()),
        out_specs=P(None, "tube", "gy", "gz"),
        check_vma=False,
    )
```

```python
import functools

import jax
import jax.numpy as jnp
import numpy as np
from jax import lax
from jax.experimental import pallas as pl
from jax.experimental.pallas import tpu as pltpu
from jax.sharding import PartitionSpec as P

SMAX = 12
HALO = 3
NCOMP = 13
ROWS = 8
SCALE = 0.25
TIME_STEP = 0.05
FLUX_FACTOR = -TIME_STEP / (6.0 * SCALE)

MOLAR = np.array([2.016, 31.998, 18.015, 1.008, 15.999, 17.007, 33.006, 34.014, 28.014]) / 18.015
GAS = 1.0 / MOLAR
FORMATION = np.array([0.0, 0.0, -1.5, 12.0, 1.5, 0.25, 0.02, -0.45, 0.0])
REACTANTS = [
    (3, 1), (4, 5), (4, 0), (3, 5), (0, 5), (2, 3), (4, 2), (5, 5), (0, 8), (3, 3, 8), (4, 4, 8),
    (3, 4, 8), (3, 5, 8), (3, 1, 8), (6, 3), (6, 3), (6, 4), (6, 5), (6, 6), (7, 8), (7, 3),
]
PRODUCTS = [
    (4, 5), (3, 1), (3, 5), (4, 0), (2, 3), (0, 5), (5, 5), (4, 2), (3, 3), (0,), (1,),
    (5,), (2,), (6,), (0, 1), (5, 5), (1, 5), (2, 1), (7, 1), (5, 5), (2, 5),
]
PREFACTOR = [
    30.0, 8.0, 20.0, 6.0, 25.0, 10.0, 12.0, 5.0, 4.0, 20.0, 15.0,
    18.0, 22.0, 25.0, 30.0, 25.0, 20.0, 30.0, 10.0, 6.0, 15.0,
]
BARRIER = [
    4.0, 1.0, 3.0, 1.5, 1.5, 4.5, 4.0, 1.5, 6.0, 0.5, 0.5,
    0.5, 0.5, 0.3, 0.8, 0.5, 0.3, 0.3, 0.5, 5.0, 1.5,
]

KAPPA = 0.609375
SPAN = 4
EPS = 3.0 * SCALE * SCALE * 1e-6


def rcp(x):
    return pl.reciprocal(x, approx=True)


def correction(d1, d2, d3, d4):
    k2 = KAPPA * (d2 * d2) + EPS
    k3 = KAPPA * (d3 * d3) + EPS
    xa = d1 - 1.375 * d2
    xb = d3 - 0.625 * d2
    xc = d4 - 1.375 * d3
    ra = rcp(xa * xa + k2)
    rb = rcp(xb * xb + k2)
    rc = rcp(xc * xc + k3)
    wa = ra * ra
    wb = 6.0 * (rb * rb)
    wc = 3.0 * (rc * rc)
    return ((xa + xb) * wa + (0.5 * (d2 + d4) - d3) * wc) * rcp(wa + wb + wc)


def face_flux(du, df, f2, f3, alpha):
    e = [alpha * d for d in du]
    p = [df[k] + e[k] for k in range(4)]
    m = [None] + [df[k] - e[k] for k in range(1, 5)]
    linear = 3.0 * (f2 + f3) - e[2] + 0.5 * (p[1] - m[3])
    return linear - correction(p[0], p[1], p[2], p[3]) + correction(m[4], m[3], m[2], m[1])


def sweep(cells, fluxes, alpha, first, last):
    du, df = {}, {}
    out = {}
    for j in range(first, last + 1):
        for k in range(j, j + 5):
            if k not in du:
                du[k] = cells(k + 1) - cells(k)
                df[k] = fluxes(k + 1) - fluxes(k)
        out[j] = face_flux(
            [du[k] for k in range(j, j + 5)],
            [df[k] for k in range(j, j + 5)],
            fluxes(j + 2),
            fluxes(j + 3),
            alpha(j),
        )
    return out


def memo(load):
    return functools.lru_cache(maxsize=None)(load)


def thermo(u):
    g = [u[k] if GAS[k] == 1.0 else u[k] * float(GAS[k]) for k in range(9)]
    s2 = g[2] + g[6] + g[7]
    s3 = g[3] + g[4]
    gas = (g[0] + g[1]) + (g[5] + g[8]) + (s2 + s3)
    heat = 2.5 * gas + (0.5 * s2 - s3)
    bond = 1.5 * (u[4] - u[2]) + 12.0 * u[3] + 0.25 * u[5] + 0.02 * u[6] - 0.45 * u[7]
    rho = ((u[0] + u[1]) + (u[2] + u[3])) + ((u[4] + u[5]) + (u[6] + u[7])) + u[8]
    back = 1.0 / rho
    cold = 1.0 / heat
    motion = 0.5 * (u[9] * u[9] + u[10] * u[10] + u[11] * u[11]) * back
    temperature = (u[12] - motion - bond) * cold
    pressure = gas * temperature
    sound = jnp.sqrt((1.0 + gas * cold) * pressure * back)
    return back, pressure, sound


def for_components(body):
    together = 3

    def step(i, _):
        for k in range(together):
            c = i * together + k
            body(c, (0, 0, 0), lambda n, c=c: jnp.maximum(c - n, 0))
        return 0

    lax.fori_loop(0, 9 // together, step, 0)
    kinds = [(1, 0, 0), (0, 1, 0), (0, 0, 1), (2, 2, 2)]
    for c in range(9, NCOMP):
        body(c, kinds[c - 9], lambda n, c=c: c - n)


def flux_of(u, speed, pressure, kind):
    if kind == 0:
        return u * speed
    if kind == 1:
        return u * speed + SCALE * pressure()
    return (u + pressure()) * speed


def own_thermo(planes, width_y, u_ref, x_refs, y_refs, z_refs, tmp):
    span = planes // 2

    def own(i, _):
        for k in range(span):
            p = i * span + k
            here = pl.ds(pl.multiple_of(p * ROWS, ROWS), ROWS)
            u = [u_ref[c, here, :] for c in range(NCOMP)]
            back, pressure, sound = thermo(u)
            back, sound = SCALE * back, SCALE * sound
            across = pl.ds(p, width_y, stride=planes)
            for d, where in ((0, here), (1, across), (2, here)):
                speed = u[9 + d] * back
                for n, value in enumerate((speed, pressure, jnp.abs(speed) + sound)):
                    if d == 2:
                        tmp[n, where, :] = value
                    else:
                        (x_refs, y_refs)[d][n][where, :] = value
        return 0

    lax.fori_loop(0, planes // span, own, 0)
    for n in range(3):
        z_refs[n][pl.ds(ROWS, tmp.shape[2]), :] = tmp[n].T


def inner_kernel(
    planes, width_y, width_z, u_ref, uz_ref,
    ux, px, ax, uy, py, ay, uz, pz, az, accx, accy, accz, alx, aly, alz, tmp,
):
    groups = planes // ROWS
    zvecs = width_z // ROWS
    own_thermo(planes, width_y, u_ref, (ux, px, ax), (uy, py, ay), (uz, pz, az), tmp)

    def xvec(ref):
        return lambda i: ref[pl.ds((i - HALO) * ROWS, ROWS), :]

    def yvec(ref, g):
        return lambda i: ref[pl.ds((i - HALO) * planes + g * ROWS, ROWS), :]

    def zvec(ref):
        return lambda i: ref[pl.ds(ROWS - HALO + i, ROWS, stride=zvecs), :]

    largest(xvec(ax), range(HALO, planes - HALO + 1), alx, lambda j: j * ROWS)
    for g in range(groups):
        largest(yvec(ay, g), range(HALO, width_y - HALO + 1), aly,
                lambda j: j * planes + g * ROWS)
    largest(zvec(az), range(HALO, zvecs - HALO + 1), alz, lambda j: j * ROWS)

    def inner(n, cells, speed, pressure, kind, alpha, put):
        cells = memo(cells)
        fluxes = memo(lambda i: flux_of(cells(i), speed(i), lambda: pressure(i), kind))
        out = sweep(cells, fluxes, alpha, HALO, n - HALO)
        put(HALO - 1, out[HALO])
        for i in range(HALO, n - HALO):
            put(i, out[i + 1] - out[i])
        put(n - HALO, out[n - HALO])

    def x_body(c, kind):
        def put(i, value):
            accx[c, pl.ds(i * ROWS, ROWS), :] = value
        inner(planes, lambda i: u_ref[c, pl.ds((i - HALO) * ROWS, ROWS), :], xvec(ux), xvec(px),
              kind, lambda j: alx[pl.ds(j * ROWS, ROWS), :], put)

    def z_body(c, kind):
        def put(i, value):
            accz[c, pl.ds(i, ROWS, stride=zvecs), :] = value
        inner(zvecs, lambda i: uz_ref[c, pl.ds(ROWS - HALO + i, ROWS, stride=zvecs), :],
              zvec(uz), zvec(pz), kind, lambda j: alz[pl.ds(j * ROWS, ROWS), :], put)

    def y_body(c, kind):
        for g in range(groups):
            def put(i, value, g=g):
                accy[c, pl.ds(g * ROWS * width_y + i, ROWS, stride=width_y), :] = value
            def cell(i, g=g):
                return u_ref[c, pl.ds(g * ROWS * width_y + i - HALO, ROWS, stride=width_y), :]
            inner(width_y, cell, yvec(uy, g), yvec(py, g), kind,
                  lambda j: aly[pl.ds(j * planes + g * ROWS, ROWS), :], put)

    def body(c, kinds, before):
        x_body(c, kinds[0])
        z_body(c, kinds[2])
        y_body(c, kinds[1])

    for_components(body)


def largest(speed, faces, ref, place):
    values = memo(speed)
    for j in faces:
        top = values(j)
        for k in range(1, 6):
            top = jnp.maximum(top, values(j + k))
        ref[pl.ds(place(j), ROWS), :] = top


def outer_kernel(
    stage, planes, width_y, width_z, x_msgs, place,
    u_ref, uz_ref, start_ref, fresh_ref, xlo_ref, xhi_ref, y0_ref, y1_ref, z0_ref, z1_ref,
    ux, px, ax, uy, py, ay, uz, pz, az, accx, accy, accz, *refs,
):
    groups = planes // ROWS
    zvecs = width_z // ROWS
    tube, tubes = place[0], place[1]
    last = stage == 3
    refs = list(refs)
    if last:
        counts_ref, out_ref = refs.pop(0), refs.pop(0)
        new_ref, made, sems = refs[-3:]
        refs = refs[:-3]
        turns = trip_counts(planes, SPAN, counts_ref)
    else:
        new_ref = refs.pop(0)
        newz_ref = refs.pop(0)
        xmsg_refs = [refs.pop(0) for _ in range(x_msgs)]
        ymsgs, zmsgs = [refs.pop(0) for _ in range(2)], [refs.pop(0) for _ in range(2)]
    xh, gx, gy, gz, alx, aly, alz, edgex, edgey, edgez, changez = refs

    def lower_y(c, rows):
        return jnp.where(place[5] == 0, y1_ref[c, rows, :], y0_ref[c, rows, :])

    def upper_y(c, rows):
        return jnp.where(place[5] == 0, y0_ref[c, rows, :], y1_ref[c, rows, :])

    def lower_z(c, rows):
        return jnp.where(place[6] == 0, z1_ref[c, rows, :], z0_ref[c, rows, :])

    def upper_z(c, rows):
        return jnp.where(place[6] == 0, z0_ref[c, rows, :], z1_ref[c, rows, :])

    def ghosts(c, _):
        for k in range(HALO):
            here = pl.ds(k * ROWS, ROWS)
            lo = jnp.where(tube == 0, u_ref[c, pl.ds(0, ROWS), :], xlo_ref[c, here, :])
            hi = jnp.where(tube == tubes - 1, fresh_ref[c], xhi_ref[c, here, :])
            xh[c, here, :] = lo
            xh[c, pl.ds((HALO + k) * ROWS, ROWS), :] = hi
        return 0

    lax.fori_loop(0, NCOMP, ghosts, 0)

    def ghost_thermo(u, d, ref, row):
        back, pressure, sound = thermo(u)
        speed = u[9 + d] * (SCALE * back)
        for n, value in enumerate((speed, pressure, jnp.abs(speed) + SCALE * sound)):
            ref[n, pl.ds(row, ROWS), :] = value

    for k in range(2 * HALO):
        ghost_thermo([xh[c, pl.ds(k * ROWS, ROWS), :] for c in range(NCOMP)], 0, gx, k * ROWS)
    for load, offset in ((lower_y, 0), (upper_y, HALO)):
        for k in range(HALO):
            for g in range(groups):
                row = k * planes + g * ROWS
                u = [load(c, pl.ds(row, ROWS)) for c in range(NCOMP)]
                ghost_thermo(u, 1, gy, offset * planes + row)
    ghost_thermo([lower_z(c, pl.ds(0, ROWS)) for c in range(NCOMP)], 2, gz, 0)
    ghost_thermo([upper_z(c, pl.ds(0, ROWS)) for c in range(NCOMP)], 2, gz, ROWS)

    def xvec(ref, n):
        def load(i):
            if HALO <= i < planes + HALO:
                return ref[pl.ds((i - HALO) * ROWS, ROWS), :]
            return gx[n, pl.ds((i if i < HALO else i - planes) * ROWS, ROWS), :]
        return load

    def yvec(ref, n, g):
        def load(i):
            if HALO <= i < width_y + HALO:
                return ref[pl.ds((i - HALO) * planes + g * ROWS, ROWS), :]
            return gy[n, pl.ds((i if i < HALO else i - width_y) * planes + g * ROWS, ROWS), :]
        return load

    row = lax.broadcasted_iota(jnp.int32, (ROWS, planes * width_y), 0)

    def joined(i, load, lo, hi):
        value = load(pl.ds(ROWS - HALO + i, ROWS, stride=zvecs))
        if i < HALO:
            return jnp.where(row == 0, lo(pl.ds(ROWS - HALO + i, 1)), value)
        if i >= zvecs + HALO:
            return jnp.where(row == ROWS - 1, hi(pl.ds(i - zvecs - HALO, 1)), value)
        return value

    def zvec(ref, n):
        def load(i):
            return joined(i, lambda s: ref[s, :], lambda s: gz[n, s, :],
                          lambda s: gz[n, pl.ds(ROWS + s.start, 1), :])
        return load

    def ends(n):
        return list(range(HALO)) + list(range(n - HALO + 1, n + 1))

    largest(xvec(ax, 2), ends(planes), alx, lambda j: j * ROWS)
    for g in range(groups):
        largest(yvec(ay, 2, g), ends(width_y), aly, lambda j: j * planes + g * ROWS)
    largest(zvec(az, 2), ends(zvecs), alz, lambda j: j * ROWS)

    def outer(n, cells, speed, pressure, kind, alpha, given, put):
        cells = memo(cells)
        fluxes = memo(lambda i: flux_of(cells(i), speed(i), lambda: pressure(i), kind))
        out = sweep(cells, fluxes, alpha, 0, HALO - 1)
        out[HALO] = given(HALO - 1)
        for i in range(HALO):
            put(i, out[i + 1] - out[i])
        out = sweep(cells, fluxes, alpha, n - HALO + 1, n)
        out[n - HALO] = given(n - HALO)
        for i in range(n - HALO, n):
            put(i, out[i + 1] - out[i])

    def between(n, rows, width):
        position = lax.broadcasted_iota(jnp.int32, (rows, width), 0) % n
        return (position >= HALO) & (position < n - HALO)

    inside_y = between(width_y, ROWS, width_z)
    inside_z = between(zvecs, width_z, planes * width_y)

    def z_body(c, kind):
        def cell(i):
            return joined(i, lambda s: uz_ref[c, s, :], lambda s: lower_z(c, s),
                          lambda s: upper_z(c, s))
        def put(i, value):
            edgez[c, pl.ds(i, ROWS, stride=zvecs), :] = value
        outer(zvecs, cell, zvec(uz, 0), zvec(pz, 1), kind,
              lambda j: alz[pl.ds(j * ROWS, ROWS), :],
              lambda i: accz[c, pl.ds(i, ROWS, stride=zvecs), :], put)

    def x_body(c, kind):
        def cell(i):
            if HALO <= i < planes + HALO:
                return u_ref[c, pl.ds((i - HALO) * ROWS, ROWS), :]
            return xh[c, pl.ds((i if i < HALO else i - planes) * ROWS, ROWS), :]
        def put(i, value):
            edgex[c, pl.ds((i if i < HALO else i - planes + 2 * HALO) * ROWS, ROWS), :] = value
        outer(planes, cell, xvec(ux, 0), xvec(px, 1), kind,
              lambda j: alx[pl.ds(j * ROWS, ROWS), :],
              lambda i: accx[c, pl.ds(i * ROWS, ROWS), :], put)

    def update(c):
        changez[...] = jnp.where(inside_z, accz[c], edgez[c]).T
        for p in range(planes):
            here = pl.ds(p * ROWS, ROWS)
            change = changez[here, :] + jnp.where(inside_y, accy[c, here, :], edgey[c, here, :])
            if HALO <= p < planes - HALO:
                change = change + accx[c, here, :]
            else:
                k = p if p < HALO else p - planes + 2 * HALO
                change = change + edgex[c, pl.ds(k * ROWS, ROWS), :]
            value = u_ref[c, here, :] + FLUX_FACTOR * change
            if stage == 2:
                value = 0.75 * start_ref[c, here, :] + 0.25 * value
            elif stage == 3:
                value = (1.0 / 3.0) * start_ref[c, here, :] + (2.0 / 3.0) * value
            new_ref[c, here, :] = value

    def pass_on(c):
        if not last:
            newz_ref[c, pl.ds(ROWS, width_z), :] = new_ref[c].T
            messages(c, planes, width_y, width_z, place, new_ref, newz_ref, xmsg_refs,
                     ymsgs, zmsgs)

    def y_body(c, kind):
        for g in range(groups):
            base = g * ROWS * width_y
            def cell(i, g=g, base=base):
                if HALO <= i < width_y + HALO:
                    return u_ref[c, pl.ds(base + i - HALO, ROWS, stride=width_y), :]
                if i < HALO:
                    return lower_y(c, pl.ds(i * planes + g * ROWS, ROWS))
                return upper_y(c, pl.ds((i - HALO - width_y) * planes + g * ROWS, ROWS))
            def put(i, value, base=base):
                edgey[c, pl.ds(base + i, ROWS, stride=width_y), :] = value
            outer(width_y, cell, yvec(uy, 0, g), yvec(py, 1, g), kind,
                  lambda j: aly[pl.ds(j * planes + g * ROWS, ROWS), :],
                  lambda i: accy[c, pl.ds(base + i, ROWS, stride=width_y), :], put)

    def body(c, kinds, before):
        pass_on(before(2))
        update(before(1))
        z_body(c, kinds[2])
        x_body(c, kinds[0])
        y_body(c, kinds[1])

    for_components(body)
    pass_on(NCOMP - 2)
    update(NCOMP - 1)
    pass_on(NCOMP - 1)
    if last:
        chemistry(planes, SPAN, turns, new_ref, counts_ref, out_ref, made, sems)


def messages(c, planes, width_y, width_z, place, u_ref, uz_ref, xmsg_refs, ymsgs, zmsgs):
    for n, ref in enumerate(xmsg_refs):
        begin = place[2 + n]
        for k in range(HALO):
            rows = pl.ds(pl.multiple_of((begin + k) * ROWS, ROWS), ROWS)
            ref[c, pl.ds(k * ROWS, ROWS), :] = u_ref[c, rows, :]
    first_up = place[5] == 0
    for k in range(HALO):
        for g in range(planes // ROWS):
            base = g * ROWS * width_y + k
            low = u_ref[c, pl.ds(base, ROWS, stride=width_y), :]
            high = u_ref[c, pl.ds(base + width_y - HALO, ROWS, stride=width_y), :]
            there = pl.ds(k * planes + g * ROWS, ROWS)
            ymsgs[0][c, there, :] = jnp.where(first_up, high, low)
            ymsgs[1][c, there, :] = jnp.where(first_up, low, high)
    for n in range(2):
        begin = pl.multiple_of(jnp.where(place[6] == n, width_z, ROWS), ROWS)
        zmsgs[n][c] = uz_ref[c, pl.ds(begin, ROWS), :]


def assemble_kernel(
    planes, width_y, width_z, x_msgs, place, state_ref, ahead_ref, fresh_ref, u_ref, uz_ref, *refs,
):
    refs = list(refs)
    xmsg_refs = [refs.pop(0) for _ in range(x_msgs)]
    ymsgs, zmsgs = refs[:2], refs[2:]
    tube, tubes, shift = place[0], place[1], place[4]
    reach = ahead_ref.shape[1] // ROWS

    def pass_on(c):
        uz_ref[c, pl.ds(ROWS, width_z), :] = u_ref[c].T
        messages(c, planes, width_y, width_z, place, u_ref, uz_ref, xmsg_refs,
                 ymsgs, zmsgs)

    for c in range(NCOMP):
        if c:
            pass_on(c - 1)
        fresh = fresh_ref[c]
        for i in range(planes):
            source = shift + i
            own = jnp.minimum(source, planes - 1)
            value = state_ref[c, pl.ds(pl.multiple_of(own * ROWS, ROWS), ROWS), :]
            if i >= planes - reach:
                beyond = jnp.clip(source - planes, 0, reach - 1)
                other = ahead_ref[c, pl.ds(pl.multiple_of(beyond * ROWS, ROWS), ROWS), :]
                other = jnp.where(tube == tubes - 1, fresh, other)
                value = jnp.where(source >= planes, other, value)
            u_ref[c, pl.ds(i * ROWS, ROWS), :] = value
    pass_on(NCOMP - 1)


def powers_of(back):
    a = jnp.exp(-0.5 * back)
    b = jnp.exp(-0.3 * back)
    a2 = a * a
    a3 = a2 * a
    a4 = a2 * a2
    a6 = a3 * a3
    a8 = a4 * a4
    return {0.5: a, 0.3: b, 1.0: a2, 1.5: a3, 3.0: a6, 4.0: a8, 4.5: a8 * a, 5.0: a8 * a2,
            6.0: a6 * a6, 0.8: a * b}


def react(conc, internal, size):
    s2 = conc[2] + conc[6] + conc[7]
    s3 = conc[3] + conc[4]
    heat = 2.5 * (((conc[0] + conc[1]) + (conc[5] + conc[8])) + (s2 + s3)) + (0.5 * s2 - s3)
    bond = None
    for k in range(9):
        if FORMATION[k]:
            term = float(FORMATION[k] * MOLAR[k]) * conc[k]
            bond = term if bond is None else bond + term
    boltzmann = powers_of(heat / (internal - bond))
    pairs = {}
    omega = [None] * 9

    def add(k, value):
        omega[k] = value if omega[k] is None else omega[k] + value

    def sub(k, value):
        omega[k] = -value if omega[k] is None else omega[k] - value

    def rate(j):
        names = REACTANTS[j]
        key = tuple(sorted(names))
        if key not in pairs:
            value = conc[names[0]] * conc[names[1]]
            if len(names) == 3:
                base = tuple(sorted(names[:2]))
                if base not in pairs:
                    pairs[base] = value
                value = pairs[base] * conc[8]
            pairs[key] = value
        return (PREFACTOR[j] * boltzmann[BARRIER[j]]) * pairs[key]

    j = 0
    while j < len(REACTANTS):
        value = rate(j)
        back = j + 1 < len(REACTANTS) and REACTANTS[j + 1] == PRODUCTS[j] \
            and PRODUCTS[j + 1] == REACTANTS[j]
        if back:
            value = value - rate(j + 1)
        for k in range(9):
            times = PRODUCTS[j].count(k) - REACTANTS[j].count(k)
            if times == 0:
                continue
            amount = value if abs(times) == 1 else value + value
            if times > 0:
                add(k, amount)
            else:
                sub(k, amount)
        j += 2 if back else 1
    return [conc[k] + size * omega[k] for k in range(9)]


def trip_counts(planes, span, counts_ref):
    most = []
    for i in range(planes // span):
        top = counts_ref[pl.ds(i * span * ROWS, ROWS), :]
        for k in range(1, span):
            top = jnp.maximum(top, counts_ref[pl.ds((i * span + k) * ROWS, ROWS), :])
        most.append(jnp.max(top))
    return most


def chemistry(planes, span, turns, third_ref, counts_ref, out_ref, made, sems):
    blocks = planes // span
    kept = pltpu.make_async_copy(
        third_ref.at[pl.ds(9, NCOMP - 9)], out_ref.at[pl.ds(9, NCOMP - 9)], sems.at[blocks])
    kept.start()
    copies = [kept]
    for i in reversed(range(blocks)):
        rows = [pl.ds((i * span + k) * ROWS, ROWS) for k in range(span)]
        counts = [counts_ref[r, :] for r in rows]
        sizes = [TIME_STEP / n.astype(jnp.float32) for n in counts]
        conc, internal = [], []
        for r in rows:
            u = [third_ref[c, r, :] for c in range(NCOMP)]
            rho = ((u[0] + u[1]) + (u[2] + u[3])) + ((u[4] + u[5]) + (u[6] + u[7])) + u[8]
            internal.append(
                u[12] - 0.5 * (u[9] * u[9] + u[10] * u[10] + u[11] * u[11]) / rho)
            conc.append([u[k] * float(GAS[k]) for k in range(9)])

        def advance(index, carry, counts=counts, sizes=sizes, internal=internal):
            new = []
            for k in range(span):
                moved = react(carry[k], internal[k], sizes[k])
                keep = index < counts[k]
                new.append([jnp.where(keep, m, o) for m, o in zip(moved, carry[k])])
            return new

        conc = lax.fori_loop(0, turns[i], advance, conc)
        for k in range(span):
            for c in range(9):
                made[c, rows[k], :] = conc[k][c] * float(MOLAR[c])
        block = pl.ds(i * span * ROWS, span * ROWS)
        copy = pltpu.make_async_copy(
            made.at[:, block], out_ref.at[pl.ds(0, 9), block], sems.at[i])
        copy.start()
        copies.append(copy)
    for copy in copies:
        copy.wait()


def shape(*dims):
    return jax.ShapeDtypeStruct(dims, jnp.float32)


def call(kernel, out_shape, scratch, n_in, scalars=True, far=False):
    vmem = pl.BlockSpec(memory_space=pltpu.VMEM)
    specs = [vmem] * n_in
    if scalars:
        specs[0] = pl.BlockSpec(memory_space=pltpu.SMEM)
    out = pl.BlockSpec(memory_space=pl.ANY) if far else vmem
    return pl.pallas_call(
        kernel,
        out_shape=out_shape,
        in_specs=specs,
        out_specs=jax.tree.map(lambda _: out, out_shape),
        scratch_shapes=[
            pltpu.VMEM(s, jnp.float32) if isinstance(s, tuple) else s for s in scratch],
        compiler_params=pltpu.CompilerParams(vmem_limit_bytes=16 * 1024 * 1024),
    )


def moved(value, axis, steps):
    count = lax.axis_size(axis)
    pairs = [(i, i + steps) for i in range(count) if 0 <= i + steps < count]
    return lax.ppermute(value, axis, pairs)


def swapped(value, axis, which):
    count = lax.axis_size(axis)
    assert count % 2 == 0
    step = 1 - 2 * which
    return lax.ppermute(
        value, axis, [(i, (i + (step if i % 2 == 0 else -step)) % count) for i in range(count)])


def on_device(state, fresh, substeps, shift):
    comps, planes, width_y, width_z = state.shape
    cross = planes * width_y
    zvecs = width_z // ROWS
    tubes = lax.axis_size("tube")
    tube = lax.axis_index("tube")
    swap = tubes == 2
    x_msgs = 1 if swap else 2
    begins = [jnp.where(tube == 0, planes - HALO, 0), 0] if swap else [0, planes - HALO]
    place = jnp.stack([
        tube.astype(jnp.int32), jnp.int32(tubes), jnp.asarray(begins[0], jnp.int32),
        jnp.asarray(begins[1], jnp.int32), shift.astype(jnp.int32),
        lax.axis_index("gy") % 2, lax.axis_index("gz") % 2])

    full = shape(comps, cross, width_z)
    fullz = shape(comps, width_z + 2 * ROWS, cross)
    xs = shape(comps, HALO * ROWS, width_z)
    ys = shape(comps, HALO * planes, width_z)
    zs = shape(comps, ROWS, cross)
    sent = (full, fullz) + (xs,) * x_msgs + (ys, ys, zs, zs)
    flat = state.reshape(comps, cross, width_z)

    def shifted(reach):
        def branch():
            ahead = moved(flat[:, :reach * width_y], "tube", -1)
            return call(
                functools.partial(assemble_kernel, planes, width_y, width_z, x_msgs),
                sent, [], 4,
            )(place, flat, ahead, fresh)
        return branch

    pieces = SMAX
    size = SMAX // pieces
    start, uz, *msgs = lax.switch(
        (shift.astype(jnp.int32) - 1) // size, [shifted((n + 1) * size) for n in range(pieces)])

    in_x, in_y, in_z = shape(cross, width_z), shape(cross, width_z), shape(
        width_z + 2 * ROWS, cross)
    inner_out = (in_x,) * 3 + (in_y,) * 3 + (in_z,) * 3 + (full, full, shape(comps, width_z, cross))
    al = [((planes + 1) * ROWS, width_z), ((width_y + 1) * planes, width_z),
          ((zvecs + 1) * ROWS, cross)]
    inner_scratch = al + [(3, cross, width_z)]
    outer_scratch = [
        (comps, 2 * HALO * ROWS, width_z), (3, 2 * HALO * ROWS, width_z),
        (3, 2 * HALO * planes, width_z), (3, 2 * ROWS, cross),
        *al, (comps, 2 * HALO * ROWS, width_z), (comps, cross, width_z), (comps, width_z, cross),
        (cross, width_z)]
    current = start
    for stage in (1, 2, 3):
        xmsg, (y0, y1, z0, z1) = msgs[:x_msgs], msgs[x_msgs:]
        y1 = swapped(y1, "gy", 1)
        if swap:
            xlo = xhi = lax.ppermute(xmsg[0], "tube", [(0, 1), (1, 0)])
        else:
            xhi = moved(xmsg[0], "tube", -1)
            xlo = moved(xmsg[1], "tube", 1)
        z1 = swapped(z1, "gz", 1)
        z0 = swapped(z0, "gz", 0)
        y0 = swapped(y0, "gy", 0)
        inner = call(
            functools.partial(inner_kernel, planes, width_y, width_z),
            inner_out, inner_scratch, 2, False)(current, uz)
        last = stage == 3
        tail = (substeps.reshape(cross, width_z),) if last else ()
        far = [full.shape, (9, cross, width_z), pltpu.SemaphoreType.DMA((planes // SPAN + 1,))]
        current, *rest = call(
            functools.partial(outer_kernel, stage, planes, width_y, width_z, x_msgs),
            (full,) if last else sent, outer_scratch + far if last else outer_scratch,
            11 + len(inner_out) + len(tail), far=last,
        )(place, current, uz, start, fresh, xlo, xhi, y0, y1, z0, z1, *inner, *tail)
        if stage < 3:
            uz, *msgs = rest

    return current.reshape(state.shape)


def solution(mesh):
    return jax.shard_map(
        on_device,
        mesh=mesh,
        in_specs=(P(None, "tube", "gy", "gz"), P(None, "gy", "gz"), P("tube", "gy", "gz"), P()),
        out_specs=P(None, "tube", "gy", "gz"),
        check_vma=False,
    )
```
